32 devices in a mesh: lat: 2 (over x), lon: 16 (over z, y, core).
Axes of the slice: x: 2, y: 2, z: 4, core: 2. Of those that a mesh axis runs over, the one named last changes fastest.
Arguments:
- field_state: bfloat16 [4, 16, 40960], P(None, 'lat', 'lon'), may hold values from -6 to 6
- reservoir_state: bfloat16 [4, 256, 4, 1024], P('lat', 'lon'), may hold values from -0.8984375 to 0.8984375
- coupling_blocks: bfloat16 [4, 2048, 128], P('lat'), may hold values from -0.375 to 0.375
- coupling_index: int32 [4, 8, 2], P('lat'), may hold values from 0 to 7, as said below
- input_blocks: bfloat16 [4, 1024, 128], P('lat'), may hold values from -0.5 to 0.5
- input_index: int32 [4, 8], P('lat'), may hold values from 0 to 19
- zonal_band_output_matrices: bfloat16 [2, 640, 1024], P('lat'), may hold values from -0.1875 to 0.1875
- region_band: int32 [4], P('lat'), may hold values from 0 to 1
Outputs:
- field_out: bfloat16 [4, 16, 40960], P(None, 'lat', 'lon')
- states_out: bfloat16 [4, 256, 4, 1024], P('lat', 'lon')
The draws below stay inside these ranges and needn't reach their ends.
Inputs may be any that keep to these rules, and one draw needn't show every extreme that they name: `coupling_index`: the 2 block columns of one block-row differ. `region_band`: a band of the region row's own latitude group of 2 region rows.
All inputs are finite; a program needn't handle non-finite values.
Results may differ from the reference program's by a relative error of at most 0.0095.
Values may be sent and summed in bfloat16 or wider, within the bound.
No kernel may reach another device: no remote copies, remote signals or barrier semaphores. Data moves between devices by JAX's collectives and lax.ppermute only.
A program may use at most 64 MiB of HBM per device.

```python
import jax
import jax.numpy as jnp
from jax import lax

UNITS = 1024
VARS = 40
BLK = 128
SLOTS = 2
BANDS_DEV = 2
MEMBERS = 4
STEPS = 3
REG_Y = 2
BANDS = 4
GROUPS = 2
OUTS = 640
LAT_REG = 4
LON_REG = 256
LAT_CELLS = 16
LON_CELLS = 1024


def draw_coupling_index(key, part):
    key = jax.random.fold_in(key, 11)
    first_key, second_key = jax.random.split(key)
    block_rows = UNITS // BLK
    first = jax.random.randint(first_key, (BANDS, block_rows), 0, block_rows)
    offset = jax.random.randint(second_key, (BANDS, block_rows), 1, block_rows)
    second = (first + offset) % block_rows
    return jnp.stack([first, second], axis=-1).astype(jnp.int32)


def plant(values, rng, low, top_value):
    index_at = [jax.random.randint(jax.random.fold_in(rng, axis), (), 0, length) for axis, length in enumerate(values.shape)]
    longest = values.shape.index(max(values.shape))
    next_to = index_at[:longest] + [(index_at[longest] + 1) % values.shape[longest]] + index_at[longest + 1:]
    return values.at[tuple(index_at)].set(low).at[tuple(next_to)].set(top_value)


def steps_of(stream_key, dims, shards, least, top_value):
    factor_of, own = 1.0, jax.random.fold_in(stream_key, 6)
    for axis_at, blocks in shards:
        draws = jnp.exp(jax.random.uniform(jax.random.fold_in(own, axis_at), (blocks,), jnp.float32, least / len(shards), top_value / len(shards)))
        factor_of = factor_of * jnp.repeat(draws, dims[axis_at] // blocks).reshape([-1 if axis == axis_at else 1 for axis in range(len(dims))])
    return factor_of


def noise(rng, extent, spread, most, cuts=(), dtype=jnp.bfloat16):
    entries = jax.random.normal(rng, extent, jnp.float32) * spread
    if len(cuts) > 0:
        entries = steps_of(rng, extent, cuts, -0.22, 0.18) * entries
    return jnp.clip(entries, min=-most, max=most).astype(dtype)


def setup_inputs(seed: int = 0) -> dict:
    keys = jax.random.split(jax.random.key(seed), 9)
    field_state = noise(keys[0], (MEMBERS, LAT_CELLS, LON_CELLS * VARS), 1.0, 6.0, ((1, 2), (2, 16)))
    reservoir_state = jnp.clip(jax.random.uniform(keys[1], (LAT_REG, LON_REG, MEMBERS, UNITS), jnp.float32, -0.8984375, 0.8984375) * steps_of(keys[1], (LAT_REG, LON_REG, MEMBERS, UNITS), ((0, 2), (1, 16)), -0.4, 0.0), -0.8984375, 0.8984375).astype(jnp.bfloat16)
    coupling_blocks = noise(keys[2], (BANDS, UNITS * SLOTS, BLK), (SLOTS * BLK) ** -0.5, 0.375, ((0, 2),))
    coupling_index = draw_coupling_index(jax.random.fold_in(keys[8], 71), 0)
    input_blocks = noise(keys[4], (BANDS, UNITS, BLK), BLK ** -0.5, 0.5, ((0, 2),))
    input_index = plant(jax.random.randint(keys[5], (BANDS, UNITS // BLK), 0, 64 * VARS // BLK), jax.random.fold_in(keys[5], 1), 0, (64 * VARS // BLK) - 1).astype(jnp.int32)
    zonal_band_output_matrices = noise(keys[6], (GROUPS, OUTS, UNITS), UNITS ** -0.5, 0.1875, ((0, 2),))
    region_band = plant(jax.random.randint(keys[7], (LAT_REG,), 0, BANDS_DEV), jax.random.fold_in(keys[7], 1), 0, BANDS_DEV - 1).astype(jnp.int32)
    return dict(field_state=field_state, reservoir_state=reservoir_state, coupling_blocks=coupling_blocks, coupling_index=coupling_index, input_blocks=input_blocks, input_index=input_index, zonal_band_output_matrices=zonal_band_output_matrices, region_band=region_band)


def region_inputs(band_slab, region_count, vertical_quantity_total):
    perturbation_copies = band_slab.shape[0]
    pieces = band_slab.reshape(perturbation_copies, 8, region_count + 1, 4 * vertical_quantity_total)
    windows = jnp.concatenate([pieces[:, :, :-1], pieces[:, :, 1:]], axis=3)
    return windows.transpose(2, 0, 1, 3).reshape(region_count * perturbation_copies, 64 * vertical_quantity_total)


def reservoir_update(state_rows, input_rows, coupling, coupling_idx, driving, driving_idx):
    row_count = state_rows.shape[0]
    block_rows = coupling_idx.shape[0]
    slot_count = coupling_idx.shape[1]
    block_size = coupling.shape[-1]
    picked = jnp.take(state_rows.reshape(row_count, block_rows, block_size), coupling_idx, axis=1)
    blocks = coupling.reshape(block_rows, slot_count, block_size, block_size)
    recurrent = jnp.einsum("nbki,bkoi->nbo", picked.astype(jnp.float32), blocks.astype(jnp.float32))
    chosen = jnp.take(input_rows.reshape(row_count, -1, block_size), driving_idx, axis=1)
    drive_blocks = driving.reshape(block_rows, block_size, block_size)
    drive_term = jnp.einsum("nbi,boi->nbo", chosen.astype(jnp.float32), drive_blocks.astype(jnp.float32))
    refreshed_activation = jnp.tanh(recurrent + drive_term)
    return refreshed_activation.reshape(row_count, block_rows * block_size).astype(jnp.bfloat16)


def reference(field_state, reservoir_state, coupling_blocks, coupling_index, input_blocks, input_index, zonal_band_output_matrices, region_band):
    vertical_quantity_total = VARS
    perturbation_copies, lat_cells, flat_cols = field_state.shape
    meridional_sector_total = flat_cols // (4 * vertical_quantity_total)
    latitude_region_count = lat_cells // 4
    current = field_state
    states_now = reservoir_state
    for step_index in range(STEPS):
        padded = jnp.pad(current, ((0, 0), (2, 2), (0, 0)))
        padded = jnp.concatenate([padded[:, :, -2 * vertical_quantity_total:], padded, padded[:, :, :2 * vertical_quantity_total]], axis=2)
        gridpoint_line_entries = []
        state_rows = []
        for region_row in range(latitude_region_count):
            zonal_band_number = region_row // REG_Y
            band_index = zonal_band_number * BANDS_DEV + region_band[region_row]
            coupling = lax.dynamic_index_in_dim(coupling_blocks, band_index, 0, keepdims=False)
            coupling_idx = lax.dynamic_index_in_dim(coupling_index, band_index, 0, keepdims=False)
            driving = lax.dynamic_index_in_dim(input_blocks, band_index, 0, keepdims=False)
            driving_idx = lax.dynamic_index_in_dim(input_index, band_index, 0, keepdims=False)
            previous = states_now[region_row].reshape(meridional_sector_total * perturbation_copies, UNITS)
            inputs_now = region_inputs(padded[:, 4 * region_row:4 * region_row + 8], meridional_sector_total, vertical_quantity_total)
            refreshed_activation = reservoir_update(previous, inputs_now, coupling, coupling_idx, driving, driving_idx)
            prediction_sequence = jnp.dot(refreshed_activation, zonal_band_output_matrices[zonal_band_number].T, preferred_element_type=jnp.float32).astype(jnp.bfloat16)
            state_rows.append(refreshed_activation.reshape(meridional_sector_total, perturbation_copies, UNITS))
            gridpoint_line_entries.append(prediction_sequence.reshape(meridional_sector_total, perturbation_copies, 4, 4 * vertical_quantity_total).transpose(1, 2, 0, 3).reshape(perturbation_copies, 4, meridional_sector_total * 4 * vertical_quantity_total))
        current = jnp.concatenate(gridpoint_line_entries, axis=1)
        states_now = jnp.stack(state_rows, axis=0)
    return current, states_now
```

```python
import functools

import jax
import jax.numpy as jnp
from jax import lax
from jax.experimental import pallas as pl
from jax.experimental.pallas import tpu as pltpu
from jax.sharding import PartitionSpec as P

VARS = 40
STEPS = 3
CELL = 4 * VARS
CHUNK = 4 * CELL
HALF = 512
MEM = 4
BLK = 128
BF = jnp.bfloat16
F32 = jnp.float32
VM = pl.BlockSpec(memory_space=pltpu.VMEM)
SM = pl.BlockSpec(memory_space=pltpu.SMEM)


def prep_kernel(edge_count, starts_ref, field_ref, state_ref, *outs):
    own_ref, left_ref, right_ref = outs[:3]
    lat_refs = outs[3 : 3 + edge_count]
    dleft_refs = outs[3 + edge_count : 3 + 2 * edge_count]
    dright_refs = outs[3 + 2 * edge_count :]
    chunks = field_ref.shape[2] // CHUNK
    tiles = []
    for q in range(chunks):
        for m in range(MEM):
            tiles.append(field_ref[m, :, q * CHUNK : (q + 1) * CHUNK].astype(F32)[None])
    rows = jnp.transpose(jnp.concatenate(tiles, axis=0), (1, 0, 2)).astype(BF)
    own_ref[...] = rows
    last = (chunks - 1) * MEM
    regions = state_ref.shape[1]
    for r in range(2):
        for j in range(2):
            left_ref[r, j * MEM : (j + 1) * MEM] = state_ref[r, j]
            right_ref[r, j * MEM : (j + 1) * MEM] = state_ref[r, regions - 2 + j]
    for k in range(8):
        at = (k % 2) * MEM
        lane = (k // 2 % 2) * HALF
        left_ref[2 + k // 4, at : at + MEM, lane : lane + HALF] = rows[k, :MEM, :HALF]
        right_ref[2 + k // 4, at : at + MEM, lane : lane + HALF] = rows[k, last:, CHUNK - HALF :]
    for e in range(edge_count):
        start = starts_ref[e]
        lat_refs[e][...] = own_ref[pl.ds(start, 2)]
        for k in range(2):
            row = own_ref[start + k]
            dleft_refs[e][k * MEM : (k + 1) * MEM] = row[:MEM, :HALF]
            dright_refs[e][k * MEM : (k + 1) * MEM] = row[last:, CHUNK - HALF :]


def widen(own, left, right):
    fill = jnp.zeros((MEM, CHUNK - HALF), F32)
    return jnp.concatenate(
        [
            jnp.concatenate([fill, left.astype(F32)], axis=1),
            own.astype(F32),
            jnp.concatenate([right.astype(F32), fill], axis=1),
        ],
        axis=0,
    )


def build_inputs(r, xs_ref, in_ref):
    rows = xs_ref.shape[1]
    parts = [[] for _ in range(4)]
    for d in range(8):
        a = xs_ref[4 * r + d]
        before = jnp.concatenate([a[rows - MEM :, CHUNK - 2 * VARS :], a[: rows - MEM, CHUNK - 2 * VARS :]], axis=0)
        after = jnp.concatenate([a[MEM:, : 2 * VARS], a[:MEM, : 2 * VARS]], axis=0)
        ext = jnp.concatenate([before, a, after], axis=1)
        for res in range(4):
            parts[res].append(ext[:, CELL * res : CELL * res + 2 * CELL])
    for res in range(4):
        parts[res] = jnp.concatenate(parts[res], axis=1)
    in_ref[...] = jnp.concatenate(parts, axis=0).astype(BF)


def advance(r, s_ref, in_ref, band_ref, cidx_ref, iidx_ref, coup_ref, inp_ref, read_ref, snew_ref):
    band = band_ref[r]
    blocks = iidx_ref.shape[1]
    new = []
    for b in range(blocks):
        pieces, mats = [], []
        for k in range(2):
            at = pl.multiple_of(cidx_ref[band, b, k] * BLK, BLK)
            pieces.append(s_ref[:, pl.ds(at, BLK)])
            row = (b * 2 + k) * BLK
            mats.append(coup_ref[band, row : row + BLK, :])
        at = pl.multiple_of(iidx_ref[band, b] * BLK, BLK)
        pieces.append(in_ref[:, pl.ds(at, BLK)])
        mats.append(inp_ref[band, b * BLK : (b + 1) * BLK, :])
        pre = lax.dot_general(
            jnp.concatenate(pieces, axis=1),
            jnp.concatenate(mats, axis=1),
            (((1,), (1,)), ((), ())),
            preferred_element_type=F32,
        )
        new.append(jnp.tanh(pre).astype(BF))
    state = jnp.concatenate(new, axis=1)
    snew_ref[...] = state
    pred = lax.dot_general(state, read_ref[0], (((1,), (1,)), ((), ())), preferred_element_type=F32)
    per = state.shape[0] // 4
    return [
        jnp.concatenate([pred[res * per : (res + 1) * per, d * CELL : (d + 1) * CELL] for res in range(4)], axis=1)
        for d in range(4)
    ]


def emit(r, lats, a_ref, edge_ref):
    for d in range(4):
        a_ref[d] = lats[d].astype(BF)
    if edge_ref is not None:
        edge_ref[...] = a_ref[pl.ds(2 * r, 2)]


def first_kernel(halo, row_ref, band_ref, cidx_ref, iidx_ref, coup_ref, inp_ref, read_ref, own_ref, state_ref, fl_ref, fr_ref, *rest):
    r = row_ref[0]
    if halo:
        lat_ref, dl_ref, dr_ref, a_ref, edge_ref, snew_ref, xs_ref, s_ref, in_ref = rest
    else:
        a_ref, snew_ref, xs_ref, s_ref, in_ref = rest
        edge_ref = None
    side = 10 * r
    for k in range(8):
        at, lane = (k % 2) * MEM, (k // 2 % 2) * HALF
        left = fl_ref[2 + k // 4, at : at + MEM, lane : lane + HALF]
        right = fr_ref[2 + k // 4, at : at + MEM, lane : lane + HALF]
        xs_ref[2 + k] = widen(own_ref[k], left, right)
    for k in range(2):
        if halo:
            at = k * MEM
            xs_ref[side + k] = widen(lat_ref[k], dl_ref[at : at + MEM], dr_ref[at : at + MEM])
        else:
            xs_ref[side + k] = jnp.zeros(xs_ref.shape[1:], F32)
    regions = state_ref.shape[1]
    chunks = regions // 4
    empty = jnp.zeros((MEM, s_ref.shape[1]), F32)
    rows = []
    for res in range(4):
        rows.append(fl_ref[r, (res - 2) * MEM : (res - 1) * MEM].astype(F32) if res >= 2 else empty)
        for q in range(chunks):
            rows.append(state_ref[r, 4 * q + res].astype(F32))
        rows.append(fr_ref[r, res * MEM : (res + 1) * MEM].astype(F32) if res < 2 else empty)
    s_ref[...] = jnp.concatenate(rows, axis=0).astype(BF)
    build_inputs(r, xs_ref, in_ref)
    lats = advance(r, s_ref, in_ref, band_ref, cidx_ref, iidx_ref, coup_ref, inp_ref, read_ref, snew_ref)
    emit(r, lats, a_ref, edge_ref)


def step_kernel(halo, final, row_ref, band_ref, cidx_ref, iidx_ref, coup_ref, inp_ref, read_ref, self_ref, other_ref, s_ref, *rest):
    r = row_ref[0]
    rest = list(rest)
    lat_ref = rest.pop(0) if halo else None
    if final:
        fin_a_ref, fin_s_ref, field_ref, states_ref, xs_ref, in_ref, snew_ref = rest
    elif halo:
        a_ref, edge_ref, snew_ref, xs_ref, in_ref = rest
    else:
        a_ref, snew_ref, xs_ref, in_ref = rest
        edge_ref = None
    side = 10 * r
    for k in range(4):
        xs_ref[2 + 4 * r + k] = self_ref[k].astype(F32)
        xs_ref[6 - 4 * r + k] = other_ref[k].astype(F32)
    for k in range(2):
        xs_ref[side + k] = lat_ref[k].astype(F32) if halo else jnp.zeros(xs_ref.shape[1:], F32)
    build_inputs(r, xs_ref, in_ref)
    lats = advance(r, s_ref, in_ref, band_ref, cidx_ref, iidx_ref, coup_ref, inp_ref, read_ref, snew_ref)
    if not final:
        emit(r, lats, a_ref, edge_ref)
        return
    own = slice(MEM, lats[0].shape[0] - MEM)
    mine = [x[own] for x in lats]
    fin = [fin_a_ref[d, own, :].astype(F32) for d in range(4)]
    low = r == 0
    rows = [jnp.where(low, mine[d], fin[d])[None] for d in range(4)]
    rows += [jnp.where(low, fin[d], mine[d])[None] for d in range(4)]
    tiles = jnp.transpose(jnp.concatenate(rows, axis=0), (1, 0, 2)).astype(BF)
    chunks = field_ref.shape[2] // CHUNK
    per = snew_ref.shape[0] // 4
    for q in range(chunks):
        for m in range(MEM):
            field_ref[m, :, q * CHUNK : (q + 1) * CHUNK] = tiles[q * MEM + m]
        for res in range(4):
            at = res * per + (q + 1) * MEM
            states_ref[r, 4 * q + res] = snew_ref[at : at + MEM]
            states_ref[1 - r, 4 * q + res] = fin_s_ref[at : at + MEM]


def call(kernel, out_shape, scratch, smem, operands, flops):
    size = sum(x.size * x.dtype.itemsize for x in operands)
    return pl.pallas_call(
        kernel,
        out_shape=out_shape,
        in_specs=[SM] * smem + [VM] * (len(operands) - smem),
        out_specs=jax.tree.map(lambda _: VM, out_shape),
        scratch_shapes=scratch,
        compiler_params=pltpu.CompilerParams(vmem_limit_bytes=40 * 1024 * 1024),
        cost_estimate=pl.CostEstimate(flops=flops, bytes_accessed=size, transcendentals=0),
    )(*operands)


def per_device(field_state, reservoir_state, coupling_blocks, coupling_index, input_blocks, input_index, readout, region_band):
    lat_count, lon_count = lax.axis_size("lat"), lax.axis_size("lon")
    lat_at = lax.axis_index("lat").astype(jnp.int32)
    region_rows, regions, members, units = reservoir_state.shape
    assert region_rows == 2 and members == MEM and regions % 4 == 0
    chunks = regions // 4
    wide = (chunks + 2) * MEM
    rows = 4 * wide
    swap = lat_count == 2
    edges = 1 if swap else 2

    def shape(*dims):
        return jax.ShapeDtypeStruct(dims, BF)

    def send(x, lat_step, lon_step):
        pairs = []
        for i in range(lat_count):
            to = 1 - i if swap and lat_step else i + lat_step
            if 0 <= to < lat_count:
                for j in range(lon_count):
                    pairs.append((i * lon_count + j, to * lon_count + (j + lon_step) % lon_count))
        return lax.ppermute(x, ("lat", "lon"), pairs)

    if swap:
        starts = jnp.where(lat_at == 0, 6, 0).reshape(1)
        rows_at = [(1 - lat_at).reshape(1), lat_at.reshape(1)]
    else:
        starts = jnp.array([0, 6], jnp.int32)
        rows_at = [jnp.array([0], jnp.int32), jnp.array([1], jnp.int32)]
    steps_of = [-1, 1][:edges]

    prep_out = (
        [shape(8, chunks * MEM, CHUNK), shape(4, 8, units), shape(4, 8, units)]
        + [shape(2, chunks * MEM, CHUNK)] * edges
        + [shape(8, HALF)] * (2 * edges)
    )
    prep = call(functools.partial(prep_kernel, edges), prep_out, [], 1, [starts, field_state, reservoir_state], 0)
    own, to_left, to_right = prep[:3]
    from_right = send(to_left, 0, -1)
    from_left = send(to_right, 0, 1)
    halos = []
    for e in range(edges):
        lat = send(prep[3 + e], steps_of[e], 0)
        dright = send(prep[3 + edges + e], steps_of[e], -1)
        dleft = send(prep[3 + 2 * edges + e], steps_of[e], 1)
        halos.append([lat, dleft, dright])
    if not swap:
        halos.reverse()

    smem = [region_band, coupling_index, input_index]
    weights = [coupling_blocks, input_blocks, readout]
    flops = 2 * rows * units * (3 * BLK + CHUNK)
    xs = pltpu.VMEM((12, wide, CHUNK), F32)
    inputs = pltpu.VMEM((rows, 16 * CELL), BF)
    state = pltpu.VMEM((rows, units), BF)

    lats, states, sent = [None, None], [None, None], [None, None]
    for i in range(2):
        halo = i < edges
        out = [shape(4, wide, CHUNK)] + ([shape(2, wide, CHUNK)] if halo else []) + [shape(rows, units)]
        operands = [rows_at[i]] + smem + weights + [own, reservoir_state, from_left, from_right] + (halos[i] if halo else [])
        got = call(functools.partial(first_kernel, halo), out, [xs, state, inputs], 4, operands, flops)
        lats[i], states[i] = got[0], got[-1]
        if halo:
            sent[i] = got[1]

    for step in range(1, STEPS):
        received = [None, None]
        for e in range(edges):
            received[e] = send(sent[e], steps_of[e], 0)
        if not swap:
            received.reverse()
        last = step == STEPS - 1
        now_lats, now_states, now_sent = [None, None], [None, None], [None, None]
        for i in (1, 0):
            halo = i < edges
            final = last and i == 0
            operands = [rows_at[i]] + smem + weights + [lats[i], lats[1 - i], states[i]] + ([received[i]] if halo else [])
            if final:
                operands += [now_lats[1], now_states[1]]
                out = [shape(MEM, 8, regions * CELL), shape(region_rows, regions, MEM, units)]
                return call(functools.partial(step_kernel, halo, True), out, [xs, inputs, state], 4, operands, flops)
            out = [shape(4, wide, CHUNK)] + ([shape(2, wide, CHUNK)] if halo else []) + [shape(rows, units)]
            got = call(functools.partial(step_kernel, halo, False), out, [xs, inputs], 4, operands, flops)
            now_lats[i], now_states[i] = got[0], got[-1]
            if halo:
                now_sent[i] = got[1]
        lats, states, sent = now_lats, now_states, now_sent


def solution(mesh):
    return jax.shard_map(
        per_device,
        mesh=mesh,
        in_specs=(
            P(None, "lat", "lon"),
            P("lat", "lon", None, None),
            P("lat", None, None),
            P("lat", None, None),
            P("lat", None, None),
            P("lat", None),
            P("lat", None, None),
            P("lat"),
        ),
        out_specs=(P(None, "lat", "lon"), P("lat", "lon", None, None)),
        check_vma=False,
    )
```

```python
import functools

import jax
import jax.numpy as jnp
from jax import lax
from jax.experimental import pallas as pl
from jax.experimental.pallas import tpu as pltpu
from jax.sharding import PartitionSpec as P

VARS = 40
STEPS = 3
CELL = 4 * VARS
CHUNK = 4 * CELL
HALF = 512
NEAR = 256
MEM = 4
BLK = 128
BF = jnp.bfloat16
F32 = jnp.float32
VM = pl.BlockSpec(memory_space=pltpu.VMEM)
SM = pl.BlockSpec(memory_space=pltpu.SMEM)
HB = pl.BlockSpec(memory_space=pltpu.HBM)
NT = (((1,), (1,)), ((), ()))


def row_of(slot, row_ref):
    return row_ref[0] if slot == 0 else 1 - row_ref[0]


def message_kernel(parity_ref, field_hbm, state_hbm, first_ref, second_ref, field_ref, state_ref, sems):
    odd = parity_ref[0]
    lanes = field_hbm.shape[2] - HALF
    regions = state_hbm.shape[1]
    copies = []
    for k in range(2):
        low = odd if k == 0 else 1 - odd
        lane = pl.multiple_of((1 - low) * lanes, BLK)
        copies.append(pltpu.make_async_copy(field_hbm.at[:, :, pl.ds(lane, HALF)], field_ref.at[k], sems.at[k]))
        at = (1 - low) * (regions - 2)
        copies.append(pltpu.make_async_copy(state_hbm.at[:, pl.ds(at, 2)], state_ref.at[k], sems.at[2 + k]))
    for c in copies:
        c.start()
    for c in copies:
        c.wait()
    for k, out in enumerate((first_ref, second_ref)):
        for r in range(2):
            for j in range(2):
                out[r, j * MEM : (j + 1) * MEM] = state_ref[k, r, j]
        rows = jnp.transpose(field_ref[k].astype(F32), (1, 0, 2)).astype(BF)
        for d in range(8):
            at, lane = (d % 2) * MEM, (d // 2 % 2) * HALF
            out[2 + d // 4, at : at + MEM, lane : lane + HALF] = rows[d]


def setup_kernel(row_ref, band_ref, field_hbm, state_hbm, coup_hbm, inp_hbm, read_hbm, own_ref, s0_ref, s1_ref, w0_ref, w1_ref, read_ref, field_ref, state_ref, sems):
    copies = []

    def start(src, dst):
        copies.append(pltpu.make_async_copy(src, dst, sems.at[len(copies)]))
        copies[-1].start()

    start(field_hbm, field_ref)
    start(state_hbm, state_ref)
    for slot, w_ref in enumerate((w0_ref, w1_ref)):
        band = band_ref[row_of(slot, row_ref)]
        for k in range(2):
            start(coup_hbm.at[band, :, k], w_ref.at[:, :, k * BLK : (k + 1) * BLK])
        start(inp_hbm.at[band], w_ref.at[:, :, 2 * BLK :])
    start(read_hbm.at[0], read_ref)
    chunks = field_ref.shape[2] // CHUNK
    copies[0].wait()
    tiles = []
    for q in range(chunks):
        for m in range(MEM):
            tiles.append(field_ref[m, :, q * CHUNK : (q + 1) * CHUNK].astype(F32)[None])
    own_ref[...] = jnp.transpose(jnp.concatenate(tiles, axis=0), (1, 0, 2)).astype(BF)
    copies[1].wait()
    for slot, s_ref in enumerate((s0_ref, s1_ref)):
        r = row_of(slot, row_ref)
        rows = [state_ref[r, 4 * q + res].astype(F32) for res in range(4) for q in range(chunks)]
        s_ref[...] = jnp.concatenate(rows, axis=0).astype(BF)
    for c in copies[2:]:
        c.wait()


def pack(row, out_ref, k):
    last = row.shape[0] - MEM
    out_ref[k, :, :CHUNK] = row[MEM:last].astype(BF)
    half = NEAR // 2
    ends = [row[:MEM, CHUNK - NEAR : CHUNK - half], row[:MEM, CHUNK - half :], row[last:, :half], row[last:, half:NEAR]]
    out_ref[k, :, CHUNK:] = jnp.concatenate(ends, axis=0).astype(BF)


def unpack(msg):
    x = msg.astype(F32)
    own, ends = x[:, :CHUNK], x[:, CHUNK:]
    fill = jnp.zeros((MEM, CHUNK - 2 * ends.shape[1]), F32)
    before = jnp.concatenate([fill, ends[:MEM], ends[MEM : 2 * MEM]], axis=1)
    after = jnp.concatenate([ends[2 * MEM : 3 * MEM], ends[3 * MEM :], fill], axis=1)
    return jnp.concatenate([before, own, after], axis=0)


def sides(parity_ref, first, second):
    odd = parity_ref[0] == 1
    return jnp.where(odd, first, second), jnp.where(odd, second, first)


def first_edge_kernel(slots, parity_ref, row_ref, own_ref, first_ref, second_ref, *outs):
    for slot in range(slots):
        r = row_of(slot, row_ref)
        for k in range(2):
            at = k * MEM
            got = []
            for ref in (first_ref, second_ref):
                low = ref[2, at : at + MEM, :HALF].astype(F32)
                high = ref[3, at : at + MEM, HALF : 2 * HALF].astype(F32)
                got.append(jnp.where(r == 0, low, high))
            left, right = sides(parity_ref, *got)
            half = HALF // 2
            ends = [left[:, :half], left[:, half:], right[:, :half], right[:, half:]]
            outs[slot][k, :, :CHUNK] = own_ref[6 * r + k]
            outs[slot][k, :, CHUNK:] = jnp.concatenate(ends, axis=0).astype(BF)


def windows(lats, narrow):
    parts = [[] for _ in range(4)]
    for a in lats:
        rows = a.shape[0]
        before = jnp.concatenate([a[rows - MEM :, CHUNK - 2 * VARS :], a[: rows - MEM, CHUNK - 2 * VARS :]], axis=0)
        after = jnp.concatenate([a[MEM:, : 2 * VARS], a[:MEM, : 2 * VARS]], axis=0)
        ext = jnp.concatenate([before, a, after], axis=1)
        if narrow:
            ext = ext[MEM : rows - MEM]
        for res in range(4):
            parts[res].append(ext[:, CELL * res : CELL * res + 2 * CELL])
    return jnp.concatenate([jnp.concatenate(p, axis=1) for p in parts], axis=0).astype(BF)


def latitude(pred, d):
    per = pred.shape[0] // 4
    return jnp.concatenate([pred[res * per : (res + 1) * per, d * CELL : (d + 1) * CELL] for res in range(4)], axis=1)


def block_pre(b, band, s_ref, in_ref, cidx_ref, iidx_ref, w_ref):
    pieces = []
    for k in range(2):
        pieces.append(s_ref[:, pl.ds(pl.multiple_of(cidx_ref[band, k, b] * BLK, BLK), BLK)])
    pieces.append(in_ref[:, pl.ds(pl.multiple_of(iidx_ref[band, b] * BLK, BLK), BLK)])
    return lax.dot_general(jnp.concatenate(pieces, axis=1), w_ref[b], NT, preferred_element_type=F32)


def shadow_kernel(first, last, slots, row_ref, parity_ref, band_ref, cidx_ref, iidx_ref, w0_ref, w1_ref, read_ref, *rest):
    rest = list(rest)

    def take(n):
        got = rest[:n]
        del rest[:n]
        return got

    if first:
        own_ref, s0_ref, s1_ref, first_ref, second_ref = take(5)
    else:
        edge_refs, s_refs = take(slots), take(slots)
        far_refs = take(2 * (2 - slots))
    pre_refs = take(slots)
    out_far = take(2 * (2 - slots))
    xs_ref, in_ref, sc0_ref, sc1_ref, pre_ref = take(5)
    rows_at = [row_of(0, row_ref), row_of(1, row_ref)]
    w_refs = [w0_ref, w1_ref]

    for k in range(2):
        xs_ref[k] = jnp.zeros(xs_ref.shape[1:], F32)
        xs_ref[10 + k] = jnp.zeros(xs_ref.shape[1:], F32)
    if first:
        fill = jnp.zeros((MEM, CHUNK - HALF), F32)
        left, right = sides(parity_ref, first_ref[...].astype(F32), second_ref[...].astype(F32))
        for d in range(8):
            at, lane = (d % 2) * MEM, (d // 2 % 2) * HALF
            lo = jnp.concatenate([fill, left[2 + d // 4, at : at + MEM, lane : lane + HALF]], axis=1)
            hi = jnp.concatenate([right[2 + d // 4, at : at + MEM, lane : lane + HALF], fill], axis=1)
            xs_ref[2 + d] = jnp.concatenate([lo, own_ref[d].astype(F32), hi], axis=0)
        empty = jnp.zeros((MEM, s0_ref.shape[1]), F32)
        per = s0_ref.shape[0] // 4
        for slot, (src, dst) in enumerate(((s0_ref, sc0_ref), (s1_ref, sc1_ref))):
            low = rows_at[slot] == 0
            lo, hi = jnp.where(low, left[0], left[1]), jnp.where(low, right[0], right[1])
            rows = []
            for res in range(4):
                rows.append(lo[(res - 2) * MEM : (res - 1) * MEM] if res >= 2 else empty)
                rows.append(src[res * per : (res + 1) * per].astype(F32))
                rows.append(hi[res * MEM : (res + 1) * MEM] if res < 2 else empty)
            dst[...] = jnp.concatenate(rows, axis=0).astype(BF)
        s_refs = [sc0_ref, sc1_ref]
    else:
        for slot in range(slots):
            r = rows_at[slot]
            half = pl.multiple_of((1 - r) * 2 * CELL, 2 * CELL)
            pred = lax.dot_general(s_refs[slot][...], read_ref[pl.ds(half, 2 * CELL), :], NT, preferred_element_type=F32)
            for d in range(2):
                xs_ref[2 + 4 * r + 2 * r + d] = edge_refs[slot][d].astype(F32)
                xs_ref[2 + 4 * r + 2 * (1 - r) + d] = latitude(pred, d).astype(BF).astype(F32)
        if far_refs:
            for d in range(4):
                xs_ref[2 + 4 * rows_at[1] + d] = far_refs[0][d].astype(F32)
            s_refs = [s_refs[0], far_refs[1]]

    for slot in (1, 0):
        r = rows_at[slot]
        band = band_ref[r]
        in_ref[...] = windows([xs_ref[4 * r + d] for d in range(8)], False)
        blocks = iidx_ref.shape[1]
        pres = [block_pre(b, band, s_refs[slot], in_ref, cidx_ref, iidx_ref, w_refs[slot]) for b in range(blocks)]
        if slot < slots:
            if not last:
                for b in range(blocks):
                    pre_refs[slot][:, b * BLK : (b + 1) * BLK] = pres[b]
            else:
                for b in range(blocks):
                    pre_ref[:, b * BLK : (b + 1) * BLK] = pres[b]
                per = pre_ref.shape[0] // 4
                short = per - 2 * MEM
                for res in range(4):
                    pre_refs[slot][res * short : (res + 1) * short] = pre_ref[res * per + MEM : (res + 1) * per - MEM]
            continue
        state = jnp.concatenate([jnp.tanh(p).astype(BF) for p in pres], axis=1)
        pred = lax.dot_general(state, read_ref[...], NT, preferred_element_type=F32)
        if not last:
            for d in range(4):
                out_far[0][d] = latitude(pred, d).astype(BF)
            out_far[1][...] = state
            continue
        for d in range(4):
            out_far[0][d] = latitude(pred, d)[MEM:-MEM].astype(BF)
        stage_ref, sem = take(2)
        per = state.shape[0] // 4
        put_states(r, state, per, MEM, stage_ref, out_far[1], sem)


def put_states(r, state, per, skip, stage_ref, states_hbm, sem):
    for res in range(4):
        for q in range((per - 2 * skip) // MEM):
            at = res * per + skip + q * MEM
            stage_ref[4 * q + res] = state[at : at + MEM]
    copy = pltpu.make_async_copy(stage_ref, states_hbm.at[r], sem)
    copy.start()
    copy.wait()


def late_kernel(slot, last, final, row_ref, band_ref, iidx_ref, w_ref, read_ref, pre_ref, got_ref, *rest):
    r = row_of(slot, row_ref)
    band = band_ref[r]
    in_ref = rest[-1]
    in_ref[...] = windows([unpack(got_ref[k]) for k in range(2)], last)
    parts = []
    for b in range(iidx_ref.shape[1]):
        k = iidx_ref[band, b] - 15 * r
        used = jnp.logical_and(k >= 0, k < 5)
        at = pl.multiple_of(jnp.where(used, k, 0) * BLK, BLK)
        term = lax.dot_general(in_ref[:, pl.ds(at, BLK)], w_ref[b, :, 2 * BLK :], NT, preferred_element_type=F32)
        pre = pre_ref[:, b * BLK : (b + 1) * BLK] + jnp.where(used, term, 0.0)
        parts.append(jnp.tanh(pre).astype(BF))
    state = jnp.concatenate(parts, axis=1)
    if not last:
        msg_ref, edge_ref, s_ref = rest[:3]
        s_ref[...] = state
        half = pl.multiple_of(r * 2 * CELL, 2 * CELL)
        pred = lax.dot_general(state, read_ref[pl.ds(half, 2 * CELL), :], NT, preferred_element_type=F32)
        for d in range(2):
            row = latitude(pred, d)
            pack(row, msg_ref, d)
            edge_ref[d] = row.astype(BF)
        return
    pred = lax.dot_general(state, read_ref[...], NT, preferred_element_type=F32)
    mine = [latitude(pred, d) for d in range(4)]
    per = state.shape[0] // 4
    if not final:
        lats_ref, states_hbm, stage_ref, sem = rest[:4]
        for d in range(4):
            lats_ref[d] = mine[d].astype(BF)
        put_states(r, state, per, 0, stage_ref, states_hbm, sem)
        return
    other_ref, _, field_ref, states_hbm, stage_ref, sem = rest[:6]
    other = [other_ref[d].astype(F32) for d in range(4)]
    low = r == 0
    rows = [jnp.where(low, mine[d], other[d])[None] for d in range(4)]
    rows += [jnp.where(low, other[d], mine[d])[None] for d in range(4)]
    tiles = jnp.transpose(jnp.concatenate(rows, axis=0), (1, 0, 2)).astype(BF)
    for q in range(field_ref.shape[2] // CHUNK):
        for m in range(MEM):
            field_ref[m, :, q * CHUNK : (q + 1) * CHUNK] = tiles[q * MEM + m]
    put_states(r, state, per, 0, stage_ref, states_hbm, sem)


def call(kernel, out_shape, out_specs, scratch, operands, flops=0, aliases=None):
    arrays = [pltpu.with_memory_space_constraint(x, pltpu.HBM) if s is HB else x for x, s in operands]
    size = sum(x.size * x.dtype.itemsize for x, _ in operands)
    return pl.pallas_call(
        kernel,
        out_shape=out_shape,
        in_specs=[s for _, s in operands],
        out_specs=out_specs,
        scratch_shapes=scratch,
        input_output_aliases=aliases or {},
        compiler_params=pltpu.CompilerParams(vmem_limit_bytes=40 * 1024 * 1024),
        cost_estimate=pl.CostEstimate(flops=flops, bytes_accessed=size, transcendentals=0),
    )(*arrays)


def per_device(field_state, reservoir_state, coupling_blocks, coupling_index, input_blocks, input_index, readout, region_band):
    lat_count, lon_count = lax.axis_size("lat"), lax.axis_size("lon")
    lat_at = lax.axis_index("lat").astype(jnp.int32)
    lon_at = lax.axis_index("lon").astype(jnp.int32)
    region_rows, regions, members, units = reservoir_state.shape
    bands = coupling_blocks.shape[0]
    blocks = units // BLK
    outs = readout.shape[1]
    assert region_rows == 2 and members == MEM and regions % 4 == 0 and lon_count % 2 == 0
    chunks = regions // 4
    own_rows = chunks * MEM
    wide = own_rows + 2 * MEM
    rows = 4 * wide
    short = 4 * own_rows
    swap = lat_count == 2
    slots = 1 if swap else 2

    def bf(*dims):
        return jax.ShapeDtypeStruct(dims, BF)

    def vm(dims, dtype=BF):
        return pltpu.VMEM(dims, dtype)

    def trade(x, offset):
        pairs = []
        for j in range(lon_count):
            step = 1 if (j - offset) % 2 == 0 else -1
            pairs.append((j, (j + step) % lon_count))
        return lax.ppermute(x, "lon", pairs)

    def across(xs):
        if swap:
            return [lax.ppermute(xs[0], "lat", [(0, 1), (1, 0)])]
        up = lax.ppermute(xs[0], "lat", [(i + 1, i) for i in range(lat_count - 1)])
        down = lax.ppermute(xs[1], "lat", [(i, i + 1) for i in range(lat_count - 1)])
        return [down, up]

    row = ((1 - lat_at if swap else lat_at * 0).reshape(1), SM)
    parity = ((lon_at % 2).reshape(1), SM)
    band, cidx, iidx = (region_band, SM), (coupling_index.transpose(0, 2, 1), SM), (input_index, SM)
    flops = 2 * rows * units * (3 * BLK + outs)

    mail = call(
        message_kernel,
        [bf(4, 2 * MEM, 2 * HALF)] * 2,
        [VM] * 2,
        [vm((2, MEM, 8, HALF)), vm((2, region_rows, 2, MEM, units)), pltpu.SemaphoreType.DMA((4,))],
        [parity, (field_state, HB), (reservoir_state, HB)],
    )
    second = trade(mail[1], 1)
    first = trade(mail[0], 0)
    own, s0, s1, w0, w1, read = call(
        setup_kernel,
        [bf(8, own_rows, CHUNK), bf(short, units), bf(short, units), bf(blocks, BLK, 3 * BLK), bf(blocks, BLK, 3 * BLK), bf(outs, units)],
        [VM] * 6,
        [vm(field_state.shape), vm(reservoir_state.shape), pltpu.SemaphoreType.DMA((9,))],
        [
            row,
            band,
            (field_state, HB),
            (reservoir_state, HB),
            (coupling_blocks.reshape(bands, blocks, 2, BLK, BLK), HB),
            (input_blocks.reshape(bands, blocks, BLK, BLK), HB),
            (readout, HB),
        ],
        flops,
    )
    weights = [(w0, VM), (w1, VM), (read, VM)]
    sent = call(
        functools.partial(first_edge_kernel, slots),
        [bf(2, own_rows, CHUNK + HALF // 2)] * slots,
        [VM] * slots,
        [],
        [parity, row, (own, VM), (first, VM), (second, VM)],
    )
    source = [(x, VM) for x in (own, s0, s1, first, second)]
    states_shape = bf(region_rows, regions, MEM, units)
    stage = [vm((regions, MEM, units)), pltpu.SemaphoreType.DMA]

    for step in range(STEPS):
        last = step == STEPS - 1
        got = across(sent)
        pre_rows = short if last else rows
        out = [jax.ShapeDtypeStruct((pre_rows, units), F32)] * slots
        specs = [VM] * slots
        scratch = [vm((12, wide, CHUNK), F32), vm((rows, 16 * CELL)), vm((rows, units)), vm((rows, units)), vm((rows, units), F32)]
        if swap:
            out += [bf(4, own_rows if last else wide, CHUNK), states_shape if last else bf(rows, units)]
            specs += [VM, HB if last else VM]
            scratch += stage if last else []
        shadow = call(
            functools.partial(shadow_kernel, step == 0, last, slots),
            out,
            specs,
            scratch,
            [row, parity, band, cidx, iidx] + weights + source,
            2 * flops,
        )
        far = shadow[slots:]
        sent, edges, states = [None] * slots, [None] * slots, [None] * slots
        for slot in reversed(range(slots)):
            operands = [row, band, iidx, weights[slot], weights[2], (shadow[slot], VM), (got[slot], VM)]
            inputs = [vm((pre_rows, 4 * CELL))]
            if not last:
                sent[slot], edges[slot], states[slot] = call(
                    functools.partial(late_kernel, slot, False, False),
                    [bf(2, own_rows, CHUNK + NEAR // 2), bf(2, wide, CHUNK), bf(rows, units)],
                    [VM] * 3,
                    inputs,
                    operands,
                    flops,
                )
            elif slot == 1:
                far = call(
                    functools.partial(late_kernel, slot, True, False),
                    [bf(4, own_rows, CHUNK), states_shape],
                    [VM, HB],
                    stage + inputs,
                    operands,
                    flops,
                )
            else:
                return call(
                    functools.partial(late_kernel, slot, True, True),
                    [bf(MEM, 8, regions * CELL), states_shape],
                    [VM, HB],
                    stage + inputs,
                    operands + [(far[0], VM), (far[1], HB)],
                    flops,
                    {len(operands) + 1: 1},
                )
        source = [(x, VM) for x in edges + states + list(far)]


def solution(mesh):
    return jax.shard_map(
        per_device,
        mesh=mesh,
        in_specs=(
            P(None, "lat", "lon"),
            P("lat", "lon", None, None),
            P("lat", None, None),
            P("lat", None, None),
            P("lat", None, None),
            P("lat", None),
            P("lat", None, None),
            P("lat"),
        ),
        out_specs=(P(None, "lat", "lon"), P("lat", "lon", None, None)),
        check_vma=False,
    )
```

```python
import functools

import jax
import jax.numpy as jnp
from jax import lax
from jax.experimental import pallas as pl
from jax.experimental.pallas import tpu as pltpu
from jax.sharding import PartitionSpec as P

VARS = 40
STEPS = 3
CELL = 4 * VARS
CHUNK = 4 * CELL
HALF = 512
NEAR = 256
MEM = 4
BLK = 128
BF = jnp.bfloat16
F32 = jnp.float32
VM = pl.BlockSpec(memory_space=pltpu.VMEM)
SM = pl.BlockSpec(memory_space=pltpu.SMEM)
HB = pl.BlockSpec(memory_space=pltpu.HBM)
NT = (((1,), (1,)), ((), ()))


def row_of(slot, row_ref):
    return row_ref[0] if slot == 0 else 1 - row_ref[0]


def message_kernel(parity_ref, field_hbm, state_hbm, band_hbm, cidx_hbm, iidx_hbm, first_ref, second_ref, own_ref, band_ref, cidx_ref, iidx_ref, field_ref, state_ref, sems):
    odd = parity_ref[0]
    regions = state_hbm.shape[1]
    pairs = [(field_hbm, field_ref)]
    for k in range(2):
        low = odd if k == 0 else 1 - odd
        at = (1 - low) * (regions - 2)
        pairs.append((state_hbm.at[:, pl.ds(at, 2)], state_ref.at[k]))
    pairs += [(band_hbm, band_ref), (cidx_hbm, cidx_ref), (iidx_hbm, iidx_ref)]
    copies = [pltpu.make_async_copy(src, dst, sems.at[i]) for i, (src, dst) in enumerate(pairs)]
    for c in copies:
        c.start()
    chunks = field_ref.shape[2] // CHUNK
    copies[0].wait()
    tiles = []
    for q in range(chunks):
        for m in range(MEM):
            tiles.append(field_ref[m, :, q * CHUNK : (q + 1) * CHUNK].astype(F32)[None])
    rows = jnp.transpose(jnp.concatenate(tiles, axis=0), (1, 0, 2)).astype(BF)
    own_ref[...] = rows
    last = (chunks - 1) * MEM
    for k, out in enumerate((first_ref, second_ref)):
        low = (odd if k == 0 else 1 - odd) == 1
        for d in range(8):
            at, lane = (d % 2) * MEM, (d // 2 % 2) * HALF
            out[2 + d // 4, at : at + MEM, lane : lane + HALF] = jnp.where(low, rows[d, :MEM, :HALF], rows[d, last:, CHUNK - HALF :])
    for c in copies[1:]:
        c.wait()
    for k, out in enumerate((first_ref, second_ref)):
        for r in range(2):
            for j in range(2):
                out[r, j * MEM : (j + 1) * MEM] = state_ref[k, r, j]


def pack(row, out_ref, k):
    last = row.shape[0] - MEM
    out_ref[k, :, :CHUNK] = row[MEM:last].astype(BF)
    half = NEAR // 2
    ends = [row[:MEM, CHUNK - NEAR : CHUNK - half], row[:MEM, CHUNK - half :], row[last:, :half], row[last:, half:NEAR]]
    out_ref[k, :, CHUNK:] = jnp.concatenate(ends, axis=0).astype(BF)


def unpack(msg):
    x = msg.astype(F32)
    own, ends = x[:, :CHUNK], x[:, CHUNK:]
    fill = jnp.zeros((MEM, CHUNK - 2 * ends.shape[1]), F32)
    before = jnp.concatenate([fill, ends[:MEM], ends[MEM : 2 * MEM]], axis=1)
    after = jnp.concatenate([ends[2 * MEM : 3 * MEM], ends[3 * MEM :], fill], axis=1)
    return jnp.concatenate([before, own, after], axis=0)


def sides(parity_ref, first, second):
    odd = parity_ref[0] == 1
    return jnp.where(odd, first, second), jnp.where(odd, second, first)


def first_edge_kernel(slots, parity_ref, row_ref, own_ref, first_ref, second_ref, *outs):
    for slot in range(slots):
        r = row_of(slot, row_ref)
        for k in range(2):
            at = k * MEM
            got = []
            for ref in (first_ref, second_ref):
                low = ref[2, at : at + MEM, :HALF].astype(F32)
                high = ref[3, at : at + MEM, HALF : 2 * HALF].astype(F32)
                got.append(jnp.where(r == 0, low, high))
            left, right = sides(parity_ref, *got)
            half = HALF // 2
            ends = [left[:, :half], left[:, half:], right[:, :half], right[:, half:]]
            outs[slot][k, :, :CHUNK] = own_ref[6 * r + k]
            outs[slot][k, :, CHUNK:] = jnp.concatenate(ends, axis=0).astype(BF)


def windows(lats, narrow):
    parts = [[] for _ in range(4)]
    for a in lats:
        rows = a.shape[0]
        before = jnp.concatenate([a[rows - MEM :, CHUNK - 2 * VARS :], a[: rows - MEM, CHUNK - 2 * VARS :]], axis=0)
        after = jnp.concatenate([a[MEM:, : 2 * VARS], a[:MEM, : 2 * VARS]], axis=0)
        ext = jnp.concatenate([before, a, after], axis=1)
        if narrow:
            ext = ext[MEM : rows - MEM]
        for res in range(4):
            parts[res].append(ext[:, CELL * res : CELL * res + 2 * CELL])
    return jnp.concatenate([jnp.concatenate(p, axis=1) for p in parts], axis=0).astype(BF)


def latitude(pred, d):
    per = pred.shape[0] // 4
    return jnp.concatenate([pred[res * per : (res + 1) * per, d * CELL : (d + 1) * CELL] for res in range(4)], axis=1)


def block_pre(b, band, s_ref, in_ref, cidx_ref, iidx_ref, w_ref):
    pieces = []
    for k in range(2):
        pieces.append(s_ref[:, pl.ds(pl.multiple_of(cidx_ref[band, k, b] * BLK, BLK), BLK)])
    pieces.append(in_ref[:, pl.ds(pl.multiple_of(iidx_ref[band, b] * BLK, BLK), BLK)])
    return lax.dot_general(jnp.concatenate(pieces, axis=1), w_ref[b], NT, preferred_element_type=F32)


def shadow_kernel(first, last, slots, row_ref, parity_ref, band_ref, cidx_ref, iidx_ref, *rest):
    rest = list(rest)

    def take(n):
        got = rest[:n]
        del rest[:n]
        return got

    if first:
        own_ref, first_ref, second_ref, state_hbm, coup_hbm, inp_hbm, read_hbm = take(7)
    else:
        w0_ref, w1_ref, read_ref = take(3)
        edge_refs, s_refs = take(slots), take(slots)
        far_refs = take(2 * (2 - slots))
    pre_refs = take(slots)
    out_far = take(2 * (2 - slots))
    if first:
        w0_ref, w1_ref, read_ref = take(3)
    xs_ref, in_ref = take(2)
    rows_at = [row_of(0, row_ref), row_of(1, row_ref)]
    w_refs = [w0_ref, w1_ref]
    waits = {}
    if first:
        sc0_ref, sc1_ref, state_ref, sems = take(4)
        pairs = {"state": [(state_hbm, state_ref)]}
        for slot in (1, 0):
            band = band_ref[rows_at[slot]]
            pairs[slot] = [(coup_hbm.at[band, :, k], w_refs[slot].at[:, :, k * BLK : (k + 1) * BLK]) for k in range(2)]
            pairs[slot].append((inp_hbm.at[band], w_refs[slot].at[:, :, 2 * BLK :]))
        pairs["read"] = [(read_hbm.at[0], read_ref)]
        count = 0
        for name in ("state", 1, "read", 0):
            waits[name] = []
            for src, dst in pairs[name]:
                copy = pltpu.make_async_copy(src, dst, sems.at[count])
                copy.start()
                waits[name].append(copy)
                count += 1

    def ready(name):
        for copy in waits.pop(name, []):
            copy.wait()

    for k in range(2):
        xs_ref[k] = jnp.zeros(xs_ref.shape[1:], F32)
        xs_ref[10 + k] = jnp.zeros(xs_ref.shape[1:], F32)
    if first:
        fill = jnp.zeros((MEM, CHUNK - HALF), F32)
        left, right = sides(parity_ref, first_ref[...].astype(F32), second_ref[...].astype(F32))
        for d in range(8):
            at, lane = (d % 2) * MEM, (d // 2 % 2) * HALF
            lo = jnp.concatenate([fill, left[2 + d // 4, at : at + MEM, lane : lane + HALF]], axis=1)
            hi = jnp.concatenate([right[2 + d // 4, at : at + MEM, lane : lane + HALF], fill], axis=1)
            xs_ref[2 + d] = jnp.concatenate([lo, own_ref[d].astype(F32), hi], axis=0)
        ready("state")
        empty = jnp.zeros((MEM, state_ref.shape[3]), F32)
        chunks = state_ref.shape[1] // 4
        for slot, dst in enumerate((sc0_ref, sc1_ref)):
            low = rows_at[slot] == 0
            lo, hi = jnp.where(low, left[0], left[1]), jnp.where(low, right[0], right[1])
            rows = []
            for res in range(4):
                rows.append(lo[(res - 2) * MEM : (res - 1) * MEM] if res >= 2 else empty)
                rows += [state_ref[rows_at[slot], 4 * q + res].astype(F32) for q in range(chunks)]
                rows.append(hi[res * MEM : (res + 1) * MEM] if res < 2 else empty)
            dst[...] = jnp.concatenate(rows, axis=0).astype(BF)
        s_refs = [sc0_ref, sc1_ref]
    else:
        for slot in range(slots):
            r = rows_at[slot]
            half = pl.multiple_of((1 - r) * 2 * CELL, 2 * CELL)
            pred = lax.dot_general(s_refs[slot][...], read_ref[pl.ds(half, 2 * CELL), :], NT, preferred_element_type=F32)
            for d in range(2):
                xs_ref[2 + 4 * r + 2 * r + d] = edge_refs[slot][d].astype(F32)
                xs_ref[2 + 4 * r + 2 * (1 - r) + d] = latitude(pred, d).astype(BF).astype(F32)
        if far_refs:
            for d in range(4):
                xs_ref[2 + 4 * rows_at[1] + d] = far_refs[0][d].astype(F32)
            s_refs = [s_refs[0], far_refs[1]]

    for slot in (1, 0):
        r = rows_at[slot]
        band = band_ref[r]
        in_ref[...] = windows([xs_ref[4 * r + d] for d in range(8)], False)
        blocks = iidx_ref.shape[1]
        ready(slot)
        pres = [block_pre(b, band, s_refs[slot], in_ref, cidx_ref, iidx_ref, w_refs[slot]) for b in range(blocks)]
        if slot < slots:
            if not last:
                for b in range(blocks):
                    pre_refs[slot][:, b * BLK : (b + 1) * BLK] = pres[b]
            else:
                pre_ref = take(1)[0]
                for b in range(blocks):
                    pre_ref[:, b * BLK : (b + 1) * BLK] = pres[b]
                per = pre_ref.shape[0] // 4
                short = per - 2 * MEM
                for res in range(4):
                    pre_refs[slot][res * short : (res + 1) * short] = pre_ref[res * per + MEM : (res + 1) * per - MEM]
            continue
        state = jnp.concatenate([jnp.tanh(p).astype(BF) for p in pres], axis=1)
        if last:
            stage_ref, sem = take(2)
            waits["out"] = [put_states(r, state, MEM, stage_ref, out_far[1], sem)]
        ready("read")
        pred = lax.dot_general(state, read_ref[...], NT, preferred_element_type=F32)
        if not last:
            for d in range(4):
                out_far[0][d] = latitude(pred, d).astype(BF)
            out_far[1][...] = state
            continue
        for d in range(4):
            out_far[0][d] = latitude(pred, d)[MEM:-MEM].astype(BF)
    for name in list(waits):
        ready(name)


def put_states(r, state, skip, stage_ref, states_hbm, sem):
    per = state.shape[0] // 4
    for res in range(4):
        for q in range((per - 2 * skip) // MEM):
            at = res * per + skip + q * MEM
            stage_ref[4 * q + res] = state[at : at + MEM]
    copy = pltpu.make_async_copy(stage_ref, states_hbm.at[r], sem)
    copy.start()
    return copy


def late_kernel(slot, last, final, row_ref, band_ref, iidx_ref, w_ref, read_ref, pre_ref, got_ref, *rest):
    r = row_of(slot, row_ref)
    band = band_ref[r]
    in_ref = rest[-1]
    in_ref[...] = windows([unpack(got_ref[k]) for k in range(2)], last)
    parts = []
    for b in range(iidx_ref.shape[1]):
        k = iidx_ref[band, b] - 15 * r
        used = jnp.logical_and(k >= 0, k < 5)
        at = pl.multiple_of(jnp.where(used, k, 0) * BLK, BLK)
        term = lax.dot_general(in_ref[:, pl.ds(at, BLK)], w_ref[b, :, 2 * BLK :], NT, preferred_element_type=F32)
        pre = pre_ref[:, b * BLK : (b + 1) * BLK] + jnp.where(used, term, 0.0)
        parts.append(jnp.tanh(pre).astype(BF))
    state = jnp.concatenate(parts, axis=1)
    if not last:
        msg_ref, edge_ref, s_ref = rest[:3]
        s_ref[...] = state
        half = pl.multiple_of(r * 2 * CELL, 2 * CELL)
        pred = lax.dot_general(state, read_ref[pl.ds(half, 2 * CELL), :], NT, preferred_element_type=F32)
        for d in range(2):
            row = latitude(pred, d)
            pack(row, msg_ref, d)
            edge_ref[d] = row.astype(BF)
        return
    if not final:
        lats_ref, states_hbm, stage_ref, sem = rest[:4]
    else:
        other_ref, _, field_hbm, states_hbm, stage_ref, sem, field_ref, field_sem = rest[:8]
    copy = put_states(r, state, 0, stage_ref, states_hbm, sem)
    pred = lax.dot_general(state, read_ref[...], NT, preferred_element_type=F32)
    mine = [latitude(pred, d) for d in range(4)]
    if not final:
        for d in range(4):
            lats_ref[d] = mine[d].astype(BF)
        copy.wait()
        return
    other = [other_ref[d].astype(F32) for d in range(4)]
    low = r == 0
    rows = [jnp.where(low, mine[d], other[d])[None] for d in range(4)]
    rows += [jnp.where(low, other[d], mine[d])[None] for d in range(4)]
    tiles = jnp.transpose(jnp.concatenate(rows, axis=0), (1, 0, 2)).astype(BF)
    for q in range(field_ref.shape[2] // CHUNK):
        for m in range(MEM):
            field_ref[m, :, q * CHUNK : (q + 1) * CHUNK] = tiles[q * MEM + m]
    out = pltpu.make_async_copy(field_ref, field_hbm, field_sem)
    out.start()
    copy.wait()
    out.wait()


def call(kernel, out_shape, out_specs, scratch, operands, flops=0, aliases=None):
    arrays = [pltpu.with_memory_space_constraint(x, pltpu.HBM) if s is HB else x for x, s in operands]
    size = sum(x.size * x.dtype.itemsize for x, _ in operands)
    return pl.pallas_call(
        kernel,
        out_shape=out_shape,
        in_specs=[s for _, s in operands],
        out_specs=out_specs,
        scratch_shapes=scratch,
        input_output_aliases=aliases or {},
        compiler_params=pltpu.CompilerParams(vmem_limit_bytes=40 * 1024 * 1024),
        cost_estimate=pl.CostEstimate(flops=flops, bytes_accessed=size, transcendentals=0),
    )(*arrays)


def per_device(field_state, reservoir_state, coupling_blocks, coupling_index, input_blocks, input_index, readout, region_band):
    lat_count, lon_count = lax.axis_size("lat"), lax.axis_size("lon")
    lat_at = lax.axis_index("lat").astype(jnp.int32)
    lon_at = lax.axis_index("lon").astype(jnp.int32)
    region_rows, regions, members, units = reservoir_state.shape
    bands = coupling_blocks.shape[0]
    blocks = units // BLK
    outs = readout.shape[1]
    assert region_rows == 2 and members == MEM and regions % 4 == 0 and lon_count % 2 == 0
    chunks = regions // 4
    own_rows = chunks * MEM
    wide = own_rows + 2 * MEM
    rows = 4 * wide
    short = 4 * own_rows
    swap = lat_count == 2
    slots = 1 if swap else 2

    def bf(*dims):
        return jax.ShapeDtypeStruct(dims, BF)

    def vm(dims, dtype=BF):
        return pltpu.VMEM(dims, dtype)

    def trade(x, offset):
        pairs = []
        for j in range(lon_count):
            step = 1 if (j - offset) % 2 == 0 else -1
            pairs.append((j, (j + step) % lon_count))
        return lax.ppermute(x, "lon", pairs)

    def across(xs):
        if swap:
            return [lax.ppermute(xs[0], "lat", [(0, 1), (1, 0)])]
        up = lax.ppermute(xs[0], "lat", [(i + 1, i) for i in range(lat_count - 1)])
        down = lax.ppermute(xs[1], "lat", [(i, i + 1) for i in range(lat_count - 1)])
        return [down, up]

    row = ((1 - lat_at if swap else lat_at * 0).reshape(1), SM)
    parity = ((lon_at % 2).reshape(1), SM)
    flops = 2 * rows * units * (3 * BLK + outs)

    small = [region_band, coupling_index.transpose(0, 2, 1), input_index]
    mail = call(
        message_kernel,
        [bf(4, 2 * MEM, 2 * HALF)] * 2 + [bf(8, own_rows, CHUNK)] + [jax.ShapeDtypeStruct(x.shape, x.dtype) for x in small],
        [VM] * 3 + [SM] * 3,
        [vm(field_state.shape), vm((2, region_rows, 2, MEM, units)), pltpu.SemaphoreType.DMA((6,))],
        [parity, (field_state, HB), (reservoir_state, HB)] + [(x, HB) for x in small],
    )
    first = trade(mail[0], 0)
    second = trade(mail[1], 1)
    own = mail[2]
    band, cidx, iidx = [(x, SM) for x in mail[3:]]
    sent = call(
        functools.partial(first_edge_kernel, slots),
        [bf(2, own_rows, CHUNK + HALF // 2)] * slots,
        [VM] * slots,
        [],
        [parity, row, (own, VM), (first, VM), (second, VM)],
    )
    source = [(x, VM) for x in (own, first, second)] + [
        (reservoir_state, HB),
        (coupling_blocks.reshape(bands, blocks, 2, BLK, BLK), HB),
        (input_blocks.reshape(bands, blocks, BLK, BLK), HB),
        (readout, HB),
    ]
    states_shape = bf(region_rows, regions, MEM, units)
    stage = [vm((regions, MEM, units)), pltpu.SemaphoreType.DMA]

    for step in range(STEPS):
        last = step == STEPS - 1
        got = across(sent)
        pre_rows = short if last else rows
        out = [jax.ShapeDtypeStruct((pre_rows, units), F32)] * slots
        specs = [VM] * slots
        scratch = [vm((12, wide, CHUNK), F32), vm((rows, 16 * CELL))]
        if swap:
            out += [bf(4, own_rows if last else wide, CHUNK), states_shape if last else bf(rows, units)]
            specs += [VM, HB if last else VM]
            scratch += stage if last else []
        if last:
            scratch += [vm((rows, units), F32)] * slots
        if step == 0:
            out += [bf(blocks, BLK, 3 * BLK)] * 2 + [bf(outs, units)]
            specs += [VM] * 3
            scratch += [vm((rows, units))] * 2 + [vm(reservoir_state.shape), pltpu.SemaphoreType.DMA((8,))]
        shadow = call(
            functools.partial(shadow_kernel, step == 0, last, slots),
            out,
            specs,
            scratch,
            [row, parity, band, cidx, iidx] + source,
            2 * flops,
        )
        far = shadow[slots : slots + 2 * (2 - slots)]
        if step == 0:
            weights = [(x, VM) for x in shadow[-3:]]
        sent, edges, states = [None] * slots, [None] * slots, [None] * slots
        for slot in reversed(range(slots)):
            operands = [row, band, iidx, weights[slot], weights[2], (shadow[slot], VM), (got[slot], VM)]
            inputs = [vm((pre_rows, 4 * CELL))]
            if not last:
                sent[slot], edges[slot], states[slot] = call(
                    functools.partial(late_kernel, slot, False, False),
                    [bf(2, own_rows, CHUNK + NEAR // 2), bf(2, wide, CHUNK), bf(rows, units)],
                    [VM] * 3,
                    inputs,
                    operands,
                    flops,
                )
            elif slot == 1:
                far = call(
                    functools.partial(late_kernel, slot, True, False),
                    [bf(4, own_rows, CHUNK), states_shape],
                    [VM, HB],
                    stage + inputs,
                    operands,
                    flops,
                )
            else:
                return call(
                    functools.partial(late_kernel, slot, True, True),
                    [bf(MEM, 8, regions * CELL), states_shape],
                    [HB, HB],
                    stage + [vm((MEM, 8, regions * CELL)), pltpu.SemaphoreType.DMA] + inputs,
                    operands + [(far[0], VM), (far[1], HB)],
                    flops,
                    {len(operands) + 1: 1},
                )
        source = weights + [(x, VM) for x in edges + states + list(far)]


def solution(mesh):
    return jax.shard_map(
        per_device,
        mesh=mesh,
        in_specs=(
            P(None, "lat", "lon"),
            P("lat", "lon", None, None),
            P("lat", None, None),
            P("lat", None, None),
            P("lat", None, None),
            P("lat", None),
            P("lat", None, None),
            P("lat"),
        ),
        out_specs=(P(None, "lat", "lon"), P("lat", "lon", None, None)),
        check_vma=False,
    )
```

```python
import functools

import jax
import jax.numpy as jnp
from jax import lax
from jax.experimental import pallas as pl
from jax.experimental.pallas import tpu as pltpu
from jax.sharding import PartitionSpec as P

VARS = 40
STEPS = 3
CELL = 4 * VARS
CHUNK = 4 * CELL
HALF = 512
NEAR = 256
MEM = 4
BLK = 128
BF = jnp.bfloat16
F32 = jnp.float32
VM = pl.BlockSpec(memory_space=pltpu.VMEM)
SM = pl.BlockSpec(memory_space=pltpu.SMEM)
HB = pl.BlockSpec(memory_space=pltpu.HBM)
NT = (((1,), (1,)), ((), ()))


def row_of(slot, row_ref):
    return row_ref[0] if slot == 0 else 1 - row_ref[0]


def message_kernel(parity_ref, field_hbm, state_hbm, first_ref, second_ref, field_ref, state_ref, sems):
    odd = parity_ref[0]
    lanes = field_hbm.shape[2] - HALF
    regions = state_hbm.shape[1]
    copies = []
    for k in range(2):
        low = odd if k == 0 else 1 - odd
        lane = pl.multiple_of((1 - low) * lanes, BLK)
        copies.append(pltpu.make_async_copy(field_hbm.at[:, :, pl.ds(lane, HALF)], field_ref.at[k], sems.at[k]))
        at = (1 - low) * (regions - 2)
        copies.append(pltpu.make_async_copy(state_hbm.at[:, pl.ds(at, 2)], state_ref.at[k], sems.at[2 + k]))
    for c in copies:
        c.start()
    for c in copies:
        c.wait()
    for k, out in enumerate((first_ref, second_ref)):
        for r in range(2):
            for j in range(2):
                out[r, j * MEM : (j + 1) * MEM] = state_ref[k, r, j]
        rows = jnp.transpose(field_ref[k].astype(F32), (1, 0, 2)).astype(BF)
        for d in range(8):
            at, lane = (d % 2) * MEM, (d // 2 % 2) * HALF
            out[2 + d // 4, at : at + MEM, lane : lane + HALF] = rows[d]


def own_kernel(row_ref, field_hbm, state_hbm, coup_hbm, inp_hbm, own_ref, s0_ref, s1_ref, w_ref, field_ref, state_ref, sems):
    copies = []

    def start(src, dst):
        copies.append(pltpu.make_async_copy(src, dst, sems.at[len(copies)]))
        copies[-1].start()

    start(field_hbm, field_ref)
    start(state_hbm, state_ref)
    for k in range(2):
        start(coup_hbm.at[:, :, k], w_ref.at[:, :, :, k * BLK : (k + 1) * BLK])
    start(inp_hbm, w_ref.at[:, :, :, 2 * BLK :])
    chunks = field_ref.shape[2] // CHUNK
    copies[0].wait()
    tiles = []
    for q in range(chunks):
        for m in range(MEM):
            tiles.append(field_ref[m, :, q * CHUNK : (q + 1) * CHUNK].astype(F32)[None])
    own_ref[...] = jnp.transpose(jnp.concatenate(tiles, axis=0), (1, 0, 2)).astype(BF)
    copies[1].wait()
    for slot, s_ref in enumerate((s0_ref, s1_ref)):
        r = row_of(slot, row_ref)
        rows = [state_ref[r, 4 * q + res].astype(F32) for res in range(4) for q in range(chunks)]
        s_ref[...] = jnp.concatenate(rows, axis=0).astype(BF)
    for c in copies[2:]:
        c.wait()


def pack(row, out_ref, k):
    last = row.shape[0] - MEM
    out_ref[k, :, :CHUNK] = row[MEM:last].astype(BF)
    half = NEAR // 2
    ends = [row[:MEM, CHUNK - NEAR : CHUNK - half], row[:MEM, CHUNK - half :], row[last:, :half], row[last:, half:NEAR]]
    out_ref[k, :, CHUNK:] = jnp.concatenate(ends, axis=0).astype(BF)


def unpack(msg):
    x = msg.astype(F32)
    own, ends = x[:, :CHUNK], x[:, CHUNK:]
    fill = jnp.zeros((MEM, CHUNK - 2 * ends.shape[1]), F32)
    before = jnp.concatenate([fill, ends[:MEM], ends[MEM : 2 * MEM]], axis=1)
    after = jnp.concatenate([ends[2 * MEM : 3 * MEM], ends[3 * MEM :], fill], axis=1)
    return jnp.concatenate([before, own, after], axis=0)


def sides(parity_ref, first, second):
    odd = parity_ref[0] == 1
    return jnp.where(odd, first, second), jnp.where(odd, second, first)


def first_edge_kernel(slots, parity_ref, row_ref, own_ref, first_ref, second_ref, *outs):
    for slot in range(slots):
        r = row_of(slot, row_ref)
        for k in range(2):
            at = k * MEM
            got = []
            for ref in (first_ref, second_ref):
                low = ref[2, at : at + MEM, :HALF].astype(F32)
                high = ref[3, at : at + MEM, HALF : 2 * HALF].astype(F32)
                got.append(jnp.where(r == 0, low, high))
            left, right = sides(parity_ref, *got)
            half = HALF // 2
            ends = [left[:, :half], left[:, half:], right[:, :half], right[:, half:]]
            outs[slot][k, :, :CHUNK] = own_ref[6 * r + k]
            outs[slot][k, :, CHUNK:] = jnp.concatenate(ends, axis=0).astype(BF)


def windows(lats, narrow):
    parts = [[] for _ in range(4)]
    for a in lats:
        rows = a.shape[0]
        before = jnp.concatenate([a[rows - MEM :, CHUNK - 2 * VARS :], a[: rows - MEM, CHUNK - 2 * VARS :]], axis=0)
        after = jnp.concatenate([a[MEM:, : 2 * VARS], a[:MEM, : 2 * VARS]], axis=0)
        ext = jnp.concatenate([before, a, after], axis=1)
        if narrow:
            ext = ext[MEM : rows - MEM]
        for res in range(4):
            parts[res].append(ext[:, CELL * res : CELL * res + 2 * CELL])
    return jnp.concatenate([jnp.concatenate(p, axis=1) for p in parts], axis=0).astype(BF)


def latitude(pred, d):
    per = pred.shape[0] // 4
    return jnp.concatenate([pred[res * per : (res + 1) * per, d * CELL : (d + 1) * CELL] for res in range(4)], axis=1)


def block_pre(b, band, s_ref, in_ref, cidx_ref, iidx_ref, w_ref):
    pieces = []
    for k in range(2):
        pieces.append(s_ref[:, pl.ds(pl.multiple_of(cidx_ref[band, k, b] * BLK, BLK), BLK)])
    pieces.append(in_ref[:, pl.ds(pl.multiple_of(iidx_ref[band, b] * BLK, BLK), BLK)])
    return lax.dot_general(jnp.concatenate(pieces, axis=1), w_ref[band, b], NT, preferred_element_type=F32)


def shadow_kernel(first, last, slots, row_ref, parity_ref, band_ref, cidx_ref, iidx_ref, *rest):
    rest = list(rest)

    def take(n):
        got = rest[:n]
        del rest[:n]
        return got

    w_ref = take(1)[0]
    if first:
        read_hbm, own_ref, s0_ref, s1_ref, first_ref, second_ref = take(6)
    else:
        read_ref = take(1)[0]
        edge_refs, s_refs = take(slots), take(slots)
        far_refs = take(2 * (2 - slots))
    pre_refs = take(slots)
    out_far = take(2 * (2 - slots))
    if first:
        read_ref = take(1)[0]
    xs_ref, in_ref = take(2)
    rows_at = [row_of(0, row_ref), row_of(1, row_ref)]
    waits = {}
    if first:
        sc0_ref, sc1_ref, sem = take(3)
        waits["read"] = pltpu.make_async_copy(read_hbm.at[0], read_ref, sem)
        waits["read"].start()

    def ready(name):
        if name in waits:
            waits.pop(name).wait()

    for k in range(2):
        xs_ref[k] = jnp.zeros(xs_ref.shape[1:], F32)
        xs_ref[10 + k] = jnp.zeros(xs_ref.shape[1:], F32)
    if first:
        fill = jnp.zeros((MEM, CHUNK - HALF), F32)
        left, right = sides(parity_ref, first_ref[...].astype(F32), second_ref[...].astype(F32))
        for d in range(8):
            at, lane = (d % 2) * MEM, (d // 2 % 2) * HALF
            lo = jnp.concatenate([fill, left[2 + d // 4, at : at + MEM, lane : lane + HALF]], axis=1)
            hi = jnp.concatenate([right[2 + d // 4, at : at + MEM, lane : lane + HALF], fill], axis=1)
            xs_ref[2 + d] = jnp.concatenate([lo, own_ref[d].astype(F32), hi], axis=0)
        empty = jnp.zeros((MEM, s0_ref.shape[1]), F32)
        per = s0_ref.shape[0] // 4
        for slot, (src, dst) in enumerate(((s0_ref, sc0_ref), (s1_ref, sc1_ref))):
            low = rows_at[slot] == 0
            lo, hi = jnp.where(low, left[0], left[1]), jnp.where(low, right[0], right[1])
            rows = []
            for res in range(4):
                rows.append(lo[(res - 2) * MEM : (res - 1) * MEM] if res >= 2 else empty)
                rows.append(src[res * per : (res + 1) * per].astype(F32))
                rows.append(hi[res * MEM : (res + 1) * MEM] if res < 2 else empty)
            dst[...] = jnp.concatenate(rows, axis=0).astype(BF)
        s_refs = [sc0_ref, sc1_ref]
    else:
        for slot in range(slots):
            r = rows_at[slot]
            half = pl.multiple_of((1 - r) * 2 * CELL, 2 * CELL)
            pred = lax.dot_general(s_refs[slot][...], read_ref[pl.ds(half, 2 * CELL), :], NT, preferred_element_type=F32)
            for d in range(2):
                xs_ref[2 + 4 * r + 2 * r + d] = edge_refs[slot][d].astype(F32)
                xs_ref[2 + 4 * r + 2 * (1 - r) + d] = latitude(pred, d).astype(BF).astype(F32)
        if far_refs:
            for d in range(4):
                xs_ref[2 + 4 * rows_at[1] + d] = far_refs[0][d].astype(F32)
            s_refs = [s_refs[0], far_refs[1]]

    far = []
    for slot in (1, 0):
        r = rows_at[slot]
        band = band_ref[r]
        in_ref[...] = windows([xs_ref[4 * r + d] for d in range(8)], False)
        blocks = iidx_ref.shape[1]
        pres = [block_pre(b, band, s_refs[slot], in_ref, cidx_ref, iidx_ref, w_ref) for b in range(blocks)]
        if slot >= slots:
            far = [jnp.concatenate([jnp.tanh(p).astype(BF) for p in pres], axis=1)]
            if last:
                stage_ref, sem = take(2)
                waits["out"] = put_states(r, far[0], MEM, stage_ref, out_far[1], sem)
        elif not last:
            for b in range(blocks):
                pre_refs[slot][:, b * BLK : (b + 1) * BLK] = pres[b]
        else:
            pre_ref = take(1)[0]
            for b in range(blocks):
                pre_ref[:, b * BLK : (b + 1) * BLK] = pres[b]
            per = pre_ref.shape[0] // 4
            short = per - 2 * MEM
            for res in range(4):
                pre_refs[slot][res * short : (res + 1) * short] = pre_ref[res * per + MEM : (res + 1) * per - MEM]
    ready("read")
    for state in far:
        pred = lax.dot_general(state, read_ref[...], NT, preferred_element_type=F32)
        for d in range(4):
            lat = latitude(pred, d).astype(BF)
            out_far[0][d] = lat[MEM:-MEM] if last else lat
        if not last:
            out_far[1][...] = state
    ready("out")


def put_states(r, state, skip, stage_ref, states_hbm, sem):
    per = state.shape[0] // 4
    for res in range(4):
        for q in range((per - 2 * skip) // MEM):
            at = res * per + skip + q * MEM
            stage_ref[4 * q + res] = state[at : at + MEM]
    copy = pltpu.make_async_copy(stage_ref, states_hbm.at[r], sem)
    copy.start()
    return copy


def late_kernel(slot, last, final, row_ref, band_ref, iidx_ref, w_ref, read_ref, pre_ref, got_ref, *rest):
    r = row_of(slot, row_ref)
    band = band_ref[r]
    in_ref = rest[-1]
    in_ref[...] = windows([unpack(got_ref[k]) for k in range(2)], last)
    parts = []
    for b in range(iidx_ref.shape[1]):
        k = iidx_ref[band, b] - 15 * r
        used = jnp.logical_and(k >= 0, k < 5)
        at = pl.multiple_of(jnp.where(used, k, 0) * BLK, BLK)
        term = lax.dot_general(in_ref[:, pl.ds(at, BLK)], w_ref[band, b, :, 2 * BLK :], NT, preferred_element_type=F32)
        pre = pre_ref[:, b * BLK : (b + 1) * BLK] + jnp.where(used, term, 0.0)
        parts.append(jnp.tanh(pre).astype(BF))
    state = jnp.concatenate(parts, axis=1)
    if not last:
        msg_ref, edge_ref, s_ref = rest[:3]
        s_ref[...] = state
        half = pl.multiple_of(r * 2 * CELL, 2 * CELL)
        pred = lax.dot_general(state, read_ref[pl.ds(half, 2 * CELL), :], NT, preferred_element_type=F32)
        for d in range(2):
            row = latitude(pred, d)
            pack(row, msg_ref, d)
            edge_ref[d] = row.astype(BF)
        return
    if not final:
        lats_ref, states_hbm, stage_ref, sem = rest[:4]
    else:
        other_ref, _, field_hbm, states_hbm, stage_ref, sem, field_ref, field_sem = rest[:8]
    copy = put_states(r, state, 0, stage_ref, states_hbm, sem)
    pred = lax.dot_general(state, read_ref[...], NT, preferred_element_type=F32)
    mine = [latitude(pred, d) for d in range(4)]
    if not final:
        for d in range(4):
            lats_ref[d] = mine[d].astype(BF)
        copy.wait()
        return
    other = [other_ref[d].astype(F32) for d in range(4)]
    low = r == 0
    rows = [jnp.where(low, mine[d], other[d])[None] for d in range(4)]
    rows += [jnp.where(low, other[d], mine[d])[None] for d in range(4)]
    tiles = jnp.transpose(jnp.concatenate(rows, axis=0), (1, 0, 2)).astype(BF)
    for q in range(field_ref.shape[2] // CHUNK):
        for m in range(MEM):
            field_ref[m, :, q * CHUNK : (q + 1) * CHUNK] = tiles[q * MEM + m]
    out = pltpu.make_async_copy(field_ref, field_hbm, field_sem)
    out.start()
    copy.wait()
    out.wait()


def call(kernel, out_shape, out_specs, scratch, operands, flops=0, aliases=None):
    arrays = [pltpu.with_memory_space_constraint(x, pltpu.HBM) if s is HB else x for x, s in operands]
    size = sum(x.size * x.dtype.itemsize for x, _ in operands)
    return pl.pallas_call(
        kernel,
        out_shape=out_shape,
        in_specs=[s for _, s in operands],
        out_specs=out_specs,
        scratch_shapes=scratch,
        input_output_aliases=aliases or {},
        compiler_params=pltpu.CompilerParams(vmem_limit_bytes=40 * 1024 * 1024),
        cost_estimate=pl.CostEstimate(flops=flops, bytes_accessed=size, transcendentals=0),
    )(*arrays)


def per_device(field_state, reservoir_state, coupling_blocks, coupling_index, input_blocks, input_index, readout, region_band):
    lat_count, lon_count = lax.axis_size("lat"), lax.axis_size("lon")
    lat_at = lax.axis_index("lat").astype(jnp.int32)
    lon_at = lax.axis_index("lon").astype(jnp.int32)
    region_rows, regions, members, units = reservoir_state.shape
    bands = coupling_blocks.shape[0]
    blocks = units // BLK
    outs = readout.shape[1]
    assert region_rows == 2 and members == MEM and regions % 4 == 0 and lon_count % 2 == 0
    chunks = regions // 4
    own_rows = chunks * MEM
    wide = own_rows + 2 * MEM
    rows = 4 * wide
    short = 4 * own_rows
    swap = lat_count == 2
    slots = 1 if swap else 2

    def bf(*dims):
        return jax.ShapeDtypeStruct(dims, BF)

    def vm(dims, dtype=BF):
        return pltpu.VMEM(dims, dtype)

    def trade(x, offset):
        pairs = []
        for j in range(lon_count):
            step = 1 if (j - offset) % 2 == 0 else -1
            pairs.append((j, (j + step) % lon_count))
        return lax.ppermute(x, "lon", pairs)

    def across(xs):
        if swap:
            return [lax.ppermute(xs[0], "lat", [(0, 1), (1, 0)])]
        up = lax.ppermute(xs[0], "lat", [(i + 1, i) for i in range(lat_count - 1)])
        down = lax.ppermute(xs[1], "lat", [(i, i + 1) for i in range(lat_count - 1)])
        return [down, up]

    row = ((1 - lat_at if swap else lat_at * 0).reshape(1), SM)
    parity = (((lon_at + 1) % 2).reshape(1), SM)
    band, cidx, iidx = (region_band, SM), (coupling_index.transpose(0, 2, 1), SM), (input_index, SM)
    flops = 2 * rows * units * (3 * BLK + outs)

    mail = call(
        message_kernel,
        [bf(4, 2 * MEM, 2 * HALF)] * 2,
        [VM] * 2,
        [vm((2, MEM, 8, HALF)), vm((2, region_rows, 2, MEM, units)), pltpu.SemaphoreType.DMA((4,))],
        [parity, (field_state, HB), (reservoir_state, HB)],
    )
    first = trade(mail[0], 1)
    second = trade(mail[1], 0)
    own, s0, s1, w = call(
        own_kernel,
        [bf(8, own_rows, CHUNK), bf(short, units), bf(short, units), bf(bands, blocks, BLK, 3 * BLK)],
        [VM] * 4,
        [vm(field_state.shape), vm(reservoir_state.shape), pltpu.SemaphoreType.DMA((5,))],
        [
            row,
            (field_state, HB),
            (reservoir_state, HB),
            (coupling_blocks.reshape(bands, blocks, 2, BLK, BLK), HB),
            (input_blocks.reshape(bands, blocks, BLK, BLK), HB),
        ],
        flops,
    )
    sent = call(
        functools.partial(first_edge_kernel, slots),
        [bf(2, own_rows, CHUNK + HALF // 2)] * slots,
        [VM] * slots,
        [],
        [parity, row, (own, VM), (first, VM), (second, VM)],
    )
    weights = [(w, VM)]
    source = weights + [(readout, HB)] + [(x, VM) for x in (own, s0, s1, first, second)]
    states_shape = bf(region_rows, regions, MEM, units)
    stage = [vm((regions, MEM, units)), pltpu.SemaphoreType.DMA]

    for step in range(STEPS):
        last = step == STEPS - 1
        got = across(sent)
        pre_rows = short if last else rows
        out = [jax.ShapeDtypeStruct((pre_rows, units), F32)] * slots
        specs = [VM] * slots
        scratch = [vm((12, wide, CHUNK), F32), vm((rows, 16 * CELL))]
        if swap:
            out += [bf(4, own_rows if last else wide, CHUNK), states_shape if last else bf(rows, units)]
            specs += [VM, HB if last else VM]
            scratch += stage if last else []
        if last:
            scratch += [vm((rows, units), F32)] * slots
        if step == 0:
            out += [bf(outs, units)]
            specs += [VM]
            scratch += [vm((rows, units))] * 2 + [pltpu.SemaphoreType.DMA]
        shadow = call(
            functools.partial(shadow_kernel, step == 0, last, slots),
            out,
            specs,
            scratch,
            [row, parity, band, cidx, iidx] + source,
            2 * flops,
        )
        far = shadow[slots : slots + 2 * (2 - slots)]
        if step == 0:
            weights.append((shadow[-1], VM))
        sent, edges, states = [None] * slots, [None] * slots, [None] * slots
        for slot in reversed(range(slots)):
            operands = [row, band, iidx] + weights + [ (shadow[slot], VM), (got[slot], VM)]
            inputs = [vm((pre_rows, 4 * CELL))]
            if not last:
                sent[slot], edges[slot], states[slot] = call(
                    functools.partial(late_kernel, slot, False, False),
                    [bf(2, own_rows, CHUNK + NEAR // 2), bf(2, wide, CHUNK), bf(rows, units)],
                    [VM] * 3,
                    inputs,
                    operands,
                    flops,
                )
            elif slot == 1:
                far = call(
                    functools.partial(late_kernel, slot, True, False),
                    [bf(4, own_rows, CHUNK), states_shape],
                    [VM, HB],
                    stage + inputs,
                    operands,
                    flops,
                )
            else:
                return call(
                    functools.partial(late_kernel, slot, True, True),
                    [bf(MEM, 8, regions * CELL), states_shape],
                    [HB, HB],
                    stage + [vm((MEM, 8, regions * CELL)), pltpu.SemaphoreType.DMA] + inputs,
                    operands + [(far[0], VM), (far[1], HB)],
                    flops,
                    {len(operands) + 1: 1},
                )
        source = weights + [(x, VM) for x in edges + states + list(far)]


def solution(mesh):
    return jax.shard_map(
        per_device,
        mesh=mesh,
        in_specs=(
            P(None, "lat", "lon"),
            P("lat", "lon", None, None),
            P("lat", None, None),
            P("lat", None, None),
            P("lat", None, None),
            P("lat", None),
            P("lat", None, None),
            P("lat"),
        ),
        out_specs=(P(None, "lat", "lon"), P("lat", "lon", None, None)),
        check_vma=False,
    )
```

```python
import functools

import jax
import jax.numpy as jnp
from jax import lax
from jax.experimental import pallas as pl
from jax.experimental.pallas import tpu as pltpu
from jax.sharding import PartitionSpec as P

VARS = 40
STEPS = 3
CELL = 4 * VARS
CHUNK = 4 * CELL
HALF = 512
NEAR = 256
MEM = 4
BLK = 128
BF = jnp.bfloat16
F32 = jnp.float32
VM = pl.BlockSpec(memory_space=pltpu.VMEM)
SM = pl.BlockSpec(memory_space=pltpu.SMEM)
HB = pl.BlockSpec(memory_space=pltpu.HBM)
NT = (((1,), (1,)), ((), ()))


def row_of(slot, row_ref):
    return row_ref[0] if slot == 0 else 1 - row_ref[0]


def message_kernel(parity_ref, field_hbm, state_hbm, first_ref, second_ref, field_ref, state_ref, sems):
    odd = parity_ref[0]
    lanes = field_hbm.shape[2] - HALF
    regions = state_hbm.shape[1]
    copies = []
    for k in range(2):
        low = odd if k == 0 else 1 - odd
        lane = pl.multiple_of((1 - low) * lanes, BLK)
        copies.append(pltpu.make_async_copy(field_hbm.at[:, :, pl.ds(lane, HALF)], field_ref.at[k], sems.at[k]))
        at = (1 - low) * (regions - 2)
        copies.append(pltpu.make_async_copy(state_hbm.at[:, pl.ds(at, 2)], state_ref.at[k], sems.at[2 + k]))
    for c in copies:
        c.start()
    for c in copies:
        c.wait()
    for k, out in enumerate((first_ref, second_ref)):
        for r in range(2):
            for j in range(2):
                out[r, j * MEM : (j + 1) * MEM] = state_ref[k, r, j]
        rows = jnp.transpose(field_ref[k].astype(F32), (1, 0, 2)).astype(BF)
        for d in range(8):
            at, lane = (d % 2) * MEM, (d // 2 % 2) * HALF
            out[2 + d // 4, at : at + MEM, lane : lane + HALF] = rows[d]


def own_kernel(row_ref, field_hbm, state_hbm, coup_hbm, inp_hbm, own_ref, s0_ref, s1_ref, w_ref, field_ref, state_ref, sems):
    copies = []

    def start(src, dst):
        copies.append(pltpu.make_async_copy(src, dst, sems.at[len(copies)]))
        copies[-1].start()

    start(field_hbm, field_ref)
    start(state_hbm, state_ref)
    for k in range(2):
        start(coup_hbm.at[:, :, k], w_ref.at[:, :, :, k * BLK : (k + 1) * BLK])
    start(inp_hbm, w_ref.at[:, :, :, 2 * BLK :])
    chunks = field_ref.shape[2] // CHUNK
    copies[0].wait()
    tiles = []
    for q in range(chunks):
        for m in range(MEM):
            tiles.append(field_ref[m, :, q * CHUNK : (q + 1) * CHUNK].astype(F32)[None])
    own_ref[...] = jnp.transpose(jnp.concatenate(tiles, axis=0), (1, 0, 2)).astype(BF)
    copies[1].wait()
    for slot, s_ref in enumerate((s0_ref, s1_ref)):
        r = row_of(slot, row_ref)
        rows = [state_ref[r, 4 * q + res].astype(F32) for res in range(4) for q in range(chunks)]
        s_ref[...] = jnp.concatenate(rows, axis=0).astype(BF)
    for c in copies[2:]:
        c.wait()


def pack(row, out_ref, k):
    last = row.shape[0] - MEM
    out_ref[k, :, :CHUNK] = row[MEM:last].astype(BF)
    half = NEAR // 2
    ends = [row[:MEM, CHUNK - NEAR : CHUNK - half], row[:MEM, CHUNK - half :], row[last:, :half], row[last:, half:NEAR]]
    out_ref[k, :, CHUNK:] = jnp.concatenate(ends, axis=0).astype(BF)


def unpack(msg):
    x = msg.astype(F32)
    own, ends = x[:, :CHUNK], x[:, CHUNK:]
    fill = jnp.zeros((MEM, CHUNK - 2 * ends.shape[1]), F32)
    before = jnp.concatenate([fill, ends[:MEM], ends[MEM : 2 * MEM]], axis=1)
    after = jnp.concatenate([ends[2 * MEM : 3 * MEM], ends[3 * MEM :], fill], axis=1)
    return jnp.concatenate([before, own, after], axis=0)


def sides(parity_ref, first, second):
    odd = parity_ref[0] == 1
    return jnp.where(odd, first, second), jnp.where(odd, second, first)


def first_edge_kernel(slots, parity_ref, row_ref, own_ref, first_ref, second_ref, *outs):
    for slot in range(slots):
        r = row_of(slot, row_ref)
        for k in range(2):
            at = k * MEM
            got = []
            for ref in (first_ref, second_ref):
                low = ref[2, at : at + MEM, :HALF].astype(F32)
                high = ref[3, at : at + MEM, HALF : 2 * HALF].astype(F32)
                got.append(jnp.where(r == 0, low, high))
            left, right = sides(parity_ref, *got)
            half = HALF // 2
            ends = [left[:, :half], left[:, half:], right[:, :half], right[:, half:]]
            outs[slot][k, :, :CHUNK] = own_ref[6 * r + k]
            outs[slot][k, :, CHUNK:] = jnp.concatenate(ends, axis=0).astype(BF)


def windows(lats, narrow):
    parts = [[] for _ in range(4)]
    for a in lats:
        rows = a.shape[0]
        before = jnp.concatenate([a[rows - MEM :, CHUNK - 2 * VARS :], a[: rows - MEM, CHUNK - 2 * VARS :]], axis=0)
        after = jnp.concatenate([a[MEM:, : 2 * VARS], a[:MEM, : 2 * VARS]], axis=0)
        ext = jnp.concatenate([before, a, after], axis=1)
        if narrow:
            ext = ext[MEM : rows - MEM]
        for res in range(4):
            parts[res].append(ext[:, CELL * res : CELL * res + 2 * CELL])
    return jnp.concatenate([jnp.concatenate(p, axis=1) for p in parts], axis=0).astype(BF)


def latitude(pred, d):
    per = pred.shape[0] // 4
    return jnp.concatenate([pred[res * per : (res + 1) * per, d * CELL : (d + 1) * CELL] for res in range(4)], axis=1)


def block_pre(b, band, s_ref, in_ref, cidx_ref, iidx_ref, w_ref):
    pieces = []
    for k in range(2):
        pieces.append(s_ref[:, pl.ds(pl.multiple_of(cidx_ref[band, k, b] * BLK, BLK), BLK)])
    pieces.append(in_ref[:, pl.ds(pl.multiple_of(iidx_ref[band, b] * BLK, BLK), BLK)])
    return lax.dot_general(jnp.concatenate(pieces, axis=1), w_ref[band, b], NT, preferred_element_type=F32)


def shadow_kernel(first, last, slots, row_ref, parity_ref, band_ref, cidx_ref, iidx_ref, *rest):
    rest = list(rest)

    def take(n):
        got = rest[:n]
        del rest[:n]
        return got

    w_ref = take(1)[0]
    if first:
        read_hbm, own_ref, s0_ref, s1_ref, first_ref, second_ref = take(6)
    else:
        read_ref = take(1)[0]
        edge_refs, s_refs = take(slots), take(slots)
        far_refs = take(2 * (2 - slots))
    pre_refs = take(slots)
    out_far = take(2 * (2 - slots))
    if first:
        read_ref = take(1)[0]
    xs_ref, in_ref = take(2)
    rows_at = [row_of(0, row_ref), row_of(1, row_ref)]
    waits = {}
    if first:
        sc0_ref, sc1_ref, sem = take(3)
        waits["read"] = pltpu.make_async_copy(read_hbm.at[0], read_ref, sem)
        waits["read"].start()

    def ready(name):
        if name in waits:
            waits.pop(name).wait()

    for k in range(2):
        xs_ref[k] = jnp.zeros(xs_ref.shape[1:], F32)
        xs_ref[10 + k] = jnp.zeros(xs_ref.shape[1:], F32)
    if first:
        fill = jnp.zeros((MEM, CHUNK - HALF), F32)
        left, right = sides(parity_ref, first_ref[...].astype(F32), second_ref[...].astype(F32))
        for d in range(8):
            at, lane = (d % 2) * MEM, (d // 2 % 2) * HALF
            lo = jnp.concatenate([fill, left[2 + d // 4, at : at + MEM, lane : lane + HALF]], axis=1)
            hi = jnp.concatenate([right[2 + d // 4, at : at + MEM, lane : lane + HALF], fill], axis=1)
            xs_ref[2 + d] = jnp.concatenate([lo, own_ref[d].astype(F32), hi], axis=0)
        empty = jnp.zeros((MEM, s0_ref.shape[1]), F32)
        per = s0_ref.shape[0] // 4
        for slot, (src, dst) in enumerate(((s0_ref, sc0_ref), (s1_ref, sc1_ref))):
            low = rows_at[slot] == 0
            lo, hi = jnp.where(low, left[0], left[1]), jnp.where(low, right[0], right[1])
            rows = []
            for res in range(4):
                rows.append(lo[(res - 2) * MEM : (res - 1) * MEM] if res >= 2 else empty)
                rows.append(src[res * per : (res + 1) * per].astype(F32))
                rows.append(hi[res * MEM : (res + 1) * MEM] if res < 2 else empty)
            dst[...] = jnp.concatenate(rows, axis=0).astype(BF)
        s_refs = [sc0_ref, sc1_ref]
    else:
        for slot in range(slots):
            r = rows_at[slot]
            half = pl.multiple_of((1 - r) * 2 * CELL, 2 * CELL)
            pred = lax.dot_general(s_refs[slot][...], read_ref[pl.ds(half, 2 * CELL), :], NT, preferred_element_type=F32)
            for d in range(2):
                xs_ref[2 + 4 * r + 2 * r + d] = edge_refs[slot][d].astype(F32)
                xs_ref[2 + 4 * r + 2 * (1 - r) + d] = latitude(pred, d).astype(BF).astype(F32)
        if far_refs:
            for d in range(4):
                xs_ref[2 + 4 * rows_at[1] + d] = far_refs[0][d].astype(F32)
            s_refs = [s_refs[0], far_refs[1]]

    far = []
    for slot in (1, 0):
        r = rows_at[slot]
        band = band_ref[r]
        in_ref[...] = windows([xs_ref[4 * r + d] for d in range(8)], False)
        blocks = iidx_ref.shape[1]
        pres = [block_pre(b, band, s_refs[slot], in_ref, cidx_ref, iidx_ref, w_ref) for b in range(blocks)]
        if slot >= slots:
            far = [jnp.concatenate([jnp.tanh(p).astype(BF) for p in pres], axis=1)]
            if last:
                stage_ref, sem = take(2)
                waits["out"] = put_states(r, far[0], MEM, stage_ref, out_far[1], sem)
        elif not last:
            for b in range(blocks):
                pre_refs[slot][:, b * BLK : (b + 1) * BLK] = pres[b]
        else:
            pre_ref = take(1)[0]
            for b in range(blocks):
                pre_ref[:, b * BLK : (b + 1) * BLK] = pres[b]
            per = pre_ref.shape[0] // 4
            short = per - 2 * MEM
            for res in range(4):
                pre_refs[slot][res * short : (res + 1) * short] = pre_ref[res * per + MEM : (res + 1) * per - MEM]
    ready("read")
    for state in far:
        pred = lax.dot_general(state, read_ref[...], NT, preferred_element_type=F32)
        for d in range(4):
            lat = latitude(pred, d).astype(BF)
            out_far[0][d] = lat[MEM:-MEM] if last else lat
        if not last:
            out_far[1][...] = state
    ready("out")


def put_states(r, state, skip, stage_ref, states_hbm, sem):
    per = state.shape[0] // 4
    for res in range(4):
        for q in range((per - 2 * skip) // MEM):
            at = res * per + skip + q * MEM
            stage_ref[4 * q + res] = state[at : at + MEM]
    copy = pltpu.make_async_copy(stage_ref, states_hbm.at[r], sem)
    copy.start()
    return copy


def late_kernel(slot, last, final, row_ref, band_ref, iidx_ref, w_ref, read_ref, pre_ref, got_ref, *rest):
    r = row_of(slot, row_ref)
    bands, index = band_ref[...], iidx_ref[...]
    band = jnp.where(r == 0, bands[0], bands[1])
    in_ref = rest[-1]
    in_ref[...] = windows([unpack(got_ref[k]) for k in range(2)], last)
    parts = []
    for b in range(iidx_ref.shape[1]):
        k = index[0, b]
        for g in range(1, index.shape[0]):
            k = jnp.where(band == g, index[g, b], k)
        k = k - 15 * r
        used = jnp.logical_and(k >= 0, k < 5)
        at = pl.multiple_of(jnp.where(used, k, 0) * BLK, BLK)
        term = lax.dot_general(in_ref[:, pl.ds(at, BLK)], w_ref[band, b, :, 2 * BLK :], NT, preferred_element_type=F32)
        pre = pre_ref[:, b * BLK : (b + 1) * BLK] + jnp.where(used, term, 0.0)
        parts.append(jnp.tanh(pre).astype(BF))
    state = jnp.concatenate(parts, axis=1)
    if not last:
        msg_ref, edge_ref, s_ref = rest[:3]
        s_ref[...] = state
        half = pl.multiple_of(r * 2 * CELL, 2 * CELL)
        pred = lax.dot_general(state, read_ref[pl.ds(half, 2 * CELL), :], NT, preferred_element_type=F32)
        for d in range(2):
            row = latitude(pred, d)
            pack(row, msg_ref, d)
            edge_ref[d] = row.astype(BF)
        return
    if not final:
        lats_ref, states_hbm, stage_ref, sem = rest[:4]
    else:
        other_ref, _, field_hbm, states_hbm, stage_ref, sem, field_ref, field_sem = rest[:8]
    copy = put_states(r, state, 0, stage_ref, states_hbm, sem)
    pred = lax.dot_general(state, read_ref[...], NT, preferred_element_type=F32)
    mine = [latitude(pred, d) for d in range(4)]
    if not final:
        for d in range(4):
            lats_ref[d] = mine[d].astype(BF)
        copy.wait()
        return
    other = [other_ref[d].astype(F32) for d in range(4)]
    low = r == 0
    rows = [jnp.where(low, mine[d], other[d])[None] for d in range(4)]
    rows += [jnp.where(low, other[d], mine[d])[None] for d in range(4)]
    tiles = jnp.transpose(jnp.concatenate(rows, axis=0), (1, 0, 2)).astype(BF)
    for q in range(field_ref.shape[2] // CHUNK):
        for m in range(MEM):
            field_ref[m, :, q * CHUNK : (q + 1) * CHUNK] = tiles[q * MEM + m]
    out = pltpu.make_async_copy(field_ref, field_hbm, field_sem)
    out.start()
    copy.wait()
    out.wait()


def call(kernel, out_shape, out_specs, scratch, operands, flops=0, aliases=None):
    arrays = [pltpu.with_memory_space_constraint(x, pltpu.HBM) if s is HB else x for x, s in operands]
    size = sum(x.size * x.dtype.itemsize for x, _ in operands)
    return pl.pallas_call(
        kernel,
        out_shape=out_shape,
        in_specs=[s for _, s in operands],
        out_specs=out_specs,
        scratch_shapes=scratch,
        input_output_aliases=aliases or {},
        compiler_params=pltpu.CompilerParams(vmem_limit_bytes=40 * 1024 * 1024),
        cost_estimate=pl.CostEstimate(flops=flops, bytes_accessed=size, transcendentals=0),
    )(*arrays)


def per_device(field_state, reservoir_state, coupling_blocks, coupling_index, input_blocks, input_index, readout, region_band):
    lat_count, lon_count = lax.axis_size("lat"), lax.axis_size("lon")
    lat_at = lax.axis_index("lat").astype(jnp.int32)
    lon_at = lax.axis_index("lon").astype(jnp.int32)
    region_rows, regions, members, units = reservoir_state.shape
    bands = coupling_blocks.shape[0]
    blocks = units // BLK
    outs = readout.shape[1]
    assert region_rows == 2 and members == MEM and regions % 4 == 0 and lon_count % 2 == 0
    chunks = regions // 4
    own_rows = chunks * MEM
    wide = own_rows + 2 * MEM
    rows = 4 * wide
    short = 4 * own_rows
    swap = lat_count == 2
    slots = 1 if swap else 2

    def bf(*dims):
        return jax.ShapeDtypeStruct(dims, BF)

    def vm(dims, dtype=BF):
        return pltpu.VMEM(dims, dtype)

    def trade(x, offset):
        pairs = []
        for j in range(lon_count):
            step = 1 if (j - offset) % 2 == 0 else -1
            pairs.append((j, (j + step) % lon_count))
        return lax.ppermute(x, "lon", pairs)

    def across(xs):
        if swap:
            return [lax.ppermute(xs[0], "lat", [(0, 1), (1, 0)])]
        up = lax.ppermute(xs[0], "lat", [(i + 1, i) for i in range(lat_count - 1)])
        down = lax.ppermute(xs[1], "lat", [(i, i + 1) for i in range(lat_count - 1)])
        return [down, up]

    row = ((1 - lat_at if swap else lat_at * 0).reshape(1), SM)
    parity = (((lon_at + 1) % 2).reshape(1), SM)
    band, cidx, iidx = (region_band, SM), (coupling_index.transpose(0, 2, 1), SM), (input_index, SM)
    flops = 2 * rows * units * (3 * BLK + outs)

    mail = call(
        message_kernel,
        [bf(4, 2 * MEM, 2 * HALF)] * 2,
        [VM] * 2,
        [vm((2, MEM, 8, HALF)), vm((2, region_rows, 2, MEM, units)), pltpu.SemaphoreType.DMA((4,))],
        [parity, (field_state, HB), (reservoir_state, HB)],
    )
    first = trade(mail[0], 1)
    second = trade(mail[1], 0)
    own, s0, s1, w = call(
        own_kernel,
        [bf(8, own_rows, CHUNK), bf(short, units), bf(short, units), bf(bands, blocks, BLK, 3 * BLK)],
        [VM] * 4,
        [vm(field_state.shape), vm(reservoir_state.shape), pltpu.SemaphoreType.DMA((5,))],
        [
            row,
            (field_state, HB),
            (reservoir_state, HB),
            (coupling_blocks.reshape(bands, blocks, 2, BLK, BLK), HB),
            (input_blocks.reshape(bands, blocks, BLK, BLK), HB),
        ],
        flops,
    )
    sent = call(
        functools.partial(first_edge_kernel, slots),
        [bf(2, own_rows, CHUNK + HALF // 2)] * slots,
        [VM] * slots,
        [],
        [parity, row, (own, VM), (first, VM), (second, VM)],
    )
    weights = [(w, VM)]
    source = weights + [(readout, HB)] + [(x, VM) for x in (own, s0, s1, first, second)]
    states_shape = bf(region_rows, regions, MEM, units)
    stage = [vm((regions, MEM, units)), pltpu.SemaphoreType.DMA]

    for step in range(STEPS):
        last = step == STEPS - 1
        got = across(sent)
        pre_rows = short if last else rows
        out = [jax.ShapeDtypeStruct((pre_rows, units), F32)] * slots
        specs = [VM] * slots
        scratch = [vm((12, wide, CHUNK), F32), vm((rows, 16 * CELL))]
        if swap:
            out += [bf(4, own_rows if last else wide, CHUNK), states_shape if last else bf(rows, units)]
            specs += [VM, HB if last else VM]
            scratch += stage if last else []
        if last:
            scratch += [vm((rows, units), F32)] * slots
        if step == 0:
            out += [bf(outs, units)]
            specs += [VM]
            scratch += [vm((rows, units))] * 2 + [pltpu.SemaphoreType.DMA]
        shadow = call(
            functools.partial(shadow_kernel, step == 0, last, slots),
            out,
            specs,
            scratch,
            [row, parity, band, cidx, iidx] + source,
            2 * flops,
        )
        far = shadow[slots : slots + 2 * (2 - slots)]
        if step == 0:
            weights.append((shadow[-1], VM))
        sent, edges, states = [None] * slots, [None] * slots, [None] * slots
        for slot in reversed(range(slots)):
            operands = [row, (band[0], VM), (iidx[0], VM)] + weights + [ (shadow[slot], VM), (got[slot], VM)]
            inputs = [vm((pre_rows, 4 * CELL))]
            if not last:
                sent[slot], edges[slot], states[slot] = call(
                    functools.partial(late_kernel, slot, False, False),
                    [bf(2, own_rows, CHUNK + NEAR // 2), bf(2, wide, CHUNK), bf(rows, units)],
                    [VM] * 3,
                    inputs,
                    operands,
                    flops,
                )
            elif slot == 1:
                far = call(
                    functools.partial(late_kernel, slot, True, False),
                    [bf(4, own_rows, CHUNK), states_shape],
                    [VM, HB],
                    stage + inputs,
                    operands,
                    flops,
                )
            else:
                return call(
                    functools.partial(late_kernel, slot, True, True),
                    [bf(MEM, 8, regions * CELL), states_shape],
                    [HB, HB],
                    stage + [vm((MEM, 8, regions * CELL)), pltpu.SemaphoreType.DMA] + inputs,
                    operands + [(far[0], VM), (far[1], HB)],
                    flops,
                    {len(operands) + 1: 1},
                )
        source = weights + [(x, VM) for x in edges + states + list(far)]


def solution(mesh):
    return jax.shard_map(
        per_device,
        mesh=mesh,
        in_specs=(
            P(None, "lat", "lon"),
            P("lat", "lon", None, None),
            P("lat", None, None),
            P("lat", None, None),
            P("lat", None, None),
            P("lat", None),
            P("lat", None, None),
            P("lat"),
        ),
        out_specs=(P(None, "lat", "lon"), P("lat", "lon", None, None)),
        check_vma=False,
    )
```

```python
import functools

import jax
import jax.numpy as jnp
from jax import lax
from jax.experimental import pallas as pl
from jax.experimental.pallas import tpu as pltpu
from jax.sharding import PartitionSpec as P

VARS = 40
STEPS = 3
CELL = 4 * VARS
CHUNK = 4 * CELL
HALF = 512
NEAR = 256
MEM = 4
BLK = 128
BF = jnp.bfloat16
F32 = jnp.float32
VM = pl.BlockSpec(memory_space=pltpu.VMEM)
SM = pl.BlockSpec(memory_space=pltpu.SMEM)
HB = pl.BlockSpec(memory_space=pltpu.HBM)
NT = (((1,), (1,)), ((), ()))


def row_of(slot, row_ref):
    return row_ref[0] if slot == 0 else 1 - row_ref[0]


def message_kernel(parity_ref, field_hbm, state_hbm, first_ref, second_ref, field_ref, state_ref, sems):
    odd = parity_ref[0]
    lanes = field_hbm.shape[2] - HALF
    regions = state_hbm.shape[1]
    copies = []
    for k in range(2):
        low = odd if k == 0 else 1 - odd
        lane = pl.multiple_of((1 - low) * lanes, BLK)
        copies.append(pltpu.make_async_copy(field_hbm.at[:, :, pl.ds(lane, HALF)], field_ref.at[k], sems.at[k]))
        at = (1 - low) * (regions - 2)
        copies.append(pltpu.make_async_copy(state_hbm.at[:, pl.ds(at, 2)], state_ref.at[k], sems.at[2 + k]))
    for c in copies:
        c.start()
    for c in copies:
        c.wait()
    for k, out in enumerate((first_ref, second_ref)):
        for r in range(2):
            for j in range(2):
                out[r, j * MEM : (j + 1) * MEM] = state_ref[k, r, j]
        rows = jnp.transpose(field_ref[k].astype(F32), (1, 0, 2)).astype(BF)
        for d in range(8):
            at, lane = (d % 2) * MEM, (d // 2 % 2) * HALF
            out[2 + d // 4, at : at + MEM, lane : lane + HALF] = rows[d]


def own_kernel(row_ref, field_hbm, state_hbm, coup_hbm, inp_hbm, own_ref, s0_ref, s1_ref, w_ref, field_ref, state_ref, sems):
    copies = []

    def start(src, dst):
        copies.append(pltpu.make_async_copy(src, dst, sems.at[len(copies)]))
        copies[-1].start()

    start(field_hbm, field_ref)
    start(state_hbm, state_ref)
    for k in range(2):
        start(coup_hbm.at[:, :, k], w_ref.at[:, :, :, k * BLK : (k + 1) * BLK])
    start(inp_hbm, w_ref.at[:, :, :, 2 * BLK :])
    chunks = field_ref.shape[2] // CHUNK
    copies[0].wait()
    tiles = []
    for q in range(chunks):
        for m in range(MEM):
            tiles.append(field_ref[m, :, q * CHUNK : (q + 1) * CHUNK].astype(F32)[None])
    own_ref[...] = jnp.transpose(jnp.concatenate(tiles, axis=0), (1, 0, 2)).astype(BF)
    copies[1].wait()
    for slot, s_ref in enumerate((s0_ref, s1_ref)):
        r = row_of(slot, row_ref)
        rows = [state_ref[r, 4 * q + res].astype(F32) for res in range(4) for q in range(chunks)]
        s_ref[...] = jnp.concatenate(rows, axis=0).astype(BF)
    for c in copies[2:]:
        c.wait()


def pack(row, out_ref, k):
    last = row.shape[0] - MEM
    out_ref[k, :, :CHUNK] = row[MEM:last].astype(BF)
    half = NEAR // 2
    ends = [row[:MEM, CHUNK - NEAR : CHUNK - half], row[:MEM, CHUNK - half :], row[last:, :half], row[last:, half:NEAR]]
    out_ref[k, :, CHUNK:] = jnp.concatenate(ends, axis=0).astype(BF)


def unpack(msg):
    x = msg.astype(F32)
    own, ends = x[:, :CHUNK], x[:, CHUNK:]
    fill = jnp.zeros((MEM, CHUNK - 2 * ends.shape[1]), F32)
    before = jnp.concatenate([fill, ends[:MEM], ends[MEM : 2 * MEM]], axis=1)
    after = jnp.concatenate([ends[2 * MEM : 3 * MEM], ends[3 * MEM :], fill], axis=1)
    return jnp.concatenate([before, own, after], axis=0)


def sides(parity_ref, first, second):
    odd = parity_ref[0] == 1
    return jnp.where(odd, first, second), jnp.where(odd, second, first)


def first_edge_kernel(slots, parity_ref, row_ref, own_ref, first_ref, second_ref, *outs):
    for slot in range(slots):
        r = row_of(slot, row_ref)
        for k in range(2):
            at = k * MEM
            got = []
            for ref in (first_ref, second_ref):
                low = ref[2, at : at + MEM, :HALF].astype(F32)
                high = ref[3, at : at + MEM, HALF : 2 * HALF].astype(F32)
                got.append(jnp.where(r == 0, low, high))
            left, right = sides(parity_ref, *got)
            half = HALF // 2
            ends = [left[:, :half], left[:, half:], right[:, :half], right[:, half:]]
            outs[slot][k, :, :CHUNK] = own_ref[6 * r + k]
            outs[slot][k, :, CHUNK:] = jnp.concatenate(ends, axis=0).astype(BF)


def windows(lats, narrow):
    parts = [[] for _ in range(4)]
    for a in lats:
        rows = a.shape[0]
        before = jnp.concatenate([a[rows - MEM :, CHUNK - 2 * VARS :], a[: rows - MEM, CHUNK - 2 * VARS :]], axis=0)
        after = jnp.concatenate([a[MEM:, : 2 * VARS], a[:MEM, : 2 * VARS]], axis=0)
        ext = jnp.concatenate([before, a, after], axis=1)
        if narrow:
            ext = ext[MEM : rows - MEM]
        for res in range(4):
            parts[res].append(ext[:, CELL * res : CELL * res + 2 * CELL])
    return jnp.concatenate([jnp.concatenate(p, axis=1) for p in parts], axis=0).astype(BF)


def latitude(pred, d):
    per = pred.shape[0] // 4
    return jnp.concatenate([pred[res * per : (res + 1) * per, d * CELL : (d + 1) * CELL] for res in range(4)], axis=1)


def of_band(band, values, *at):
    got = values[(0, *at)]
    for g in range(1, values.shape[0]):
        got = jnp.where(band == g, values[(g, *at)], got)
    return got


def block_at(index, ref):
    return pl.multiple_of(jnp.clip(index, 0, ref.shape[1] // BLK - 1) * BLK, BLK)


def block_pre(b, band, s_ref, in_ref, cidx, iidx, w_ref):
    pieces = []
    for k in range(2):
        pieces.append(s_ref[:, pl.ds(block_at(of_band(band, cidx, k, b), s_ref), BLK)])
    pieces.append(in_ref[:, pl.ds(block_at(of_band(band, iidx, b), in_ref), BLK)])
    return lax.dot_general(jnp.concatenate(pieces, axis=1), w_ref[band, b], NT, preferred_element_type=F32)


def shadow_kernel(first, last, slots, row_ref, parity_ref, band_ref, cidx_ref, iidx_ref, *rest):
    rest = list(rest)

    def take(n):
        got = rest[:n]
        del rest[:n]
        return got

    w_ref = take(1)[0]
    if first:
        read_hbm, own_ref, s0_ref, s1_ref, first_ref, second_ref = take(6)
    else:
        read_ref = take(1)[0]
        edge_refs, s_refs = take(slots), take(slots)
        far_refs = take(2 * (2 - slots))
    pre_refs = take(slots)
    out_far = take(2 * (2 - slots))
    if first:
        read_ref = take(1)[0]
    xs_ref, in_ref = take(2)
    rows_at = [row_of(0, row_ref), row_of(1, row_ref)]
    waits = {}
    if first:
        sc0_ref, sc1_ref, sem = take(3)
        waits["read"] = pltpu.make_async_copy(read_hbm.at[0], read_ref, sem)
        waits["read"].start()

    def ready(name):
        if name in waits:
            waits.pop(name).wait()

    for k in range(2):
        xs_ref[k] = jnp.zeros(xs_ref.shape[1:], F32)
        xs_ref[10 + k] = jnp.zeros(xs_ref.shape[1:], F32)
    if first:
        fill = jnp.zeros((MEM, CHUNK - HALF), F32)
        left, right = sides(parity_ref, first_ref[...].astype(F32), second_ref[...].astype(F32))
        for d in range(8):
            at, lane = (d % 2) * MEM, (d // 2 % 2) * HALF
            lo = jnp.concatenate([fill, left[2 + d // 4, at : at + MEM, lane : lane + HALF]], axis=1)
            hi = jnp.concatenate([right[2 + d // 4, at : at + MEM, lane : lane + HALF], fill], axis=1)
            xs_ref[2 + d] = jnp.concatenate([lo, own_ref[d].astype(F32), hi], axis=0)
        empty = jnp.zeros((MEM, s0_ref.shape[1]), F32)
        per = s0_ref.shape[0] // 4
        for slot, (src, dst) in enumerate(((s0_ref, sc0_ref), (s1_ref, sc1_ref))):
            low = rows_at[slot] == 0
            lo, hi = jnp.where(low, left[0], left[1]), jnp.where(low, right[0], right[1])
            rows = []
            for res in range(4):
                rows.append(lo[(res - 2) * MEM : (res - 1) * MEM] if res >= 2 else empty)
                rows.append(src[res * per : (res + 1) * per].astype(F32))
                rows.append(hi[res * MEM : (res + 1) * MEM] if res < 2 else empty)
            dst[...] = jnp.concatenate(rows, axis=0).astype(BF)
        s_refs = [sc0_ref, sc1_ref]
    else:
        for slot in range(slots):
            r = rows_at[slot]
            half = pl.multiple_of((1 - r) * 2 * CELL, 2 * CELL)
            pred = lax.dot_general(s_refs[slot][...], read_ref[pl.ds(half, 2 * CELL), :], NT, preferred_element_type=F32)
            for d in range(2):
                xs_ref[2 + 4 * r + 2 * r + d] = edge_refs[slot][d].astype(F32)
                xs_ref[2 + 4 * r + 2 * (1 - r) + d] = latitude(pred, d).astype(BF).astype(F32)
        if far_refs:
            for d in range(4):
                xs_ref[2 + 4 * rows_at[1] + d] = far_refs[0][d].astype(F32)
            s_refs = [s_refs[0], far_refs[1]]

    far = []
    bands, cidx, iidx = band_ref[...], cidx_ref[...], iidx_ref[...]
    for slot in (1, 0):
        r = rows_at[slot]
        band = jnp.where(r == 0, bands[0], bands[1])
        in_ref[...] = windows([xs_ref[4 * r + d] for d in range(8)], False)
        blocks = iidx_ref.shape[1]
        pres = [block_pre(b, band, s_refs[slot], in_ref, cidx, iidx, w_ref) for b in range(blocks)]
        if slot >= slots:
            far = [jnp.concatenate([jnp.tanh(p).astype(BF) for p in pres], axis=1)]
            if last:
                stage_ref, sem = take(2)
                waits["out"] = put_states(r, far[0], MEM, stage_ref, out_far[1], sem)
        elif not last:
            for b in range(blocks):
                pre_refs[slot][:, b * BLK : (b + 1) * BLK] = pres[b]
        else:
            pre_ref = take(1)[0]
            for b in range(blocks):
                pre_ref[:, b * BLK : (b + 1) * BLK] = pres[b]
            per = pre_ref.shape[0] // 4
            short = per - 2 * MEM
            for res in range(4):
                pre_refs[slot][res * short : (res + 1) * short] = pre_ref[res * per + MEM : (res + 1) * per - MEM]
    ready("read")
    for state in far:
        pred = lax.dot_general(state, read_ref[...], NT, preferred_element_type=F32)
        for d in range(4):
            lat = latitude(pred, d).astype(BF)
            out_far[0][d] = lat[MEM:-MEM] if last else lat
        if not last:
            out_far[1][...] = state
    ready("out")


def put_states(r, state, skip, stage_ref, states_hbm, sem):
    per = state.shape[0] // 4
    for res in range(4):
        for q in range((per - 2 * skip) // MEM):
            at = res * per + skip + q * MEM
            stage_ref[4 * q + res] = state[at : at + MEM]
    copy = pltpu.make_async_copy(stage_ref, states_hbm.at[r], sem)
    copy.start()
    return copy


def late_kernel(slot, last, final, row_ref, band_ref, iidx_ref, w_ref, read_ref, pre_ref, got_ref, *rest):
    r = row_of(slot, row_ref)
    bands, iidx = band_ref[...], iidx_ref[...]
    band = jnp.where(r == 0, bands[0], bands[1])
    in_ref = rest[-1]
    in_ref[...] = windows([unpack(got_ref[k]) for k in range(2)], last)
    parts = []
    for b in range(iidx_ref.shape[1]):
        k = of_band(band, iidx, b) - 15 * r
        used = jnp.logical_and(k >= 0, k < 5)
        at = pl.multiple_of(jnp.where(used, k, 0) * BLK, BLK)
        term = lax.dot_general(in_ref[:, pl.ds(at, BLK)], w_ref[band, b, :, 2 * BLK :], NT, preferred_element_type=F32)
        pre = pre_ref[:, b * BLK : (b + 1) * BLK] + jnp.where(used, term, 0.0)
        parts.append(jnp.tanh(pre).astype(BF))
    state = jnp.concatenate(parts, axis=1)
    if not last:
        msg_ref, edge_ref, s_ref = rest[:3]
        s_ref[...] = state
        half = pl.multiple_of(r * 2 * CELL, 2 * CELL)
        pred = lax.dot_general(state, read_ref[pl.ds(half, 2 * CELL), :], NT, preferred_element_type=F32)
        for d in range(2):
            row = latitude(pred, d)
            pack(row, msg_ref, d)
            edge_ref[d] = row.astype(BF)
        return
    if not final:
        lats_ref, states_hbm, stage_ref, sem = rest[:4]
    else:
        other_ref, _, field_hbm, states_hbm, stage_ref, sem, field_ref, field_sem = rest[:8]
    copy = put_states(r, state, 0, stage_ref, states_hbm, sem)
    pred = lax.dot_general(state, read_ref[...], NT, preferred_element_type=F32)
    mine = [latitude(pred, d) for d in range(4)]
    if not final:
        for d in range(4):
            lats_ref[d] = mine[d].astype(BF)
        copy.wait()
        return
    other = [other_ref[d].astype(F32) for d in range(4)]
    low = r == 0
    rows = [jnp.where(low, mine[d], other[d])[None] for d in range(4)]
    rows += [jnp.where(low, other[d], mine[d])[None] for d in range(4)]
    tiles = jnp.transpose(jnp.concatenate(rows, axis=0), (1, 0, 2)).astype(BF)
    for q in range(field_ref.shape[2] // CHUNK):
        for m in range(MEM):
            field_ref[m, :, q * CHUNK : (q + 1) * CHUNK] = tiles[q * MEM + m]
    out = pltpu.make_async_copy(field_ref, field_hbm, field_sem)
    out.start()
    copy.wait()
    out.wait()


def call(kernel, out_shape, out_specs, scratch, operands, flops=0, aliases=None):
    arrays = [pltpu.with_memory_space_constraint(x, pltpu.HBM) if s is HB else x for x, s in operands]
    size = sum(x.size * x.dtype.itemsize for x, _ in operands)
    return pl.pallas_call(
        kernel,
        out_shape=out_shape,
        in_specs=[s for _, s in operands],
        out_specs=out_specs,
        scratch_shapes=scratch,
        input_output_aliases=aliases or {},
        compiler_params=pltpu.CompilerParams(vmem_limit_bytes=40 * 1024 * 1024),
        cost_estimate=pl.CostEstimate(flops=flops, bytes_accessed=size, transcendentals=0),
    )(*arrays)


def per_device(field_state, reservoir_state, coupling_blocks, coupling_index, input_blocks, input_index, readout, region_band):
    lat_count, lon_count = lax.axis_size("lat"), lax.axis_size("lon")
    lat_at = lax.axis_index("lat").astype(jnp.int32)
    lon_at = lax.axis_index("lon").astype(jnp.int32)
    region_rows, regions, members, units = reservoir_state.shape
    bands = coupling_blocks.shape[0]
    blocks = units // BLK
    outs = readout.shape[1]
    assert region_rows == 2 and members == MEM and regions % 4 == 0 and lon_count % 2 == 0
    chunks = regions // 4
    own_rows = chunks * MEM
    wide = own_rows + 2 * MEM
    rows = 4 * wide
    short = 4 * own_rows
    swap = lat_count == 2
    slots = 1 if swap else 2

    def bf(*dims):
        return jax.ShapeDtypeStruct(dims, BF)

    def vm(dims, dtype=BF):
        return pltpu.VMEM(dims, dtype)

    def trade(x, offset):
        pairs = []
        for j in range(lon_count):
            step = 1 if (j - offset) % 2 == 0 else -1
            pairs.append((j, (j + step) % lon_count))
        return lax.ppermute(x, "lon", pairs)

    def across(xs):
        if swap:
            return [lax.ppermute(xs[0], "lat", [(0, 1), (1, 0)])]
        up = lax.ppermute(xs[0], "lat", [(i + 1, i) for i in range(lat_count - 1)])
        down = lax.ppermute(xs[1], "lat", [(i, i + 1) for i in range(lat_count - 1)])
        return [down, up]

    row = ((1 - lat_at if swap else lat_at * 0).reshape(1), SM)
    parity = (((lon_at + 1) % 2).reshape(1), SM)
    band, cidx, iidx = (region_band, VM), (coupling_index.transpose(0, 2, 1), VM), (input_index, VM)
    flops = 2 * rows * units * (3 * BLK + outs)

    mail = call(
        message_kernel,
        [bf(4, 2 * MEM, 2 * HALF)] * 2,
        [VM] * 2,
        [vm((2, MEM, 8, HALF)), vm((2, region_rows, 2, MEM, units)), pltpu.SemaphoreType.DMA((4,))],
        [parity, (field_state, HB), (reservoir_state, HB)],
    )
    first = trade(mail[0], 1)
    second = trade(mail[1], 0)
    own, s0, s1, w = call(
        own_kernel,
        [bf(8, own_rows, CHUNK), bf(short, units), bf(short, units), bf(bands, blocks, BLK, 3 * BLK)],
        [VM] * 4,
        [vm(field_state.shape), vm(reservoir_state.shape), pltpu.SemaphoreType.DMA((5,))],
        [
            row,
            (field_state, HB),
            (reservoir_state, HB),
            (coupling_blocks.reshape(bands, blocks, 2, BLK, BLK), HB),
            (input_blocks.reshape(bands, blocks, BLK, BLK), HB),
        ],
        flops,
    )
    sent = call(
        functools.partial(first_edge_kernel, slots),
        [bf(2, own_rows, CHUNK + HALF // 2)] * slots,
        [VM] * slots,
        [],
        [parity, row, (own, VM), (first, VM), (second, VM)],
    )
    weights = [(w, VM)]
    source = weights + [(readout, HB)] + [(x, VM) for x in (own, s0, s1, first, second)]
    states_shape = bf(region_rows, regions, MEM, units)
    stage = [vm((regions, MEM, units)), pltpu.SemaphoreType.DMA]

    for step in range(STEPS):
        last = step == STEPS - 1
        got = across(sent)
        pre_rows = short if last else rows
        out = [jax.ShapeDtypeStruct((pre_rows, units), F32)] * slots
        specs = [VM] * slots
        scratch = [vm((12, wide, CHUNK), F32), vm((rows, 16 * CELL))]
        if swap:
            out += [bf(4, own_rows if last else wide, CHUNK), states_shape if last else bf(rows, units)]
            specs += [VM, HB if last else VM]
            scratch += stage if last else []
        if last:
            scratch += [vm((rows, units), F32)] * slots
        if step == 0:
            out += [bf(outs, units)]
            specs += [VM]
            scratch += [vm((rows, units))] * 2 + [pltpu.SemaphoreType.DMA]
        shadow = call(
            functools.partial(shadow_kernel, step == 0, last, slots),
            out,
            specs,
            scratch,
            [row, parity, band, cidx, iidx] + source,
            2 * flops,
        )
        far = shadow[slots : slots + 2 * (2 - slots)]
        if step == 0:
            weights.append((shadow[-1], VM))
        sent, edges, states = [None] * slots, [None] * slots, [None] * slots
        for slot in reversed(range(slots)):
            operands = [row, band, iidx] + weights + [ (shadow[slot], VM), (got[slot], VM)]
            inputs = [vm((pre_rows, 4 * CELL))]
            if not last:
                sent[slot], edges[slot], states[slot] = call(
                    functools.partial(late_kernel, slot, False, False),
                    [bf(2, own_rows, CHUNK + NEAR // 2), bf(2, wide, CHUNK), bf(rows, units)],
                    [VM] * 3,
                    inputs,
                    operands,
                    flops,
                )
            elif slot == 1:
                far = call(
                    functools.partial(late_kernel, slot, True, False),
                    [bf(4, own_rows, CHUNK), states_shape],
                    [VM, HB],
                    stage + inputs,
                    operands,
                    flops,
                )
            else:
                return call(
                    functools.partial(late_kernel, slot, True, True),
                    [bf(MEM, 8, regions * CELL), states_shape],
                    [HB, HB],
                    stage + [vm((MEM, 8, regions * CELL)), pltpu.SemaphoreType.DMA] + inputs,
                    operands + [(far[0], VM), (far[1], HB)],
                    flops,
                    {len(operands) + 1: 1},
                )
        source = weights + [(x, VM) for x in edges + states + list(far)]


def solution(mesh):
    return jax.shard_map(
        per_device,
        mesh=mesh,
        in_specs=(
            P(None, "lat", "lon"),
            P("lat", "lon", None, None),
            P("lat", None, None),
            P("lat", None, None),
            P("lat", None, None),
            P("lat", None),
            P("lat", None, None),
            P("lat"),
        ),
        out_specs=(P(None, "lat", "lon"), P("lat", "lon", None, None)),
        check_vma=False,
    )
```

```python
import functools

import jax
import jax.numpy as jnp
from jax import lax
from jax.experimental import pallas as pl
from jax.experimental.pallas import tpu as pltpu
from jax.sharding import PartitionSpec as P

VARS = 40
STEPS = 3
CELL = 4 * VARS
CHUNK = 4 * CELL
HALF = 512
NEAR = 256
MEM = 4
BLK = 128
BF = jnp.bfloat16
F32 = jnp.float32
VM = pl.BlockSpec(memory_space=pltpu.VMEM)
SM = pl.BlockSpec(memory_space=pltpu.SMEM)
HB = pl.BlockSpec(memory_space=pltpu.HBM)
NT = (((1,), (1,)), ((), ()))


def row_of(slot, row_ref):
    return row_ref[0] if slot == 0 else 1 - row_ref[0]


def message_kernel(slots, row_ref, field_hbm, state_hbm, right_ref, left_ref, own_ref, *rest):
    field_ref, state_ref, sems = rest[3 * slots :]
    regions = state_hbm.shape[1]
    copies = [
        pltpu.make_async_copy(field_hbm, field_ref, sems.at[0]),
        pltpu.make_async_copy(state_hbm.at[:, pl.ds(regions - 2, 2)], state_ref.at[0], sems.at[1]),
        pltpu.make_async_copy(state_hbm.at[:, pl.ds(0, 2)], state_ref.at[1], sems.at[2]),
    ]
    for c in copies:
        c.start()
    for c in copies:
        c.wait()
    chunks = field_ref.shape[2] // CHUNK
    tiles = []
    for q in range(chunks):
        for m in range(MEM):
            tiles.append(field_ref[m, :, q * CHUNK : (q + 1) * CHUNK].astype(F32)[None])
    rows = jnp.transpose(jnp.concatenate(tiles, axis=0), (1, 0, 2)).astype(BF)
    own_ref[...] = rows
    last = (chunks - 1) * MEM
    for k, out in enumerate((right_ref, left_ref)):
        for r in range(2):
            for j in range(2):
                out[r, j * MEM : (j + 1) * MEM] = state_ref[k, r, j]
        for d in range(8):
            at, lane = (d % 2) * MEM, (d // 2 % 2) * HALF
            out[2 + d // 4, at : at + MEM, lane : lane + HALF] = rows[d, last:, CHUNK - HALF :] if k == 0 else rows[d, :MEM, :HALF]
    for slot in range(slots):
        low = row_of(slot, row_ref) == 0
        dright_ref, edge_ref, dleft_ref = rest[3 * slot : 3 * slot + 3]
        edge_ref[...] = jnp.zeros(edge_ref.shape, BF)
        dright_ref[...] = jnp.zeros(dright_ref.shape, BF)
        for k in range(2):
            row = jnp.where(low, rows[k], rows[6 + k])
            edge_ref[k, :, :CHUNK] = row
            dright_ref[0, k * MEM : (k + 1) * MEM, :HALF] = row[last:, CHUNK - HALF :]
            dleft_ref[k * MEM : (k + 1) * MEM] = row[:MEM, :HALF]


def own_kernel(row_ref, state_hbm, coup_hbm, inp_hbm, read_hbm, s0_ref, s1_ref, coup_ref, inp_ref, read_ref, state_ref, sems):
    pairs = [(state_hbm, state_ref), (coup_hbm, coup_ref), (inp_hbm, inp_ref), (read_hbm.at[0], read_ref)]
    copies = [pltpu.make_async_copy(src, dst, sems.at[i]) for i, (src, dst) in enumerate(pairs)]
    for c in copies:
        c.start()
    copies[0].wait()
    chunks = state_ref.shape[1] // 4
    for slot, s_ref in enumerate((s0_ref, s1_ref)):
        r = row_of(slot, row_ref)
        rows = [state_ref[r, 4 * q + res].astype(F32) for res in range(4) for q in range(chunks)]
        s_ref[...] = jnp.concatenate(rows, axis=0).astype(BF)
    for c in copies[1:]:
        c.wait()


def pack(row, out_ref, k):
    last = row.shape[0] - MEM
    out_ref[k, :, :CHUNK] = row[MEM:last].astype(BF)
    half = NEAR // 2
    ends = [row[:MEM, CHUNK - NEAR : CHUNK - half], row[:MEM, CHUNK - half :], row[last:, :half], row[last:, half:NEAR]]
    out_ref[k, :, CHUNK:] = jnp.concatenate(ends, axis=0).astype(BF)


def unpack(msg):
    x = msg.astype(F32)
    own, ends = x[:, :CHUNK], x[:, CHUNK:]
    fill = jnp.zeros((MEM, CHUNK - 2 * ends.shape[1]), F32)
    before = jnp.concatenate([fill, ends[:MEM], ends[MEM : 2 * MEM]], axis=1)
    after = jnp.concatenate([ends[2 * MEM : 3 * MEM], ends[3 * MEM :], fill], axis=1)
    return jnp.concatenate([before, own, after], axis=0)


def windows(lats, narrow):
    parts = [[] for _ in range(4)]
    for a in lats:
        rows = a.shape[0]
        before = jnp.concatenate([a[rows - MEM :, CHUNK - 2 * VARS :], a[: rows - MEM, CHUNK - 2 * VARS :]], axis=0)
        after = jnp.concatenate([a[MEM:, : 2 * VARS], a[:MEM, : 2 * VARS]], axis=0)
        ext = jnp.concatenate([before, a, after], axis=1)
        if narrow:
            ext = ext[MEM : rows - MEM]
        for res in range(4):
            parts[res].append(ext[:, CELL * res : CELL * res + 2 * CELL])
    return jnp.concatenate([jnp.concatenate(p, axis=1) for p in parts], axis=0).astype(BF)


def latitude(pred, d):
    per = pred.shape[0] // 4
    return jnp.concatenate([pred[res * per : (res + 1) * per, d * CELL : (d + 1) * CELL] for res in range(4)], axis=1)


def of_band(band, values, *at):
    got = values[(0, *at)]
    for g in range(1, values.shape[0]):
        got = jnp.where(band == g, values[(g, *at)], got)
    return got


def block_at(index, ref):
    return pl.multiple_of(jnp.clip(index, 0, ref.shape[1] // BLK - 1) * BLK, BLK)


def block_pre(b, band, s_ref, in_ref, cidx, iidx, coup_ref, inp_ref):
    pieces = []
    mats = [coup_ref[band, (2 * b + k) * BLK : (2 * b + k + 1) * BLK, :] for k in range(2)]
    mats.append(inp_ref[band, b * BLK : (b + 1) * BLK, :])
    for k in range(2):
        pieces.append(s_ref[:, pl.ds(block_at(of_band(band, cidx, k, b), s_ref), BLK)])
    pieces.append(in_ref[:, pl.ds(block_at(of_band(band, iidx, b), in_ref), BLK)])
    return lax.dot_general(jnp.concatenate(pieces, axis=1), jnp.concatenate(mats, axis=1), NT, preferred_element_type=F32)


def half_of(r, rest_lats):
    return pl.ds(pl.multiple_of((1 - r if rest_lats else r) * 2 * CELL, 2 * CELL), 2 * CELL)


def send_edge(r, state, read_ref, msg_ref, edge_ref, s_ref):
    s_ref[...] = state
    pred = lax.dot_general(state, read_ref[half_of(r, False), :], NT, preferred_element_type=F32)
    for d in range(2):
        row = latitude(pred, d)
        pack(row, msg_ref, d)
        edge_ref[d] = row.astype(BF)


def first_kernel(slot, edge, row_ref, band_ref, cidx_ref, iidx_ref, coup_ref, inp_ref, read_ref, own_ref, s0_ref, fl_ref, *rest):
    rest = list(rest)
    r = row_of(slot, row_ref)
    if edge:
        dl_ref, lat_ref, fr_ref, dr_ref = rest[:4]
        del rest[:4]
    else:
        fr_ref = rest.pop(0)
    outs, (xs_ref, s_ref, in_ref) = rest[:-3], rest[-3:]
    fill = jnp.zeros((MEM, CHUNK - HALF), F32)

    def widen(own, left, right):
        left = jnp.concatenate([fill, left.astype(F32)], axis=1)
        right = jnp.concatenate([right.astype(F32), fill], axis=1)
        return jnp.concatenate([left, own.astype(F32), right], axis=0)

    for d in range(8):
        at, lane = (d % 2) * MEM, (d // 2 % 2) * HALF
        left = fl_ref[2 + d // 4, at : at + MEM, lane : lane + HALF]
        right = fr_ref[2 + d // 4, at : at + MEM, lane : lane + HALF]
        xs_ref[2 + d] = widen(own_ref[d], left, right)
    for k in range(2):
        at = k * MEM
        if edge:
            xs_ref[10 * r + k] = widen(lat_ref[k, :, :CHUNK], dl_ref[0, at : at + MEM, :HALF], dr_ref[at : at + MEM])
        else:
            xs_ref[10 * r + k] = jnp.zeros(xs_ref.shape[1:], F32)
    empty = jnp.zeros((MEM, s0_ref.shape[1]), F32)
    per = s0_ref.shape[0] // 4
    rows = []
    for res in range(4):
        rows.append(fl_ref[r, (res - 2) * MEM : (res - 1) * MEM].astype(F32) if res >= 2 else empty)
        rows.append(s0_ref[res * per : (res + 1) * per].astype(F32))
        rows.append(fr_ref[r, res * MEM : (res + 1) * MEM].astype(F32) if res < 2 else empty)
    s_ref[...] = jnp.concatenate(rows, axis=0).astype(BF)
    in_ref[...] = windows([xs_ref[4 * r + d] for d in range(8)], False)
    bands, cidx, iidx = band_ref[...], cidx_ref[...], iidx_ref[...]
    band = jnp.where(r == 0, bands[0], bands[1])
    pres = [block_pre(b, band, s_ref, in_ref, cidx, iidx, coup_ref, inp_ref) for b in range(iidx_ref.shape[1])]
    state = jnp.concatenate([jnp.tanh(p).astype(BF) for p in pres], axis=1)
    if edge:
        send_edge(r, state, read_ref, *outs)
        return
    outs[1][...] = state
    pred = lax.dot_general(state, read_ref[...], NT, preferred_element_type=F32)
    for d in range(4):
        outs[0][d] = latitude(pred, d).astype(BF)


def narrowed(s):
    per = s.shape[0] // 4
    return jnp.concatenate([s[res * per + MEM : (res + 1) * per - MEM] for res in range(4)], axis=0)


def shadow_kernel(last, slots, row_ref, band_ref, cidx_ref, iidx_ref, coup_ref, inp_ref, read_ref, *rest):
    rest = list(rest)

    def take(n):
        got = rest[:n]
        del rest[:n]
        return got

    edge_refs, s_refs = take(slots), take(slots)
    far_refs = take(2 * (2 - slots))
    pre_refs = take(slots)
    out_far = take(2 * (2 - slots))
    xs_ref, in_ref = take(2)
    rows_at = [row_of(0, row_ref), row_of(1, row_ref)]
    for k in range(2):
        xs_ref[k] = jnp.zeros(xs_ref.shape[1:], F32)
        xs_ref[10 + k] = jnp.zeros(xs_ref.shape[1:], F32)
    for slot in range(slots):
        r = rows_at[slot]
        pred = lax.dot_general(s_refs[slot][...], read_ref[half_of(r, True), :], NT, preferred_element_type=F32)
        for d in range(2):
            xs_ref[2 + 4 * r + 2 * r + d] = edge_refs[slot][d].astype(F32)
            xs_ref[2 + 4 * r + 2 * (1 - r) + d] = latitude(pred, d).astype(BF).astype(F32)
    if far_refs:
        for d in range(4):
            xs_ref[2 + 4 * rows_at[1] + d] = far_refs[0][d].astype(F32)
        s_refs = [s_refs[0], far_refs[1]]
    if last:
        short_refs = take(2)
        for slot in range(2):
            short_refs[slot][...] = narrowed(s_refs[slot][...].astype(F32)).astype(BF)
        s_refs = short_refs

    bands, cidx, iidx = band_ref[...], cidx_ref[...], iidx_ref[...]
    copy = None
    for slot in (1, 0):
        r = rows_at[slot]
        band = jnp.where(r == 0, bands[0], bands[1])
        in_ref[...] = windows([xs_ref[4 * r + d] for d in range(8)], last)
        blocks = iidx_ref.shape[1]
        pres = [block_pre(b, band, s_refs[slot], in_ref, cidx, iidx, coup_ref, inp_ref) for b in range(blocks)]
        if slot < slots:
            for b in range(blocks):
                pre_refs[slot][:, b * BLK : (b + 1) * BLK] = pres[b]
            continue
        state = jnp.concatenate([jnp.tanh(p).astype(BF) for p in pres], axis=1)
        if last:
            stage_ref, sem = take(2)
            copy = put_states(r, state, stage_ref, out_far[1], sem)
        else:
            out_far[1][...] = state
        pred = lax.dot_general(state, read_ref[...], NT, preferred_element_type=F32)
        for d in range(4):
            out_far[0][d] = latitude(pred, d).astype(BF)
    if copy is not None:
        copy.wait()


def put_states(r, state, stage_ref, states_hbm, sem):
    per = state.shape[0] // 4
    for res in range(4):
        for q in range(per // MEM):
            at = res * per + q * MEM
            stage_ref[4 * q + res] = state[at : at + MEM]
    copy = pltpu.make_async_copy(stage_ref, states_hbm.at[r], sem)
    copy.start()
    return copy


def late_kernel(slot, last, final, row_ref, band_ref, iidx_ref, inp_ref, read_ref, pre_ref, got_ref, *rest):
    r = row_of(slot, row_ref)
    bands, iidx = band_ref[...], iidx_ref[...]
    band = jnp.where(r == 0, bands[0], bands[1])
    in_ref = rest[-1]
    in_ref[...] = windows([unpack(got_ref[k]) for k in range(2)], last)
    parts = []
    for b in range(iidx_ref.shape[1]):
        k = of_band(band, iidx, b) - 15 * r
        used = jnp.logical_and(k >= 0, k < 5)
        at = pl.multiple_of(jnp.where(used, k, 0) * BLK, BLK)
        term = lax.dot_general(in_ref[:, pl.ds(at, BLK)], inp_ref[band, b * BLK : (b + 1) * BLK, :], NT, preferred_element_type=F32)
        pre = pre_ref[:, b * BLK : (b + 1) * BLK] + jnp.where(used, term, 0.0)
        parts.append(jnp.tanh(pre).astype(BF))
    state = jnp.concatenate(parts, axis=1)
    if not last:
        send_edge(r, state, read_ref, *rest[:3])
        return
    if not final:
        lats_ref, states_hbm, stage_ref, sem = rest[:4]
    else:
        other_ref, _, field_hbm, states_hbm, stage_ref, sem, field_ref, field_sem = rest[:8]
    copy = put_states(r, state, stage_ref, states_hbm, sem)
    pred = lax.dot_general(state, read_ref[...], NT, preferred_element_type=F32)
    mine = [latitude(pred, d) for d in range(4)]
    if not final:
        for d in range(4):
            lats_ref[d] = mine[d].astype(BF)
        copy.wait()
        return
    other = [other_ref[d].astype(F32) for d in range(4)]
    low = r == 0
    rows = [jnp.where(low, mine[d], other[d])[None] for d in range(4)]
    rows += [jnp.where(low, other[d], mine[d])[None] for d in range(4)]
    tiles = jnp.transpose(jnp.concatenate(rows, axis=0), (1, 0, 2)).astype(BF)
    for q in range(field_ref.shape[2] // CHUNK):
        for m in range(MEM):
            field_ref[m, :, q * CHUNK : (q + 1) * CHUNK] = tiles[q * MEM + m]
    out = pltpu.make_async_copy(field_ref, field_hbm, field_sem)
    out.start()
    copy.wait()
    out.wait()


def call(kernel, out_shape, out_specs, scratch, operands, flops=0, aliases=None):
    arrays = [pltpu.with_memory_space_constraint(x, pltpu.HBM) if s is HB else x for x, s in operands]
    size = sum(x.size * x.dtype.itemsize for x, _ in operands)
    return pl.pallas_call(
        kernel,
        out_shape=out_shape,
        in_specs=[s for _, s in operands],
        out_specs=out_specs,
        scratch_shapes=scratch,
        input_output_aliases=aliases or {},
        compiler_params=pltpu.CompilerParams(vmem_limit_bytes=40 * 1024 * 1024),
        cost_estimate=pl.CostEstimate(flops=flops, bytes_accessed=size, transcendentals=0),
    )(*arrays)


def per_device(field_state, reservoir_state, coupling_blocks, coupling_index, input_blocks, input_index, readout, region_band):
    lat_count, lon_count = lax.axis_size("lat"), lax.axis_size("lon")
    lat_at = lax.axis_index("lat").astype(jnp.int32)
    region_rows, regions, members, units = reservoir_state.shape
    outs = readout.shape[1]
    assert region_rows == 2 and members == MEM and regions % 4 == 0
    chunks = regions // 4
    own_rows = chunks * MEM
    wide = own_rows + 2 * MEM
    rows = 4 * wide
    short = 4 * own_rows
    swap = lat_count == 2
    slots = 1 if swap else 2

    def bf(*dims):
        return jax.ShapeDtypeStruct(dims, BF)

    def vm(dims, dtype=BF):
        return pltpu.VMEM(dims, dtype)

    def send(x, lat_step, lon_step):
        pairs = []
        for i in range(lat_count):
            to = 1 - i if swap and lat_step else i + lat_step
            if 0 <= to < lat_count:
                for j in range(lon_count):
                    pairs.append((i * lon_count + j, to * lon_count + (j + lon_step) % lon_count))
        return lax.ppermute(x, ("lat", "lon"), pairs)

    def across(xs, lon_step=0):
        if swap:
            return [send(xs[0], 1, lon_step)]
        return [send(xs[1], 1, lon_step), send(xs[0], -1, lon_step)]

    row = ((1 - lat_at if swap else lat_at * 0).reshape(1), SM)
    small = [(region_band, VM), (coupling_index.transpose(0, 2, 1), VM), (input_index, VM)]
    band, _, iidx = small
    flops = 2 * rows * units * (3 * BLK + outs)

    mail = call(
        functools.partial(message_kernel, slots),
        [bf(4, 2 * MEM, 2 * HALF)] * 2 + [bf(8, own_rows, CHUNK)] + [bf(4, 2 * MEM, 2 * HALF), bf(2, own_rows, 4 * HALF * 2 * MEM // own_rows), bf(2 * MEM, HALF)] * slots,
        [VM] * (3 + 3 * slots),
        [vm(field_state.shape), vm((2, region_rows, 2, MEM, units)), pltpu.SemaphoreType.DMA((3,))],
        [row, (field_state, HB), (reservoir_state, HB)],
    )
    from_left = send(mail[0], 0, 1)
    from_dleft = across(mail[3::3], 1)
    from_lat = across(mail[4::3])
    from_right = send(mail[1], 0, -1)
    from_dright = across(mail[5::3], -1)
    own = (mail[2], VM)
    s0, s1, coup, inp, read = call(
        own_kernel,
        [bf(short, units), bf(short, units), bf(*coupling_blocks.shape), bf(*input_blocks.shape), bf(outs, units)],
        [VM] * 5,
        [vm(reservoir_state.shape), pltpu.SemaphoreType.DMA((4,))],
        [row, (reservoir_state, HB), (coupling_blocks, HB), (input_blocks, HB), (readout, HB)],
        flops,
    )
    weights = [(x, VM) for x in (coup, inp, read)]
    states_shape = bf(region_rows, regions, MEM, units)
    stage = [vm((regions, MEM, units)), pltpu.SemaphoreType.DMA]
    padded = vm((12, wide, CHUNK), F32)
    send_out = [bf(2, own_rows, CHUNK + NEAR // 2), bf(2, wide, CHUNK), bf(rows, units)]

    sent, edges, states, far = [None] * slots, [None] * slots, [None] * slots, []
    for slot in range(2):
        edge = slot < slots
        operands = [row] + small + weights + [own, ((s0, s1)[slot], VM), (from_left, VM)]
        if edge:
            operands += [(from_dleft[slot], VM), (from_lat[slot], VM)]
        operands.append((from_right, VM))
        if edge:
            operands.append((from_dright[slot], VM))
        got = call(
            functools.partial(first_kernel, slot, edge),
            send_out if edge else [bf(4, wide, CHUNK), bf(rows, units)],
            [VM] * (3 if edge else 2),
            [padded, vm((rows, units)), vm((rows, 16 * CELL))],
            operands,
            flops,
        )
        if edge:
            sent[slot], edges[slot], states[slot] = got
        else:
            far = list(got)

    for step in range(1, STEPS):
        last = step == STEPS - 1
        got = across(sent)
        pre_rows = short if last else rows
        out = [jax.ShapeDtypeStruct((pre_rows, units), F32)] * slots
        specs = [VM] * slots
        scratch = [padded, vm((pre_rows, 16 * CELL))] + [vm((short, units))] * (2 if last else 0)
        if swap:
            out += [bf(4, own_rows if last else wide, CHUNK), states_shape if last else bf(rows, units)]
            specs += [VM, HB if last else VM]
            scratch += stage if last else []
        shadow = call(
            functools.partial(shadow_kernel, last, slots),
            out,
            specs,
            scratch,
            [row] + small + weights + [(x, VM) for x in edges + states + far],
            2 * flops,
        )
        far = list(shadow[slots:])
        for slot in reversed(range(slots)):
            operands = [row, band, iidx] + weights[1:] + [(shadow[slot], VM), (got[slot], VM)]
            inputs = [vm((pre_rows, 4 * CELL))]
            if not last:
                sent[slot], edges[slot], states[slot] = call(
                    functools.partial(late_kernel, slot, False, False), send_out, [VM] * 3, inputs, operands, flops
                )
            elif slot == 1:
                far = call(
                    functools.partial(late_kernel, slot, True, False),
                    [bf(4, own_rows, CHUNK), states_shape],
                    [VM, HB],
                    stage + inputs,
                    operands,
                    flops,
                )
            else:
                return call(
                    functools.partial(late_kernel, slot, True, True),
                    [bf(MEM, 8, regions * CELL), states_shape],
                    [HB, HB],
                    stage + [vm((MEM, 8, regions * CELL)), pltpu.SemaphoreType.DMA] + inputs,
                    operands + [(far[0], VM), (far[1], HB)],
                    flops,
                    {len(operands) + 1: 1},
                )


def solution(mesh):
    return jax.shard_map(
        per_device,
        mesh=mesh,
        in_specs=(
            P(None, "lat", "lon"),
            P("lat", "lon", None, None),
            P("lat", None, None),
            P("lat", None, None),
            P("lat", None, None),
            P("lat", None),
            P("lat", None, None),
            P("lat"),
        ),
        out_specs=(P(None, "lat", "lon"), P("lat", "lon", None, None)),
        check_vma=False,
    )
```

```python
import functools

import jax
import jax.numpy as jnp
from jax import lax
from jax.experimental import pallas as pl
from jax.experimental.pallas import tpu as pltpu
from jax.sharding import PartitionSpec as P

VARS = 40
STEPS = 3
CELL = 4 * VARS
CHUNK = 4 * CELL
HALF = 512
NEAR = 256
MEM = 4
BLK = 128
AHEAD = 10**10
BF = jnp.bfloat16
F32 = jnp.float32
VM = pl.BlockSpec(memory_space=pltpu.VMEM)
SM = pl.BlockSpec(memory_space=pltpu.SMEM)
HB = pl.BlockSpec(memory_space=pltpu.HBM)
NT = (((1,), (1,)), ((), ()))


def row_of(slot, row_ref):
    return row_ref[0] if slot == 0 else 1 - row_ref[0]


def message_kernel(slots, row_ref, field_hbm, state_hbm, right_ref, left_ref, own_ref, *rest):
    field_ref, state_ref, sems = rest[3 * slots :]
    regions = state_hbm.shape[1]
    copies = [
        pltpu.make_async_copy(field_hbm, field_ref, sems.at[0]),
        pltpu.make_async_copy(state_hbm.at[:, pl.ds(regions - 2, 2)], state_ref.at[0], sems.at[1]),
        pltpu.make_async_copy(state_hbm.at[:, pl.ds(0, 2)], state_ref.at[1], sems.at[2]),
    ]
    for c in copies:
        c.start()
    for c in copies:
        c.wait()
    chunks = field_ref.shape[2] // CHUNK
    tiles = []
    for q in range(chunks):
        for m in range(MEM):
            tiles.append(field_ref[m, :, q * CHUNK : (q + 1) * CHUNK].astype(F32)[None])
    rows = jnp.transpose(jnp.concatenate(tiles, axis=0), (1, 0, 2)).astype(BF)
    own_ref[...] = rows
    last = (chunks - 1) * MEM
    for k, out in enumerate((right_ref, left_ref)):
        for r in range(2):
            for j in range(2):
                out[r, j * MEM : (j + 1) * MEM] = state_ref[k, r, j]
        for d in range(8):
            at, lane = (d % 2) * MEM, (d // 2 % 2) * HALF
            out[2 + d // 4, at : at + MEM, lane : lane + HALF] = rows[d, last:, CHUNK - HALF :] if k == 0 else rows[d, :MEM, :HALF]
    for slot in range(slots):
        low = row_of(slot, row_ref) == 0
        dright_ref, edge_ref, dleft_ref = rest[3 * slot : 3 * slot + 3]
        edge_ref[...] = jnp.zeros(edge_ref.shape, BF)
        dright_ref[...] = jnp.zeros(dright_ref.shape, BF)
        for k in range(2):
            row = jnp.where(low, rows[k], rows[6 + k])
            edge_ref[k, :, :CHUNK] = row
            dright_ref[0, k * MEM : (k + 1) * MEM, :HALF] = row[last:, CHUNK - HALF :]
            dleft_ref[k * MEM : (k + 1) * MEM] = row[:MEM, :HALF]


def own_kernel(row_ref, state_ref, s0_ref, s1_ref):
    chunks = state_ref.shape[1] // 4
    for slot, s_ref in enumerate((s0_ref, s1_ref)):
        r = row_of(slot, row_ref)
        rows = [state_ref[r, 4 * q + res].astype(F32) for res in range(4) for q in range(chunks)]
        s_ref[...] = jnp.concatenate(rows, axis=0).astype(BF)


def pack(row, out_ref, k):
    last = row.shape[0] - MEM
    out_ref[k, :, :CHUNK] = row[MEM:last].astype(BF)
    half = NEAR // 2
    ends = [row[:MEM, CHUNK - NEAR : CHUNK - half], row[:MEM, CHUNK - half :], row[last:, :half], row[last:, half:NEAR]]
    out_ref[k, :, CHUNK:] = jnp.concatenate(ends, axis=0).astype(BF)


def unpack(msg):
    x = msg.astype(F32)
    own, ends = x[:, :CHUNK], x[:, CHUNK:]
    fill = jnp.zeros((MEM, CHUNK - 2 * ends.shape[1]), F32)
    before = jnp.concatenate([fill, ends[:MEM], ends[MEM : 2 * MEM]], axis=1)
    after = jnp.concatenate([ends[2 * MEM : 3 * MEM], ends[3 * MEM :], fill], axis=1)
    return jnp.concatenate([before, own, after], axis=0)


def windows(lats, narrow):
    parts = [[] for _ in range(4)]
    for a in lats:
        rows = a.shape[0]
        before = jnp.concatenate([a[rows - MEM :, CHUNK - 2 * VARS :], a[: rows - MEM, CHUNK - 2 * VARS :]], axis=0)
        after = jnp.concatenate([a[MEM:, : 2 * VARS], a[:MEM, : 2 * VARS]], axis=0)
        ext = jnp.concatenate([before, a, after], axis=1)
        if narrow:
            ext = ext[MEM : rows - MEM]
        for res in range(4):
            parts[res].append(ext[:, CELL * res : CELL * res + 2 * CELL])
    return jnp.concatenate([jnp.concatenate(p, axis=1) for p in parts], axis=0).astype(BF)


def latitude(pred, d):
    per = pred.shape[0] // 4
    return jnp.concatenate([pred[res * per : (res + 1) * per, d * CELL : (d + 1) * CELL] for res in range(4)], axis=1)


def of_band(band, values, *at):
    got = values[(0, *at)]
    for g in range(1, values.shape[0]):
        got = jnp.where(band == g, values[(g, *at)], got)
    return got


def block_at(index, ref):
    return pl.multiple_of(jnp.clip(index, 0, ref.shape[1] // BLK - 1) * BLK, BLK)


def block_pre(b, band, s_ref, in_ref, cidx, iidx, coup_ref, inp_ref):
    pieces = []
    mats = [coup_ref[band, (2 * b + k) * BLK : (2 * b + k + 1) * BLK, :] for k in range(2)]
    mats.append(inp_ref[band, b * BLK : (b + 1) * BLK, :])
    for k in range(2):
        pieces.append(s_ref[:, pl.ds(block_at(of_band(band, cidx, k, b), s_ref), BLK)])
    pieces.append(in_ref[:, pl.ds(block_at(of_band(band, iidx, b), in_ref), BLK)])
    return lax.dot_general(jnp.concatenate(pieces, axis=1), jnp.concatenate(mats, axis=1), NT, preferred_element_type=F32)


def half_of(r, rest_lats):
    return pl.ds(pl.multiple_of((1 - r if rest_lats else r) * 2 * CELL, 2 * CELL), 2 * CELL)


def send_edge(r, state, read_ref, msg_ref, edge_ref, s_ref):
    s_ref[...] = state
    pred = lax.dot_general(state, read_ref[half_of(r, False), :], NT, preferred_element_type=F32)
    for d in range(2):
        row = latitude(pred, d)
        pack(row, msg_ref, d)
        edge_ref[d] = row.astype(BF)


def first_kernel(slot, edge, row_ref, band_ref, cidx_ref, iidx_ref, coup_ref, inp_ref, read_ref, own_ref, s0_ref, fl_ref, *rest):
    rest = list(rest)
    r = row_of(slot, row_ref)
    if edge:
        dl_ref, lat_ref, fr_ref, dr_ref = rest[:4]
        del rest[:4]
    else:
        fr_ref = rest.pop(0)
    outs, (xs_ref, s_ref, in_ref) = rest[:-3], rest[-3:]
    fill = jnp.zeros((MEM, CHUNK - HALF), F32)

    def widen(own, left, right):
        left = jnp.concatenate([fill, left.astype(F32)], axis=1)
        right = jnp.concatenate([right.astype(F32), fill], axis=1)
        return jnp.concatenate([left, own.astype(F32), right], axis=0)

    for d in range(8):
        at, lane = (d % 2) * MEM, (d // 2 % 2) * HALF
        left = fl_ref[2 + d // 4, at : at + MEM, lane : lane + HALF]
        right = fr_ref[2 + d // 4, at : at + MEM, lane : lane + HALF]
        xs_ref[2 + d] = widen(own_ref[d], left, right)
    for k in range(2):
        at = k * MEM
        if edge:
            xs_ref[10 * r + k] = widen(lat_ref[k, :, :CHUNK], dl_ref[0, at : at + MEM, :HALF], dr_ref[at : at + MEM])
        else:
            xs_ref[10 * r + k] = jnp.zeros(xs_ref.shape[1:], F32)
    empty = jnp.zeros((MEM, s0_ref.shape[1]), F32)
    per = s0_ref.shape[0] // 4
    rows = []
    for res in range(4):
        rows.append(fl_ref[r, (res - 2) * MEM : (res - 1) * MEM].astype(F32) if res >= 2 else empty)
        rows.append(s0_ref[res * per : (res + 1) * per].astype(F32))
        rows.append(fr_ref[r, res * MEM : (res + 1) * MEM].astype(F32) if res < 2 else empty)
    s_ref[...] = jnp.concatenate(rows, axis=0).astype(BF)
    in_ref[...] = windows([xs_ref[4 * r + d] for d in range(8)], False)
    bands, cidx, iidx = band_ref[...], cidx_ref[...], iidx_ref[...]
    band = jnp.where(r == 0, bands[0], bands[1])
    pres = [block_pre(b, band, s_ref, in_ref, cidx, iidx, coup_ref, inp_ref) for b in range(iidx_ref.shape[1])]
    state = jnp.concatenate([jnp.tanh(p).astype(BF) for p in pres], axis=1)
    if edge:
        send_edge(r, state, read_ref, *outs)
        return
    outs[1][...] = state
    pred = lax.dot_general(state, read_ref[...], NT, preferred_element_type=F32)
    for d in range(4):
        outs[0][d] = latitude(pred, d).astype(BF)


def narrowed(s):
    per = s.shape[0] // 4
    return jnp.concatenate([s[res * per + MEM : (res + 1) * per - MEM] for res in range(4)], axis=0)


def shadow_kernel(last, slots, row_ref, band_ref, cidx_ref, iidx_ref, coup_ref, inp_ref, read_ref, *rest):
    rest = list(rest)

    def take(n):
        got = rest[:n]
        del rest[:n]
        return got

    edge_refs, s_refs = take(slots), take(slots)
    far_refs = take(2 * (2 - slots))
    pre_refs = take(slots)
    out_far = take(2 * (2 - slots))
    xs_ref, in_ref = take(2)
    rows_at = [row_of(0, row_ref), row_of(1, row_ref)]
    for k in range(2):
        xs_ref[k] = jnp.zeros(xs_ref.shape[1:], F32)
        xs_ref[10 + k] = jnp.zeros(xs_ref.shape[1:], F32)
    for slot in range(slots):
        r = rows_at[slot]
        pred = lax.dot_general(s_refs[slot][...], read_ref[half_of(r, True), :], NT, preferred_element_type=F32)
        for d in range(2):
            xs_ref[2 + 4 * r + 2 * r + d] = edge_refs[slot][d].astype(F32)
            xs_ref[2 + 4 * r + 2 * (1 - r) + d] = latitude(pred, d).astype(BF).astype(F32)
    if far_refs:
        for d in range(4):
            xs_ref[2 + 4 * rows_at[1] + d] = far_refs[0][d].astype(F32)
        s_refs = [s_refs[0], far_refs[1]]
    if last:
        short_refs = take(2)
        for slot in range(2):
            short_refs[slot][...] = narrowed(s_refs[slot][...].astype(F32)).astype(BF)
        s_refs = short_refs

    bands, cidx, iidx = band_ref[...], cidx_ref[...], iidx_ref[...]
    copy = None
    for slot in (1, 0):
        r = rows_at[slot]
        band = jnp.where(r == 0, bands[0], bands[1])
        in_ref[...] = windows([xs_ref[4 * r + d] for d in range(8)], last)
        blocks = iidx_ref.shape[1]
        pres = [block_pre(b, band, s_refs[slot], in_ref, cidx, iidx, coup_ref, inp_ref) for b in range(blocks)]
        if slot < slots:
            for b in range(blocks):
                pre_refs[slot][:, b * BLK : (b + 1) * BLK] = pres[b]
            continue
        state = jnp.concatenate([jnp.tanh(p).astype(BF) for p in pres], axis=1)
        if last:
            stage_ref, sem = take(2)
            copy = put_states(r, state, stage_ref, out_far[1], sem)
        else:
            out_far[1][...] = state
        pred = lax.dot_general(state, read_ref[...], NT, preferred_element_type=F32)
        for d in range(4):
            out_far[0][d] = latitude(pred, d).astype(BF)
    if copy is not None:
        copy.wait()


def put_states(r, state, stage_ref, states_hbm, sem):
    per = state.shape[0] // 4
    for res in range(4):
        for q in range(per // MEM):
            at = res * per + q * MEM
            stage_ref[4 * q + res] = state[at : at + MEM]
    copy = pltpu.make_async_copy(stage_ref, states_hbm.at[r], sem)
    copy.start()
    return copy


def late_kernel(slot, last, final, row_ref, band_ref, iidx_ref, inp_ref, read_ref, pre_ref, got_ref, *rest):
    r = row_of(slot, row_ref)
    bands, iidx = band_ref[...], iidx_ref[...]
    band = jnp.where(r == 0, bands[0], bands[1])
    in_ref = rest[-1]
    in_ref[...] = windows([unpack(got_ref[k]) for k in range(2)], last)
    parts = []
    for b in range(iidx_ref.shape[1]):
        k = of_band(band, iidx, b) - 15 * r
        used = jnp.logical_and(k >= 0, k < 5)
        at = pl.multiple_of(jnp.where(used, k, 0) * BLK, BLK)
        term = lax.dot_general(in_ref[:, pl.ds(at, BLK)], inp_ref[band, b * BLK : (b + 1) * BLK, :], NT, preferred_element_type=F32)
        pre = pre_ref[:, b * BLK : (b + 1) * BLK] + jnp.where(used, term, 0.0)
        parts.append(jnp.tanh(pre).astype(BF))
    state = jnp.concatenate(parts, axis=1)
    if not last:
        send_edge(r, state, read_ref, *rest[:3])
        return
    if not final:
        lats_ref, states_hbm, stage_ref, sem = rest[:4]
    else:
        other_ref, _, field_hbm, states_hbm, stage_ref, sem, field_ref, field_sem = rest[:8]
    copy = put_states(r, state, stage_ref, states_hbm, sem)
    pred = lax.dot_general(state, read_ref[...], NT, preferred_element_type=F32)
    mine = [latitude(pred, d) for d in range(4)]
    if not final:
        for d in range(4):
            lats_ref[d] = mine[d].astype(BF)
        copy.wait()
        return
    other = [other_ref[d].astype(F32) for d in range(4)]
    low = r == 0
    rows = [jnp.where(low, mine[d], other[d])[None] for d in range(4)]
    rows += [jnp.where(low, other[d], mine[d])[None] for d in range(4)]
    tiles = jnp.transpose(jnp.concatenate(rows, axis=0), (1, 0, 2)).astype(BF)
    for q in range(field_ref.shape[2] // CHUNK):
        for m in range(MEM):
            field_ref[m, :, q * CHUNK : (q + 1) * CHUNK] = tiles[q * MEM + m]
    out = pltpu.make_async_copy(field_ref, field_hbm, field_sem)
    out.start()
    copy.wait()
    out.wait()


def call(kernel, out_shape, out_specs, scratch, operands, flops=0, aliases=None):
    arrays = [pltpu.with_memory_space_constraint(x, pltpu.HBM) if s is HB else x for x, s in operands]
    size = sum(x.size * x.dtype.itemsize for x, _ in operands)
    return pl.pallas_call(
        kernel,
        out_shape=out_shape,
        in_specs=[s for _, s in operands],
        out_specs=out_specs,
        scratch_shapes=scratch,
        input_output_aliases=aliases or {},
        compiler_params=pltpu.CompilerParams(vmem_limit_bytes=40 * 1024 * 1024),
        cost_estimate=pl.CostEstimate(flops=flops, bytes_accessed=size, transcendentals=0),
    )(*arrays)


def per_device(field_state, reservoir_state, coupling_blocks, coupling_index, input_blocks, input_index, readout, region_band):
    lat_count, lon_count = lax.axis_size("lat"), lax.axis_size("lon")
    lat_at = lax.axis_index("lat").astype(jnp.int32)
    region_rows, regions, members, units = reservoir_state.shape
    outs = readout.shape[1]
    assert region_rows == 2 and members == MEM and regions % 4 == 0
    chunks = regions // 4
    own_rows = chunks * MEM
    wide = own_rows + 2 * MEM
    rows = 4 * wide
    short = 4 * own_rows
    swap = lat_count == 2
    slots = 1 if swap else 2

    def bf(*dims):
        return jax.ShapeDtypeStruct(dims, BF)

    def vm(dims, dtype=BF):
        return pltpu.VMEM(dims, dtype)

    def send(x, lat_step, lon_step):
        pairs = []
        for i in range(lat_count):
            to = 1 - i if swap and lat_step else i + lat_step
            if 0 <= to < lat_count:
                for j in range(lon_count):
                    pairs.append((i * lon_count + j, to * lon_count + (j + lon_step) % lon_count))
        return lax.ppermute(x, ("lat", "lon"), pairs)

    def across(xs, lon_step=0):
        if swap:
            return [send(xs[0], 1, lon_step)]
        return [send(xs[1], 1, lon_step), send(xs[0], -1, lon_step)]

    row = ((1 - lat_at if swap else lat_at * 0).reshape(1), SM)
    small = [(region_band, VM), (coupling_index.transpose(0, 2, 1), VM), (input_index, VM)]
    band, _, iidx = small
    flops = 2 * rows * units * (3 * BLK + outs)

    mail = call(
        functools.partial(message_kernel, slots),
        [bf(4, 2 * MEM, 2 * HALF)] * 2 + [bf(8, own_rows, CHUNK)] + [bf(4, 2 * MEM, 2 * HALF), bf(2, own_rows, 4 * HALF * 2 * MEM // own_rows), bf(2 * MEM, HALF)] * slots,
        [VM] * (3 + 3 * slots),
        [vm(field_state.shape), vm((2, region_rows, 2, MEM, units)), pltpu.SemaphoreType.DMA((3,))],
        [row, (field_state, HB), (reservoir_state, HB)],
        AHEAD,
    )
    from_left = send(mail[0], 0, 1)
    from_dleft = across(mail[3::3], 1)
    from_lat = across(mail[4::3])
    from_right = send(mail[1], 0, -1)
    from_dright = across(mail[5::3], -1)
    own = (mail[2], VM)
    s0, s1 = call(own_kernel, [bf(short, units)] * 2, [VM] * 2, [], [row, (reservoir_state, VM)], flops)
    weights = [(x, VM) for x in (coupling_blocks, input_blocks, readout[0])]
    states_shape = bf(region_rows, regions, MEM, units)
    stage = [vm((regions, MEM, units)), pltpu.SemaphoreType.DMA]
    padded = vm((12, wide, CHUNK), F32)
    send_out = [bf(2, own_rows, CHUNK + NEAR // 2), bf(2, wide, CHUNK), bf(rows, units)]

    sent, edges, states, far = [None] * slots, [None] * slots, [None] * slots, []
    for slot in range(2):
        edge = slot < slots
        operands = [row] + small + weights + [own, ((s0, s1)[slot], VM), (from_left, VM)]
        if edge:
            operands += [(from_dleft[slot], VM), (from_lat[slot], VM)]
        operands.append((from_right, VM))
        if edge:
            operands.append((from_dright[slot], VM))
        got = call(
            functools.partial(first_kernel, slot, edge),
            send_out if edge else [bf(4, wide, CHUNK), bf(rows, units)],
            [VM] * (3 if edge else 2),
            [padded, vm((rows, units)), vm((rows, 16 * CELL))],
            operands,
            flops,
        )
        if edge:
            sent[slot], edges[slot], states[slot] = got
        else:
            far = list(got)

    for step in range(1, STEPS):
        last = step == STEPS - 1
        got = across(sent)
        pre_rows = short if last else rows
        out = [jax.ShapeDtypeStruct((pre_rows, units), F32)] * slots
        specs = [VM] * slots
        scratch = [padded, vm((pre_rows, 16 * CELL))] + [vm((short, units))] * (2 if last else 0)
        if swap:
            out += [bf(4, own_rows if last else wide, CHUNK), states_shape if last else bf(rows, units)]
            specs += [VM, HB if last else VM]
            scratch += stage if last else []
        shadow = call(
            functools.partial(shadow_kernel, last, slots),
            out,
            specs,
            scratch,
            [row] + small + weights + [(x, VM) for x in edges + states + far],
            2 * flops,
        )
        far = list(shadow[slots:])
        for slot in reversed(range(slots)):
            operands = [row, band, iidx] + weights[1:] + [(shadow[slot], VM), (got[slot], VM)]
            inputs = [vm((pre_rows, 4 * CELL))]
            if not last:
                sent[slot], edges[slot], states[slot] = call(
                    functools.partial(late_kernel, slot, False, False), send_out, [VM] * 3, inputs, operands, flops
                )
            elif slot == 1:
                far = call(
                    functools.partial(late_kernel, slot, True, False),
                    [bf(4, own_rows, CHUNK), states_shape],
                    [VM, HB],
                    stage + inputs,
                    operands,
                    flops,
                )
            else:
                return call(
                    functools.partial(late_kernel, slot, True, True),
                    [bf(MEM, 8, regions * CELL), states_shape],
                    [HB, HB],
                    stage + [vm((MEM, 8, regions * CELL)), pltpu.SemaphoreType.DMA] + inputs,
                    operands + [(far[0], VM), (far[1], HB)],
                    flops,
                    {len(operands) + 1: 1},
                )


def solution(mesh):
    return jax.shard_map(
        per_device,
        mesh=mesh,
        in_specs=(
            P(None, "lat", "lon"),
            P("lat", "lon", None, None),
            P("lat", None, None),
            P("lat", None, None),
            P("lat", None, None),
            P("lat", None),
            P("lat", None, None),
            P("lat"),
        ),
        out_specs=(P(None, "lat", "lon"), P("lat", "lon", None, None)),
        check_vma=False,
    )
```

```python
import functools

import jax
import jax.numpy as jnp
from jax import lax
from jax.experimental import pallas as pl
from jax.experimental.pallas import tpu as pltpu
from jax.sharding import PartitionSpec as P

VARS = 40
STEPS = 3
CELL = 4 * VARS
CHUNK = 4 * CELL
HALF = 512
NEAR = 256
MEM = 4
BLK = 128
AHEAD = 10**10
BF = jnp.bfloat16
F32 = jnp.float32
VM = pl.BlockSpec(memory_space=pltpu.VMEM)
SM = pl.BlockSpec(memory_space=pltpu.SMEM)
HB = pl.BlockSpec(memory_space=pltpu.HBM)
NT = (((1,), (1,)), ((), ()))


def row_of(slot, row_ref):
    return row_ref[0] if slot == 0 else 1 - row_ref[0]


def message_kernel(slots, row_ref, field_hbm, state_hbm, right_ref, left_ref, own_ref, *rest):
    field_ref, state_ref, sems = rest[3 * slots :]
    regions = state_hbm.shape[1]
    copies = [
        pltpu.make_async_copy(field_hbm, field_ref, sems.at[0]),
        pltpu.make_async_copy(state_hbm.at[:, pl.ds(regions - 2, 2)], state_ref.at[0], sems.at[1]),
        pltpu.make_async_copy(state_hbm.at[:, pl.ds(0, 2)], state_ref.at[1], sems.at[2]),
    ]
    for c in copies:
        c.start()
    chunks = field_ref.shape[2] // CHUNK
    copies[0].wait()
    tiles = []
    for q in range(chunks):
        for m in range(MEM):
            tiles.append(field_ref[m, :, q * CHUNK : (q + 1) * CHUNK].astype(F32)[None])
    rows = jnp.transpose(jnp.concatenate(tiles, axis=0), (1, 0, 2)).astype(BF)
    own_ref[...] = rows
    last = (chunks - 1) * MEM
    for c in copies[1:]:
        c.wait()
    for k, out in enumerate((right_ref, left_ref)):
        for r in range(2):
            for j in range(2):
                out[r, j * MEM : (j + 1) * MEM] = state_ref[k, r, j]
        for d in range(8):
            at, lane = (d % 2) * MEM, (d // 2 % 2) * HALF
            out[2 + d // 4, at : at + MEM, lane : lane + HALF] = rows[d, last:, CHUNK - HALF :] if k == 0 else rows[d, :MEM, :HALF]
    for slot in range(slots):
        low = row_of(slot, row_ref) == 0
        dright_ref, edge_ref, dleft_ref = rest[3 * slot : 3 * slot + 3]
        for k in range(2):
            row = jnp.where(low, rows[k], rows[6 + k])
            edge_ref[k, :, :CHUNK] = row
            dright_ref[0, k * MEM : (k + 1) * MEM, :HALF] = row[last:, CHUNK - HALF :]
            dleft_ref[k * MEM : (k + 1) * MEM] = row[:MEM, :HALF]


def own_kernel(row_ref, state_ref, s0_ref, s1_ref):
    chunks = state_ref.shape[1] // 4
    for slot, s_ref in enumerate((s0_ref, s1_ref)):
        r = row_of(slot, row_ref)
        rows = [state_ref[r, 4 * q + res].astype(F32) for res in range(4) for q in range(chunks)]
        s_ref[...] = jnp.concatenate(rows, axis=0).astype(BF)


def pack(row, out_ref, k):
    last = row.shape[0] - MEM
    out_ref[k, :, :CHUNK] = row[MEM:last].astype(BF)
    half = NEAR // 2
    ends = [row[:MEM, CHUNK - NEAR : CHUNK - half], row[:MEM, CHUNK - half :], row[last:, :half], row[last:, half:NEAR]]
    out_ref[k, :, CHUNK:] = jnp.concatenate(ends, axis=0).astype(BF)


def unpack(msg):
    x = msg.astype(F32)
    own, ends = x[:, :CHUNK], x[:, CHUNK:]
    fill = jnp.zeros((MEM, CHUNK - 2 * ends.shape[1]), F32)
    before = jnp.concatenate([fill, ends[:MEM], ends[MEM : 2 * MEM]], axis=1)
    after = jnp.concatenate([ends[2 * MEM : 3 * MEM], ends[3 * MEM :], fill], axis=1)
    return jnp.concatenate([before, own, after], axis=0)


def windows(lats, narrow):
    parts = [[] for _ in range(4)]
    for a in lats:
        rows = a.shape[0]
        before = jnp.concatenate([a[rows - MEM :, CHUNK - 2 * VARS :], a[: rows - MEM, CHUNK - 2 * VARS :]], axis=0)
        after = jnp.concatenate([a[MEM:, : 2 * VARS], a[:MEM, : 2 * VARS]], axis=0)
        ext = jnp.concatenate([before, a, after], axis=1)
        if narrow:
            ext = ext[MEM : rows - MEM]
        for res in range(4):
            parts[res].append(ext[:, CELL * res : CELL * res + 2 * CELL])
    return jnp.concatenate([jnp.concatenate(p, axis=1) for p in parts], axis=0).astype(BF)


def latitude(pred, d):
    per = pred.shape[0] // 4
    return jnp.concatenate([pred[res * per : (res + 1) * per, d * CELL : (d + 1) * CELL] for res in range(4)], axis=1)


def of_band(band, values, *at):
    got = values[(0, *at)]
    for g in range(1, values.shape[0]):
        got = jnp.where(band == g, values[(g, *at)], got)
    return got


def block_at(index, ref):
    return pl.multiple_of(jnp.clip(index, 0, ref.shape[1] // BLK - 1) * BLK, BLK)


def block_pre(b, band, s_ref, in_ref, cidx, iidx, coup_ref, inp_ref):
    pieces = []
    mats = [coup_ref[band, (2 * b + k) * BLK : (2 * b + k + 1) * BLK, :] for k in range(2)]
    mats.append(inp_ref[band, b * BLK : (b + 1) * BLK, :])
    for k in range(2):
        pieces.append(s_ref[:, pl.ds(block_at(of_band(band, cidx, k, b), s_ref), BLK)])
    pieces.append(in_ref[:, pl.ds(block_at(of_band(band, iidx, b), in_ref), BLK)])
    return lax.dot_general(jnp.concatenate(pieces, axis=1), jnp.concatenate(mats, axis=1), NT, preferred_element_type=F32)


def half_of(r, rest_lats):
    return pl.ds(pl.multiple_of((1 - r if rest_lats else r) * 2 * CELL, 2 * CELL), 2 * CELL)


def send_edge(r, state, read_ref, msg_ref, edge_ref, s_ref):
    s_ref[...] = state
    pred = lax.dot_general(state, read_ref[half_of(r, False), :], NT, preferred_element_type=F32)
    for d in range(2):
        row = latitude(pred, d)
        pack(row, msg_ref, d)
        edge_ref[d] = row.astype(BF)


def first_kernel(slot, edge, behind, row_ref, band_ref, cidx_ref, iidx_ref, coup_ref, inp_ref, read_ref, own_ref, s0_ref, fl_ref, *rest):
    rest = list(rest)
    r = row_of(slot, row_ref)
    if edge:
        dl_ref, lat_ref, fr_ref, dr_ref = rest[:4]
        del rest[: 4 + behind]
    else:
        fr_ref = rest[2]
        del rest[:3]
    outs, (xs_ref, s_ref, in_ref) = rest[:-3], rest[-3:]
    fill = jnp.zeros((MEM, CHUNK - HALF), F32)

    def widen(own, left, right):
        left = jnp.concatenate([fill, left.astype(F32)], axis=1)
        right = jnp.concatenate([right.astype(F32), fill], axis=1)
        return jnp.concatenate([left, own.astype(F32), right], axis=0)

    for d in range(8):
        at, lane = (d % 2) * MEM, (d // 2 % 2) * HALF
        left = fl_ref[2 + d // 4, at : at + MEM, lane : lane + HALF]
        right = fr_ref[2 + d // 4, at : at + MEM, lane : lane + HALF]
        xs_ref[2 + d] = widen(own_ref[d], left, right)
    for k in range(2):
        at = k * MEM
        if edge:
            xs_ref[10 * r + k] = widen(lat_ref[k, :, :CHUNK], dl_ref[0, at : at + MEM, :HALF], dr_ref[at : at + MEM])
        else:
            xs_ref[10 * r + k] = jnp.zeros(xs_ref.shape[1:], F32)
    empty = jnp.zeros((MEM, s0_ref.shape[1]), F32)
    per = s0_ref.shape[0] // 4
    rows = []
    for res in range(4):
        rows.append(fl_ref[r, (res - 2) * MEM : (res - 1) * MEM].astype(F32) if res >= 2 else empty)
        rows.append(s0_ref[res * per : (res + 1) * per].astype(F32))
        rows.append(fr_ref[r, res * MEM : (res + 1) * MEM].astype(F32) if res < 2 else empty)
    s_ref[...] = jnp.concatenate(rows, axis=0).astype(BF)
    in_ref[...] = windows([xs_ref[4 * r + d] for d in range(8)], False)
    bands, cidx, iidx = band_ref[...], cidx_ref[...], iidx_ref[...]
    band = jnp.where(r == 0, bands[0], bands[1])
    pres = [block_pre(b, band, s_ref, in_ref, cidx, iidx, coup_ref, inp_ref) for b in range(iidx_ref.shape[1])]
    state = jnp.concatenate([jnp.tanh(p).astype(BF) for p in pres], axis=1)
    if edge:
        send_edge(r, state, read_ref, *outs)
        return
    outs[1][...] = state
    pred = lax.dot_general(state, read_ref[...], NT, preferred_element_type=F32)
    for d in range(4):
        outs[0][d] = latitude(pred, d).astype(BF)


def narrowed(s):
    per = s.shape[0] // 4
    return jnp.concatenate([s[res * per + MEM : (res + 1) * per - MEM] for res in range(4)], axis=0)


def shadow_kernel(last, slots, row_ref, band_ref, cidx_ref, iidx_ref, coup_ref, inp_ref, read_ref, *rest):
    rest = list(rest)

    def take(n):
        got = rest[:n]
        del rest[:n]
        return got

    edge_refs, s_refs = take(slots), take(slots)
    far_refs = take(2 * (2 - slots))
    pre_refs = take(slots)
    out_far = take(2 * (2 - slots))
    xs_ref, in_ref = take(2)
    rows_at = [row_of(0, row_ref), row_of(1, row_ref)]
    for k in range(2):
        xs_ref[k] = jnp.zeros(xs_ref.shape[1:], F32)
        xs_ref[10 + k] = jnp.zeros(xs_ref.shape[1:], F32)
    for slot in range(slots):
        r = rows_at[slot]
        pred = lax.dot_general(s_refs[slot][...], read_ref[half_of(r, True), :], NT, preferred_element_type=F32)
        for d in range(2):
            xs_ref[2 + 4 * r + 2 * r + d] = edge_refs[slot][d].astype(F32)
            xs_ref[2 + 4 * r + 2 * (1 - r) + d] = latitude(pred, d).astype(BF).astype(F32)
    if far_refs:
        for d in range(4):
            xs_ref[2 + 4 * rows_at[1] + d] = far_refs[0][d].astype(F32)
        s_refs = [s_refs[0], far_refs[1]]
    if last:
        short_refs = take(2)
        for slot in range(2):
            short_refs[slot][...] = narrowed(s_refs[slot][...].astype(F32)).astype(BF)
        s_refs = short_refs

    bands, cidx, iidx = band_ref[...], cidx_ref[...], iidx_ref[...]
    copy = None
    for slot in (1, 0):
        r = rows_at[slot]
        band = jnp.where(r == 0, bands[0], bands[1])
        in_ref[...] = windows([xs_ref[4 * r + d] for d in range(8)], last)
        blocks = iidx_ref.shape[1]
        pres = [block_pre(b, band, s_refs[slot], in_ref, cidx, iidx, coup_ref, inp_ref) for b in range(blocks)]
        if slot < slots:
            for b in range(blocks):
                pre_refs[slot][:, b * BLK : (b + 1) * BLK] = pres[b]
            continue
        state = jnp.concatenate([jnp.tanh(p).astype(BF) for p in pres], axis=1)
        if last:
            stage_ref, sem = take(2)
            copy = put_states(r, state, stage_ref, out_far[1], sem)
        else:
            out_far[1][...] = state
        pred = lax.dot_general(state, read_ref[...], NT, preferred_element_type=F32)
        for d in range(4):
            out_far[0][d] = latitude(pred, d).astype(BF)
    if copy is not None:
        copy.wait()


def put_states(r, state, stage_ref, states_hbm, sem):
    per = state.shape[0] // 4
    for res in range(4):
        for q in range(per // MEM):
            at = res * per + q * MEM
            stage_ref[4 * q + res] = state[at : at + MEM]
    copy = pltpu.make_async_copy(stage_ref, states_hbm.at[r], sem)
    copy.start()
    return copy


def late_kernel(slot, last, final, row_ref, band_ref, iidx_ref, inp_ref, read_ref, pre_ref, got_ref, *rest):
    r = row_of(slot, row_ref)
    bands, iidx = band_ref[...], iidx_ref[...]
    band = jnp.where(r == 0, bands[0], bands[1])
    in_ref = rest[-1]
    in_ref[...] = windows([unpack(got_ref[k]) for k in range(2)], last)
    parts = []
    for b in range(iidx_ref.shape[1]):
        k = of_band(band, iidx, b) - 15 * r
        used = jnp.logical_and(k >= 0, k < 5)
        at = pl.multiple_of(jnp.where(used, k, 0) * BLK, BLK)
        term = lax.dot_general(in_ref[:, pl.ds(at, BLK)], inp_ref[band, b * BLK : (b + 1) * BLK, :], NT, preferred_element_type=F32)
        pre = pre_ref[:, b * BLK : (b + 1) * BLK] + jnp.where(used, term, 0.0)
        parts.append(jnp.tanh(pre).astype(BF))
    state = jnp.concatenate(parts, axis=1)
    if not last:
        send_edge(r, state, read_ref, *rest[:3])
        return
    if not final:
        lats_ref, states_hbm, stage_ref, sem = rest[:4]
    else:
        other_ref, _, field_hbm, states_hbm, stage_ref, sem, field_ref, field_sem = rest[:8]
    copy = put_states(r, state, stage_ref, states_hbm, sem)
    pred = lax.dot_general(state, read_ref[...], NT, preferred_element_type=F32)
    mine = [latitude(pred, d) for d in range(4)]
    if not final:
        for d in range(4):
            lats_ref[d] = mine[d].astype(BF)
        copy.wait()
        return
    other = [other_ref[d].astype(F32) for d in range(4)]
    low = r == 0
    rows = [jnp.where(low, mine[d], other[d])[None] for d in range(4)]
    rows += [jnp.where(low, other[d], mine[d])[None] for d in range(4)]
    tiles = jnp.transpose(jnp.concatenate(rows, axis=0), (1, 0, 2)).astype(BF)
    for q in range(field_ref.shape[2] // CHUNK):
        for m in range(MEM):
            field_ref[m, :, q * CHUNK : (q + 1) * CHUNK] = tiles[q * MEM + m]
    out = pltpu.make_async_copy(field_ref, field_hbm, field_sem)
    out.start()
    copy.wait()
    out.wait()


def call(kernel, out_shape, out_specs, scratch, operands, flops=0, aliases=None):
    arrays = [pltpu.with_memory_space_constraint(x, pltpu.HBM) if s is HB else x for x, s in operands]
    size = sum(x.size * x.dtype.itemsize for x, _ in operands)
    return pl.pallas_call(
        kernel,
        out_shape=out_shape,
        in_specs=[s for _, s in operands],
        out_specs=out_specs,
        scratch_shapes=scratch,
        input_output_aliases=aliases or {},
        compiler_params=pltpu.CompilerParams(vmem_limit_bytes=40 * 1024 * 1024),
        cost_estimate=pl.CostEstimate(flops=flops, bytes_accessed=size, transcendentals=0),
    )(*arrays)


def per_device(field_state, reservoir_state, coupling_blocks, coupling_index, input_blocks, input_index, readout, region_band):
    lat_count, lon_count = lax.axis_size("lat"), lax.axis_size("lon")
    lat_at = lax.axis_index("lat").astype(jnp.int32)
    region_rows, regions, members, units = reservoir_state.shape
    outs = readout.shape[1]
    assert region_rows == 2 and members == MEM and regions % 4 == 0
    chunks = regions // 4
    own_rows = chunks * MEM
    wide = own_rows + 2 * MEM
    rows = 4 * wide
    short = 4 * own_rows
    swap = lat_count == 2
    slots = 1 if swap else 2

    def bf(*dims):
        return jax.ShapeDtypeStruct(dims, BF)

    def vm(dims, dtype=BF):
        return pltpu.VMEM(dims, dtype)

    def send(x, lat_step, lon_step):
        pairs = []
        for i in range(lat_count):
            to = 1 - i if swap and lat_step else i + lat_step
            if 0 <= to < lat_count:
                for j in range(lon_count):
                    pairs.append((i * lon_count + j, to * lon_count + (j + lon_step) % lon_count))
        return lax.ppermute(x, ("lat", "lon"), pairs)

    def across(xs, lon_step=0):
        if swap:
            return [send(xs[0], 1, lon_step)]
        return [send(xs[1], 1, lon_step), send(xs[0], -1, lon_step)]

    row = ((1 - lat_at if swap else lat_at * 0).reshape(1), SM)
    small = [(region_band, VM), (coupling_index.transpose(0, 2, 1), VM), (input_index, VM)]
    band, _, iidx = small
    flops = 2 * rows * units * (3 * BLK + outs)

    mail = call(
        functools.partial(message_kernel, slots),
        [bf(4, 2 * MEM, 2 * HALF)] * 2 + [bf(8, own_rows, CHUNK)] + [bf(4, 2 * MEM, 2 * HALF), bf(2, own_rows, 4 * HALF * 2 * MEM // own_rows), bf(2 * MEM, HALF)] * slots,
        [VM] * (3 + 3 * slots),
        [vm(field_state.shape), vm((2, region_rows, 2, MEM, units)), pltpu.SemaphoreType.DMA((3,))],
        [row, (field_state, HB), (reservoir_state, HB)],
        AHEAD,
    )
    from_left = send(mail[0], 0, 1)
    from_dleft = across(mail[3::3], 1)
    from_lat = across(mail[4::3])
    from_right = send(mail[1], 0, -1)
    from_dright = across(mail[5::3], -1)
    own = (mail[2], VM)
    s0, s1 = call(own_kernel, [bf(short, units)] * 2, [VM] * 2, [], [row, (reservoir_state, VM)], flops)
    weights = [(x, VM) for x in (coupling_blocks, input_blocks, readout[0])]
    states_shape = bf(region_rows, regions, MEM, units)
    stage = [vm((regions, MEM, units)), pltpu.SemaphoreType.DMA]
    padded = vm((12, wide, CHUNK), F32)
    send_out = [bf(2, own_rows, CHUNK + NEAR // 2), bf(2, wide, CHUNK), bf(rows, units)]

    sent, edges, states, far = [None] * slots, [None] * slots, [None] * slots, []
    for slot in (1, 0):
        edge = slot < slots
        operands = [row] + small + weights + [own, ((s0, s1)[slot], VM), (from_left, VM)]
        at = slot if edge else 0
        operands += [(from_dleft[at], VM), (from_lat[at], VM)]
        operands.append((from_right, VM))
        if edge:
            operands.append((from_dright[slot], VM))
            operands += [(x, VM) for x in far[1:]]
        got = call(
            functools.partial(first_kernel, slot, edge, len(far[1:])),
            send_out if edge else [bf(4, wide, CHUNK), bf(rows, units)],
            [VM] * (3 if edge else 2),
            [padded, vm((rows, units)), vm((rows, 16 * CELL))],
            operands,
            flops,
        )
        if edge:
            sent[slot], edges[slot], states[slot] = got
        else:
            far = list(got)

    for step in range(1, STEPS):
        last = step == STEPS - 1
        got = across(sent)
        pre_rows = short if last else rows
        out = [jax.ShapeDtypeStruct((pre_rows, units), F32)] * slots
        specs = [VM] * slots
        scratch = [padded, vm((pre_rows, 16 * CELL))] + [vm((short, units))] * (2 if last else 0)
        if swap:
            out += [bf(4, own_rows if last else wide, CHUNK), states_shape if last else bf(rows, units)]
            specs += [VM, HB if last else VM]
            scratch += stage if last else []
        shadow = call(
            functools.partial(shadow_kernel, last, slots),
            out,
            specs,
            scratch,
            [row] + small + weights + [(x, VM) for x in edges + states + far],
            2 * flops,
        )
        far = list(shadow[slots:])
        for slot in reversed(range(slots)):
            operands = [row, band, iidx] + weights[1:] + [(shadow[slot], VM), (got[slot], VM)]
            inputs = [vm((pre_rows, 4 * CELL))]
            if not last:
                sent[slot], edges[slot], states[slot] = call(
                    functools.partial(late_kernel, slot, False, False), send_out, [VM] * 3, inputs, operands, flops
                )
            elif slot == 1:
                far = call(
                    functools.partial(late_kernel, slot, True, False),
                    [bf(4, own_rows, CHUNK), states_shape],
                    [VM, HB],
                    stage + inputs,
                    operands,
                    flops,
                )
            else:
                return call(
                    functools.partial(late_kernel, slot, True, True),
                    [bf(MEM, 8, regions * CELL), states_shape],
                    [HB, HB],
                    stage + [vm((MEM, 8, regions * CELL)), pltpu.SemaphoreType.DMA] + inputs,
                    operands + [(far[0], VM), (far[1], HB)],
                    flops,
                    {len(operands) + 1: 1},
                )


def solution(mesh):
    return jax.shard_map(
        per_device,
        mesh=mesh,
        in_specs=(
            P(None, "lat", "lon"),
            P("lat", "lon", None, None),
            P("lat", None, None),
            P("lat", None, None),
            P("lat", None, None),
            P("lat", None),
            P("lat", None, None),
            P("lat"),
        ),
        out_specs=(P(None, "lat", "lon"), P("lat", "lon", None, None)),
        check_vma=False,
    )
```

```python
import functools

import jax
import jax.numpy as jnp
from jax import lax
from jax.experimental import pallas as pl
from jax.experimental.pallas import tpu as pltpu
from jax.sharding import PartitionSpec as P

VARS = 40
STEPS = 3
CELL = 4 * VARS
CHUNK = 4 * CELL
HALF = 512
NEAR = 256
MEM = 4
BLK = 128
AHEAD = 10**10
PAD = 128
BF = jnp.bfloat16
F32 = jnp.float32
VM = pl.BlockSpec(memory_space=pltpu.VMEM)
SM = pl.BlockSpec(memory_space=pltpu.SMEM)
HB = pl.BlockSpec(memory_space=pltpu.HBM)
NT = (((1,), (1,)), ((), ()))


def row_of(slot, row_ref):
    return row_ref[0] if slot == 0 else 1 - row_ref[0]


def message_kernel(slots, row_ref, field_hbm, state_hbm, right_ref, left_ref, own_ref, *rest):
    field_ref, state_ref, sems = rest[3 * slots :]
    regions = state_hbm.shape[1]
    copies = [
        pltpu.make_async_copy(field_hbm, field_ref, sems.at[0]),
        pltpu.make_async_copy(state_hbm.at[:, pl.ds(regions - 2, 2)], state_ref.at[0], sems.at[1]),
        pltpu.make_async_copy(state_hbm.at[:, pl.ds(0, 2)], state_ref.at[1], sems.at[2]),
    ]
    for c in copies:
        c.start()
    chunks = field_ref.shape[2] // CHUNK
    copies[0].wait()
    tiles = []
    for q in range(chunks):
        for m in range(MEM):
            tiles.append(field_ref[m, :, q * CHUNK : (q + 1) * CHUNK].astype(F32)[None])
    rows = jnp.transpose(jnp.concatenate(tiles, axis=0), (1, 0, 2)).astype(BF)
    own_ref[...] = rows
    last = (chunks - 1) * MEM
    for c in copies[1:]:
        c.wait()
    for k, out in enumerate((right_ref, left_ref)):
        for r in range(2):
            for j in range(2):
                out[r, j * MEM : (j + 1) * MEM, : 2 * HALF] = state_ref[k, r, j]
        for d in range(8):
            at, lane = (d % 2) * MEM, (d // 2 % 2) * HALF
            out[2 + d // 4, at : at + MEM, lane : lane + HALF] = rows[d, last:, CHUNK - HALF :] if k == 0 else rows[d, :MEM, :HALF]
    for slot in range(slots):
        low = row_of(slot, row_ref) == 0
        dright_ref, edge_ref, dleft_ref = rest[3 * slot : 3 * slot + 3]
        for k in range(2):
            row = jnp.where(low, rows[k], rows[6 + k])
            edge_ref[k, :, :CHUNK] = row
            dright_ref[0, k * MEM : (k + 1) * MEM, :HALF] = row[last:, CHUNK - HALF :]
            dleft_ref[k * MEM : (k + 1) * MEM] = row[:MEM, :HALF]


def own_kernel(row_ref, state_ref, s0_ref, s1_ref):
    chunks = state_ref.shape[1] // 4
    for slot, s_ref in enumerate((s0_ref, s1_ref)):
        r = row_of(slot, row_ref)
        rows = [state_ref[r, 4 * q + res].astype(F32) for res in range(4) for q in range(chunks)]
        s_ref[...] = jnp.concatenate(rows, axis=0).astype(BF)


def pack(row, out_ref, k):
    last = row.shape[0] - MEM
    out_ref[k, :, :CHUNK] = row[MEM:last].astype(BF)
    half = NEAR // 2
    ends = [row[:MEM, CHUNK - NEAR : CHUNK - half], row[:MEM, CHUNK - half :], row[last:, :half], row[last:, half:NEAR]]
    out_ref[k, :, CHUNK:] = jnp.concatenate(ends, axis=0).astype(BF)


def unpack(msg):
    x = msg.astype(F32)
    own, ends = x[:, :CHUNK], x[:, CHUNK:]
    fill = jnp.zeros((MEM, CHUNK - 2 * ends.shape[1]), F32)
    before = jnp.concatenate([fill, ends[:MEM], ends[MEM : 2 * MEM]], axis=1)
    after = jnp.concatenate([ends[2 * MEM : 3 * MEM], ends[3 * MEM :], fill], axis=1)
    return jnp.concatenate([before, own, after], axis=0)


def windows(lats, narrow):
    parts = [[] for _ in range(4)]
    for a in lats:
        rows = a.shape[0]
        before = jnp.concatenate([a[rows - MEM :, CHUNK - 2 * VARS :], a[: rows - MEM, CHUNK - 2 * VARS :]], axis=0)
        after = jnp.concatenate([a[MEM:, : 2 * VARS], a[:MEM, : 2 * VARS]], axis=0)
        ext = jnp.concatenate([before, a, after], axis=1)
        if narrow:
            ext = ext[MEM : rows - MEM]
        for res in range(4):
            parts[res].append(ext[:, CELL * res : CELL * res + 2 * CELL])
    return jnp.concatenate([jnp.concatenate(p, axis=1) for p in parts], axis=0).astype(BF)


def latitude(pred, d):
    per = pred.shape[0] // 4
    return jnp.concatenate([pred[res * per : (res + 1) * per, d * CELL : (d + 1) * CELL] for res in range(4)], axis=1)


def of_band(band, values, *at):
    got = values[(0, *at)]
    for g in range(1, values.shape[0]):
        got = jnp.where(band == g, values[(g, *at)], got)
    return got


def block_at(index, ref):
    return pl.multiple_of(jnp.clip(index, 0, ref.shape[1] // BLK - 1) * BLK, BLK)


def block_pre(b, band, s_ref, in_ref, cidx, iidx, coup_ref, inp_ref):
    pieces = []
    mats = [coup_ref[band, (2 * b + k) * BLK : (2 * b + k + 1) * BLK, :] for k in range(2)]
    mats.append(inp_ref[band, b * BLK : (b + 1) * BLK, :])
    for k in range(2):
        pieces.append(s_ref[:, pl.ds(block_at(of_band(band, cidx, k, b), s_ref), BLK)])
    pieces.append(in_ref[:, pl.ds(block_at(of_band(band, iidx, b), in_ref), BLK)])
    return lax.dot_general(jnp.concatenate(pieces, axis=1), jnp.concatenate(mats, axis=1), NT, preferred_element_type=F32)


def half_of(r, rest_lats):
    return pl.ds(pl.multiple_of((1 - r if rest_lats else r) * 2 * CELL, 2 * CELL), 2 * CELL)


def send_edge(r, state, read_ref, msg_ref, edge_ref, s_ref):
    s_ref[...] = state
    pred = lax.dot_general(state, read_ref[half_of(r, False), :], NT, preferred_element_type=F32)
    for d in range(2):
        row = latitude(pred, d)
        pack(row, msg_ref, d)
        edge_ref[d] = row.astype(BF)


def first_kernel(slot, edge, behind, row_ref, band_ref, cidx_ref, iidx_ref, coup_ref, inp_ref, read_ref, own_ref, s0_ref, fl_ref, *rest):
    rest = list(rest)
    r = row_of(slot, row_ref)
    if edge:
        dl_ref, lat_ref, fr_ref, dr_ref = rest[:4]
        del rest[: 4 + behind]
    else:
        fr_ref = rest[1]
        del rest[:2]
    outs, (xs_ref, s_ref, in_ref) = rest[:-3], rest[-3:]
    fill = jnp.zeros((MEM, CHUNK - HALF), F32)

    def widen(own, left, right):
        left = jnp.concatenate([fill, left.astype(F32)], axis=1)
        right = jnp.concatenate([right.astype(F32), fill], axis=1)
        return jnp.concatenate([left, own.astype(F32), right], axis=0)

    for d in range(8):
        at, lane = (d % 2) * MEM, (d // 2 % 2) * HALF
        left = fl_ref[2 + d // 4, at : at + MEM, lane : lane + HALF]
        right = fr_ref[2 + d // 4, at : at + MEM, lane : lane + HALF]
        xs_ref[2 + d] = widen(own_ref[d], left, right)
    for k in range(2):
        at = k * MEM
        if edge:
            xs_ref[10 * r + k] = widen(lat_ref[k, :, :CHUNK], dl_ref[0, at : at + MEM, :HALF], dr_ref[at : at + MEM])
        else:
            xs_ref[10 * r + k] = jnp.zeros(xs_ref.shape[1:], F32)
    empty = jnp.zeros((MEM, s0_ref.shape[1]), F32)
    per = s0_ref.shape[0] // 4
    rows = []
    for res in range(4):
        rows.append(fl_ref[r, (res - 2) * MEM : (res - 1) * MEM, : 2 * HALF].astype(F32) if res >= 2 else empty)
        rows.append(s0_ref[res * per : (res + 1) * per].astype(F32))
        rows.append(fr_ref[r, res * MEM : (res + 1) * MEM].astype(F32) if res < 2 else empty)
    s_ref[...] = jnp.concatenate(rows, axis=0).astype(BF)
    in_ref[...] = windows([xs_ref[4 * r + d] for d in range(8)], False)
    bands, cidx, iidx = band_ref[...], cidx_ref[...], iidx_ref[...]
    band = jnp.where(r == 0, bands[0], bands[1])
    pres = [block_pre(b, band, s_ref, in_ref, cidx, iidx, coup_ref, inp_ref) for b in range(iidx_ref.shape[1])]
    state = jnp.concatenate([jnp.tanh(p).astype(BF) for p in pres], axis=1)
    if edge:
        send_edge(r, state, read_ref, *outs)
        return
    outs[1][...] = state
    pred = lax.dot_general(state, read_ref[...], NT, preferred_element_type=F32)
    for d in range(4):
        outs[0][d] = latitude(pred, d).astype(BF)


def narrowed(s):
    per = s.shape[0] // 4
    return jnp.concatenate([s[res * per + MEM : (res + 1) * per - MEM] for res in range(4)], axis=0)


def shadow_kernel(last, slots, row_ref, band_ref, cidx_ref, iidx_ref, coup_ref, inp_ref, read_ref, *rest):
    rest = list(rest)

    def take(n):
        got = rest[:n]
        del rest[:n]
        return got

    edge_refs, s_refs = take(slots), take(slots)
    far_refs = take(2 * (2 - slots))
    pre_refs = take(slots)
    out_far = take(2 * (2 - slots))
    xs_ref, in_ref = take(2)
    rows_at = [row_of(0, row_ref), row_of(1, row_ref)]
    for k in range(2):
        xs_ref[k] = jnp.zeros(xs_ref.shape[1:], F32)
        xs_ref[10 + k] = jnp.zeros(xs_ref.shape[1:], F32)
    for slot in range(slots):
        r = rows_at[slot]
        pred = lax.dot_general(s_refs[slot][...], read_ref[half_of(r, True), :], NT, preferred_element_type=F32)
        for d in range(2):
            xs_ref[2 + 4 * r + 2 * r + d] = edge_refs[slot][d].astype(F32)
            xs_ref[2 + 4 * r + 2 * (1 - r) + d] = latitude(pred, d).astype(BF).astype(F32)
    if far_refs:
        for d in range(4):
            xs_ref[2 + 4 * rows_at[1] + d] = far_refs[0][d].astype(F32)
        s_refs = [s_refs[0], far_refs[1]]
    if last:
        short_refs = take(2)
        for slot in range(2):
            short_refs[slot][...] = narrowed(s_refs[slot][...].astype(F32)).astype(BF)
        s_refs = short_refs

    bands, cidx, iidx = band_ref[...], cidx_ref[...], iidx_ref[...]
    copy = None
    for slot in (1, 0):
        r = rows_at[slot]
        band = jnp.where(r == 0, bands[0], bands[1])
        in_ref[...] = windows([xs_ref[4 * r + d] for d in range(8)], last)
        blocks = iidx_ref.shape[1]
        pres = [block_pre(b, band, s_refs[slot], in_ref, cidx, iidx, coup_ref, inp_ref) for b in range(blocks)]
        if slot < slots:
            for b in range(blocks):
                pre_refs[slot][:, b * BLK : (b + 1) * BLK] = pres[b]
            continue
        state = jnp.concatenate([jnp.tanh(p).astype(BF) for p in pres], axis=1)
        if last:
            stage_ref, sem = take(2)
            copy = put_states(r, state, stage_ref, out_far[1], sem)
        else:
            out_far[1][...] = state
        pred = lax.dot_general(state, read_ref[...], NT, preferred_element_type=F32)
        for d in range(4):
            out_far[0][d] = latitude(pred, d).astype(BF)
    if copy is not None:
        copy.wait()


def put_states(r, state, stage_ref, states_hbm, sem):
    per = state.shape[0] // 4
    for res in range(4):
        for q in range(per // MEM):
            at = res * per + q * MEM
            stage_ref[4 * q + res] = state[at : at + MEM]
    copy = pltpu.make_async_copy(stage_ref, states_hbm.at[r], sem)
    copy.start()
    return copy


def late_kernel(slot, last, final, row_ref, band_ref, iidx_ref, inp_ref, read_ref, pre_ref, got_ref, *rest):
    r = row_of(slot, row_ref)
    bands, iidx = band_ref[...], iidx_ref[...]
    band = jnp.where(r == 0, bands[0], bands[1])
    in_ref = rest[-1]
    in_ref[...] = windows([unpack(got_ref[k]) for k in range(2)], last)
    parts = []
    for b in range(iidx_ref.shape[1]):
        k = of_band(band, iidx, b) - 15 * r
        used = jnp.logical_and(k >= 0, k < 5)
        at = pl.multiple_of(jnp.where(used, k, 0) * BLK, BLK)
        term = lax.dot_general(in_ref[:, pl.ds(at, BLK)], inp_ref[band, b * BLK : (b + 1) * BLK, :], NT, preferred_element_type=F32)
        pre = pre_ref[:, b * BLK : (b + 1) * BLK] + jnp.where(used, term, 0.0)
        parts.append(jnp.tanh(pre).astype(BF))
    state = jnp.concatenate(parts, axis=1)
    if not last:
        send_edge(r, state, read_ref, *rest[:3])
        return
    if not final:
        lats_ref, states_hbm, stage_ref, sem = rest[:4]
    else:
        other_ref, _, field_hbm, states_hbm, stage_ref, sem, field_ref, field_sem = rest[:8]
    copy = put_states(r, state, stage_ref, states_hbm, sem)
    pred = lax.dot_general(state, read_ref[...], NT, preferred_element_type=F32)
    mine = [latitude(pred, d) for d in range(4)]
    if not final:
        for d in range(4):
            lats_ref[d] = mine[d].astype(BF)
        copy.wait()
        return
    other = [other_ref[d].astype(F32) for d in range(4)]
    low = r == 0
    rows = [jnp.where(low, mine[d], other[d])[None] for d in range(4)]
    rows += [jnp.where(low, other[d], mine[d])[None] for d in range(4)]
    tiles = jnp.transpose(jnp.concatenate(rows, axis=0), (1, 0, 2)).astype(BF)
    for q in range(field_ref.shape[2] // CHUNK):
        for m in range(MEM):
            field_ref[m, :, q * CHUNK : (q + 1) * CHUNK] = tiles[q * MEM + m]
    out = pltpu.make_async_copy(field_ref, field_hbm, field_sem)
    out.start()
    copy.wait()
    out.wait()


def call(kernel, out_shape, out_specs, scratch, operands, flops=0, aliases=None):
    arrays = [pltpu.with_memory_space_constraint(x, pltpu.HBM) if s is HB else x for x, s in operands]
    size = sum(x.size * x.dtype.itemsize for x, _ in operands)
    return pl.pallas_call(
        kernel,
        out_shape=out_shape,
        in_specs=[s for _, s in operands],
        out_specs=out_specs,
        scratch_shapes=scratch,
        input_output_aliases=aliases or {},
        compiler_params=pltpu.CompilerParams(vmem_limit_bytes=40 * 1024 * 1024),
        cost_estimate=pl.CostEstimate(flops=flops, bytes_accessed=size, transcendentals=0),
    )(*arrays)


def per_device(field_state, reservoir_state, coupling_blocks, coupling_index, input_blocks, input_index, readout, region_band):
    lat_count, lon_count = lax.axis_size("lat"), lax.axis_size("lon")
    lat_at = lax.axis_index("lat").astype(jnp.int32)
    region_rows, regions, members, units = reservoir_state.shape
    outs = readout.shape[1]
    assert region_rows == 2 and members == MEM and regions % 4 == 0
    chunks = regions // 4
    own_rows = chunks * MEM
    wide = own_rows + 2 * MEM
    rows = 4 * wide
    short = 4 * own_rows
    swap = lat_count == 2
    slots = 1 if swap else 2

    def bf(*dims):
        return jax.ShapeDtypeStruct(dims, BF)

    def vm(dims, dtype=BF):
        return pltpu.VMEM(dims, dtype)

    def send(x, lat_step, lon_step):
        pairs = []
        for i in range(lat_count):
            to = 1 - i if swap and lat_step else i + lat_step
            if 0 <= to < lat_count:
                for j in range(lon_count):
                    pairs.append((i * lon_count + j, to * lon_count + (j + lon_step) % lon_count))
        return lax.ppermute(x, ("lat", "lon"), pairs)

    def across(xs, lon_step=0):
        if swap:
            return [send(xs[0], 1, lon_step)]
        return [send(xs[1], 1, lon_step), send(xs[0], -1, lon_step)]

    row = ((1 - lat_at if swap else lat_at * 0).reshape(1), SM)
    small = [(region_band, VM), (coupling_index.transpose(0, 2, 1), VM), (input_index, VM)]
    band, _, iidx = small
    flops = 2 * rows * units * (3 * BLK + outs)

    mail = call(
        functools.partial(message_kernel, slots),
        [bf(4, 2 * MEM, 2 * HALF + PAD), bf(4, 2 * MEM, 2 * HALF), bf(8, own_rows, CHUNK)]
        + [bf(4, 2 * MEM, 2 * HALF + PAD), bf(2, own_rows, 4 * HALF * 2 * MEM // own_rows), bf(2 * MEM, HALF)] * slots,
        [VM] * (3 + 3 * slots),
        [vm(field_state.shape), vm((2, region_rows, 2, MEM, units)), pltpu.SemaphoreType.DMA((3,))],
        [row, (field_state, HB), (reservoir_state, HB)],
        AHEAD,
    )
    from_left = send(mail[0], 0, 1)
    from_dleft = across(mail[3::3], 1)
    from_lat = across(mail[4::3])
    from_right = send(mail[1], 0, -1)
    from_dright = across(mail[5::3], -1)
    own = (mail[2], VM)
    s0, s1 = call(own_kernel, [bf(short, units)] * 2, [VM] * 2, [], [row, (reservoir_state, VM)], flops)
    weights = [(x, VM) for x in (coupling_blocks, input_blocks, readout[0])]
    states_shape = bf(region_rows, regions, MEM, units)
    stage = [vm((regions, MEM, units)), pltpu.SemaphoreType.DMA]
    padded = vm((12, wide, CHUNK), F32)
    send_out = [bf(2, own_rows, CHUNK + NEAR // 2), bf(2, wide, CHUNK), bf(rows, units)]

    sent, edges, states, far = [None] * slots, [None] * slots, [None] * slots, []
    for slot in (1, 0):
        edge = slot < slots
        operands = [row] + small + weights + [own, ((s0, s1)[slot], VM), (from_left, VM)]
        if edge:
            operands.append((from_dleft[slot], VM))
        operands.append((from_lat[slot if edge else 0], VM))
        operands.append((from_right, VM))
        if edge:
            operands.append((from_dright[slot], VM))
            operands += [(x, VM) for x in far[1:]]
        got = call(
            functools.partial(first_kernel, slot, edge, len(far[1:])),
            send_out if edge else [bf(4, wide, CHUNK), bf(rows, units)],
            [VM] * (3 if edge else 2),
            [padded, vm((rows, units)), vm((rows, 16 * CELL))],
            operands,
            flops if edge else 0,
        )
        if edge:
            sent[slot], edges[slot], states[slot] = got
        else:
            far = list(got)

    for step in range(1, STEPS):
        last = step == STEPS - 1
        got = across(sent)
        pre_rows = short if last else rows
        out = [jax.ShapeDtypeStruct((pre_rows, units), F32)] * slots
        specs = [VM] * slots
        scratch = [padded, vm((pre_rows, 16 * CELL))] + [vm((short, units))] * (2 if last else 0)
        if swap:
            out += [bf(4, own_rows if last else wide, CHUNK), states_shape if last else bf(rows, units)]
            specs += [VM, HB if last else VM]
            scratch += stage if last else []
        shadow = call(
            functools.partial(shadow_kernel, last, slots),
            out,
            specs,
            scratch,
            [row] + small + weights + [(x, VM) for x in edges + states + far],
            2 * flops,
        )
        far = list(shadow[slots:])
        for slot in reversed(range(slots)):
            operands = [row, band, iidx] + weights[1:] + [(shadow[slot], VM), (got[slot], VM)]
            inputs = [vm((pre_rows, 4 * CELL))]
            if not last:
                sent[slot], edges[slot], states[slot] = call(
                    functools.partial(late_kernel, slot, False, False), send_out, [VM] * 3, inputs, operands, flops
                )
            elif slot == 1:
                far = call(
                    functools.partial(late_kernel, slot, True, False),
                    [bf(4, own_rows, CHUNK), states_shape],
                    [VM, HB],
                    stage + inputs,
                    operands,
                    flops,
                )
            else:
                return call(
                    functools.partial(late_kernel, slot, True, True),
                    [bf(MEM, 8, regions * CELL), states_shape],
                    [HB, HB],
                    stage + [vm((MEM, 8, regions * CELL)), pltpu.SemaphoreType.DMA] + inputs,
                    operands + [(far[0], VM), (far[1], HB)],
                    flops,
                    {len(operands) + 1: 1},
                )


def solution(mesh):
    return jax.shard_map(
        per_device,
        mesh=mesh,
        in_specs=(
            P(None, "lat", "lon"),
            P("lat", "lon", None, None),
            P("lat", None, None),
            P("lat", None, None),
            P("lat", None, None),
            P("lat", None),
            P("lat", None, None),
            P("lat"),
        ),
        out_specs=(P(None, "lat", "lon"), P("lat", "lon", None, None)),
        check_vma=False,
    )
```

```python
import functools

import jax
import jax.numpy as jnp
from jax import lax
from jax.experimental import pallas as pl
from jax.experimental.pallas import tpu as pltpu
from jax.sharding import PartitionSpec as P

VARS = 40
STEPS = 3
CELL = 4 * VARS
CHUNK = 4 * CELL
HALF = 512
NEAR = 256
MEM = 4
BLK = 128
AHEAD = 10**10
PAD = 128
BF = jnp.bfloat16
F32 = jnp.float32
VM = pl.BlockSpec(memory_space=pltpu.VMEM)
SM = pl.BlockSpec(memory_space=pltpu.SMEM)
HB = pl.BlockSpec(memory_space=pltpu.HBM)
NT = (((1,), (1,)), ((), ()))


def row_of(slot, row_ref):
    return row_ref[0] if slot == 0 else 1 - row_ref[0]


def message_kernel(slots, row_ref, field_hbm, state_hbm, right_ref, left_ref, own_ref, *rest):
    field_ref, state_ref, sems = rest[3 * slots :]
    regions = state_hbm.shape[1]
    copies = [
        pltpu.make_async_copy(field_hbm, field_ref, sems.at[0]),
        pltpu.make_async_copy(state_hbm.at[:, pl.ds(regions - 2, 2)], state_ref.at[0], sems.at[1]),
        pltpu.make_async_copy(state_hbm.at[:, pl.ds(0, 2)], state_ref.at[1], sems.at[2]),
    ]
    for c in copies:
        c.start()
    chunks = field_ref.shape[2] // CHUNK
    copies[0].wait()
    tiles = []
    for q in range(chunks):
        for m in range(MEM):
            tiles.append(field_ref[m, :, q * CHUNK : (q + 1) * CHUNK].astype(F32)[None])
    rows = jnp.transpose(jnp.concatenate(tiles, axis=0), (1, 0, 2)).astype(BF)
    own_ref[...] = rows
    last = (chunks - 1) * MEM
    for c in copies[1:]:
        c.wait()
    for k, out in enumerate((right_ref, left_ref)):
        for r in range(2):
            for j in range(2):
                out[r, j * MEM : (j + 1) * MEM, : 2 * HALF] = state_ref[k, r, j]
        for d in range(8):
            at, lane = (d % 2) * MEM, (d // 2 % 2) * HALF
            out[2 + d // 4, at : at + MEM, lane : lane + HALF] = rows[d, last:, CHUNK - HALF :] if k == 0 else rows[d, :MEM, :HALF]
    for slot in range(slots):
        low = row_of(slot, row_ref) == 0
        dright_ref, edge_ref, dleft_ref = rest[3 * slot : 3 * slot + 3]
        for k in range(2):
            row = jnp.where(low, rows[k], rows[6 + k])
            edge_ref[k, :, :CHUNK] = row
            dright_ref[0, k * MEM : (k + 1) * MEM, :HALF] = row[last:, CHUNK - HALF :]
            dleft_ref[k * MEM : (k + 1) * MEM] = row[:MEM, :HALF]


def own_kernel(row_ref, state_ref, s0_ref, s1_ref):
    chunks = state_ref.shape[1] // 4
    for slot, s_ref in enumerate((s0_ref, s1_ref)):
        r = row_of(slot, row_ref)
        rows = [state_ref[r, 4 * q + res].astype(F32) for res in range(4) for q in range(chunks)]
        s_ref[...] = jnp.concatenate(rows, axis=0).astype(BF)


def pack(row, out_ref, k):
    last = row.shape[0] - MEM
    out_ref[k, :, :CHUNK] = row[MEM:last].astype(BF)
    half = NEAR // 2
    ends = [row[:MEM, CHUNK - NEAR : CHUNK - half], row[:MEM, CHUNK - half :], row[last:, :half], row[last:, half:NEAR]]
    out_ref[k, :, CHUNK:] = jnp.concatenate(ends, axis=0).astype(BF)


def unpack(msg):
    x = msg.astype(F32)
    own, ends = x[:, :CHUNK], x[:, CHUNK:]
    fill = jnp.zeros((MEM, CHUNK - 2 * ends.shape[1]), F32)
    before = jnp.concatenate([fill, ends[:MEM], ends[MEM : 2 * MEM]], axis=1)
    after = jnp.concatenate([ends[2 * MEM : 3 * MEM], ends[3 * MEM :], fill], axis=1)
    return jnp.concatenate([before, own, after], axis=0)


def windows(lats, narrow):
    parts = [[] for _ in range(4)]
    side = 2 * VARS
    for a in lats:
        rows = a.shape[0]
        before = jnp.concatenate([a[rows - MEM :, CHUNK - side :], a[: rows - MEM, CHUNK - side :]], axis=0)
        after = jnp.concatenate([a[MEM:, :side], a[:MEM, :side]], axis=0)
        parts[0] += [before, a[:, : 3 * side]]
        parts[1].append(a[:, side : 5 * side])
        parts[2].append(a[:, 3 * side : 7 * side])
        parts[3] += [a[:, 5 * side :], after]
    if narrow:
        parts = [[x[MEM : x.shape[0] - MEM] for x in p] for p in parts]
    return jnp.concatenate([jnp.concatenate(p, axis=1) for p in parts], axis=0).astype(BF)


def latitude(pred, d):
    per = pred.shape[0] // 4
    return jnp.concatenate([pred[res * per : (res + 1) * per, d * CELL : (d + 1) * CELL] for res in range(4)], axis=1)


def of_band(band, values, *at):
    got = values[(0, *at)]
    for g in range(1, values.shape[0]):
        got = jnp.where(band == g, values[(g, *at)], got)
    return got


def block_at(index, ref):
    return pl.multiple_of(jnp.clip(index, 0, ref.shape[1] // BLK - 1) * BLK, BLK)


def block_pre(b, band, s_ref, in_ref, cidx, iidx, coup_ref, inp_ref):
    pieces = []
    mats = [coup_ref[band, (2 * b + k) * BLK : (2 * b + k + 1) * BLK, :] for k in range(2)]
    mats.append(inp_ref[band, b * BLK : (b + 1) * BLK, :])
    for k in range(2):
        pieces.append(s_ref[:, pl.ds(block_at(of_band(band, cidx, k, b), s_ref), BLK)])
    pieces.append(in_ref[:, pl.ds(block_at(of_band(band, iidx, b), in_ref), BLK)])
    return lax.dot_general(jnp.concatenate(pieces, axis=1), jnp.concatenate(mats, axis=1), NT, preferred_element_type=F32)


def half_of(r, rest_lats):
    return pl.ds(pl.multiple_of((1 - r if rest_lats else r) * 2 * CELL, 2 * CELL), 2 * CELL)


def send_edge(r, state, read_ref, msg_ref, edge_ref, s_ref):
    s_ref[...] = state
    pred = lax.dot_general(state, read_ref[half_of(r, False), :], NT, preferred_element_type=F32)
    for d in range(2):
        row = latitude(pred, d)
        pack(row, msg_ref, d)
        edge_ref[d] = row.astype(BF)


def first_kernel(slot, edge, behind, row_ref, band_ref, cidx_ref, iidx_ref, coup_ref, inp_ref, read_ref, own_ref, s0_ref, fl_ref, *rest):
    rest = list(rest)
    r = row_of(slot, row_ref)
    if edge:
        dl_ref, lat_ref, fr_ref, dr_ref = rest[:4]
        del rest[: 4 + behind]
    else:
        fr_ref = rest[1]
        del rest[:2]
    outs, (xs_ref, s_ref, in_ref) = rest[:-3], rest[-3:]
    fill = jnp.zeros((MEM, CHUNK - HALF), F32)

    def widen(own, left, right):
        left = jnp.concatenate([fill, left.astype(F32)], axis=1)
        right = jnp.concatenate([right.astype(F32), fill], axis=1)
        return jnp.concatenate([left, own.astype(F32), right], axis=0)

    for d in range(8):
        at, lane = (d % 2) * MEM, (d // 2 % 2) * HALF
        left = fl_ref[2 + d // 4, at : at + MEM, lane : lane + HALF]
        right = fr_ref[2 + d // 4, at : at + MEM, lane : lane + HALF]
        xs_ref[2 + d] = widen(own_ref[d], left, right)
    for k in range(2):
        at = k * MEM
        if edge:
            xs_ref[10 * r + k] = widen(lat_ref[k, :, :CHUNK], dl_ref[0, at : at + MEM, :HALF], dr_ref[at : at + MEM])
        else:
            xs_ref[10 * r + k] = jnp.zeros(xs_ref.shape[1:], F32)
    empty = jnp.zeros((MEM, s0_ref.shape[1]), F32)
    per = s0_ref.shape[0] // 4
    rows = []
    for res in range(4):
        rows.append(fl_ref[r, (res - 2) * MEM : (res - 1) * MEM, : 2 * HALF].astype(F32) if res >= 2 else empty)
        rows.append(s0_ref[res * per : (res + 1) * per].astype(F32))
        rows.append(fr_ref[r, res * MEM : (res + 1) * MEM].astype(F32) if res < 2 else empty)
    s_ref[...] = jnp.concatenate(rows, axis=0).astype(BF)
    in_ref[...] = windows([xs_ref[4 * r + d] for d in range(8)], False)
    bands, cidx, iidx = band_ref[...], cidx_ref[...], iidx_ref[...]
    band = jnp.where(r == 0, bands[0], bands[1])
    pres = [block_pre(b, band, s_ref, in_ref, cidx, iidx, coup_ref, inp_ref) for b in range(iidx_ref.shape[1])]
    state = jnp.concatenate([jnp.tanh(p).astype(BF) for p in pres], axis=1)
    if edge:
        send_edge(r, state, read_ref, *outs)
        return
    outs[1][...] = state
    pred = lax.dot_general(state, read_ref[...], NT, preferred_element_type=F32)
    for d in range(4):
        outs[0][d] = latitude(pred, d).astype(BF)


def narrowed(s):
    per = s.shape[0] // 4
    return jnp.concatenate([s[res * per + MEM : (res + 1) * per - MEM] for res in range(4)], axis=0)


def shadow_kernel(last, slots, row_ref, band_ref, cidx_ref, iidx_ref, coup_ref, inp_ref, read_ref, *rest):
    rest = list(rest)

    def take(n):
        got = rest[:n]
        del rest[:n]
        return got

    edge_refs, s_refs = take(slots), take(slots)
    far_refs = take(2 * (2 - slots))
    pre_refs = take(slots)
    out_far = take(2 * (2 - slots))
    xs_ref, in_ref = take(2)
    rows_at = [row_of(0, row_ref), row_of(1, row_ref)]
    for k in range(2):
        xs_ref[k] = jnp.zeros(xs_ref.shape[1:], F32)
        xs_ref[10 + k] = jnp.zeros(xs_ref.shape[1:], F32)
    for slot in range(slots):
        r = rows_at[slot]
        pred = lax.dot_general(s_refs[slot][...], read_ref[half_of(r, True), :], NT, preferred_element_type=F32)
        for d in range(2):
            xs_ref[2 + 4 * r + 2 * r + d] = edge_refs[slot][d].astype(F32)
            xs_ref[2 + 4 * r + 2 * (1 - r) + d] = latitude(pred, d).astype(BF).astype(F32)
    if far_refs:
        for d in range(4):
            xs_ref[2 + 4 * rows_at[1] + d] = far_refs[0][d].astype(F32)
        s_refs = [s_refs[0], far_refs[1]]
    if last:
        short_refs = take(2)
        for slot in range(2):
            short_refs[slot][...] = narrowed(s_refs[slot][...].astype(F32)).astype(BF)
        s_refs = short_refs

    bands, cidx, iidx = band_ref[...], cidx_ref[...], iidx_ref[...]
    copy = None
    for slot in (1, 0):
        r = rows_at[slot]
        band = jnp.where(r == 0, bands[0], bands[1])
        in_ref[...] = windows([xs_ref[4 * r + d] for d in range(8)], last)
        blocks = iidx_ref.shape[1]
        pres = [block_pre(b, band, s_refs[slot], in_ref, cidx, iidx, coup_ref, inp_ref) for b in range(blocks)]
        if slot < slots:
            for b in range(blocks):
                pre_refs[slot][:, b * BLK : (b + 1) * BLK] = pres[b]
            continue
        state = jnp.concatenate([jnp.tanh(p).astype(BF) for p in pres], axis=1)
        if last:
            stage_ref, sem = take(2)
            copy = put_states(r, state, stage_ref, out_far[1], sem)
        else:
            out_far[1][...] = state
        pred = lax.dot_general(state, read_ref[...], NT, preferred_element_type=F32)
        for d in range(4):
            out_far[0][d] = latitude(pred, d).astype(BF)
    if copy is not None:
        copy.wait()


def put_states(r, state, stage_ref, states_hbm, sem):
    per = state.shape[0] // 4
    for res in range(4):
        for q in range(per // MEM):
            at = res * per + q * MEM
            stage_ref[4 * q + res] = state[at : at + MEM]
    copy = pltpu.make_async_copy(stage_ref, states_hbm.at[r], sem)
    copy.start()
    return copy


def late_kernel(slot, last, final, row_ref, band_ref, iidx_ref, inp_ref, read_ref, pre_ref, got_ref, *rest):
    r = row_of(slot, row_ref)
    bands, iidx = band_ref[...], iidx_ref[...]
    band = jnp.where(r == 0, bands[0], bands[1])
    in_ref = rest[-1]
    in_ref[...] = windows([unpack(got_ref[k]) for k in range(2)], last)
    parts = []
    for b in range(iidx_ref.shape[1]):
        k = of_band(band, iidx, b) - 15 * r
        used = jnp.logical_and(k >= 0, k < 5)
        at = pl.multiple_of(jnp.where(used, k, 0) * BLK, BLK)
        term = lax.dot_general(in_ref[:, pl.ds(at, BLK)], inp_ref[band, b * BLK : (b + 1) * BLK, :], NT, preferred_element_type=F32)
        pre = pre_ref[:, b * BLK : (b + 1) * BLK] + jnp.where(used, term, 0.0)
        parts.append(jnp.tanh(pre).astype(BF))
    state = jnp.concatenate(parts, axis=1)
    if not last:
        send_edge(r, state, read_ref, *rest[:3])
        return
    if not final:
        lats_ref, states_hbm, stage_ref, sem = rest[:4]
    else:
        other_ref, _, field_hbm, states_hbm, stage_ref, sem, field_ref, field_sem = rest[:8]
    copy = put_states(r, state, stage_ref, states_hbm, sem)
    pred = lax.dot_general(state, read_ref[...], NT, preferred_element_type=F32)
    mine = [latitude(pred, d) for d in range(4)]
    if not final:
        for d in range(4):
            lats_ref[d] = mine[d].astype(BF)
        copy.wait()
        return
    other = [other_ref[d].astype(F32) for d in range(4)]
    low = r == 0
    rows = [jnp.where(low, mine[d], other[d])[None] for d in range(4)]
    rows += [jnp.where(low, other[d], mine[d])[None] for d in range(4)]
    tiles = jnp.transpose(jnp.concatenate(rows, axis=0), (1, 0, 2)).astype(BF)
    for q in range(field_ref.shape[2] // CHUNK):
        for m in range(MEM):
            field_ref[m, :, q * CHUNK : (q + 1) * CHUNK] = tiles[q * MEM + m]
    out = pltpu.make_async_copy(field_ref, field_hbm, field_sem)
    out.start()
    copy.wait()
    out.wait()


def call(kernel, out_shape, out_specs, scratch, operands, flops=0, aliases=None):
    arrays = [pltpu.with_memory_space_constraint(x, pltpu.HBM) if s is HB else x for x, s in operands]
    size = sum(x.size * x.dtype.itemsize for x, _ in operands)
    return pl.pallas_call(
        kernel,
        out_shape=out_shape,
        in_specs=[s for _, s in operands],
        out_specs=out_specs,
        scratch_shapes=scratch,
        input_output_aliases=aliases or {},
        compiler_params=pltpu.CompilerParams(vmem_limit_bytes=40 * 1024 * 1024),
        cost_estimate=pl.CostEstimate(flops=flops, bytes_accessed=size, transcendentals=0),
    )(*arrays)


def per_device(field_state, reservoir_state, coupling_blocks, coupling_index, input_blocks, input_index, readout, region_band):
    lat_count, lon_count = lax.axis_size("lat"), lax.axis_size("lon")
    lat_at = lax.axis_index("lat").astype(jnp.int32)
    region_rows, regions, members, units = reservoir_state.shape
    outs = readout.shape[1]
    assert region_rows == 2 and members == MEM and regions % 4 == 0
    chunks = regions // 4
    own_rows = chunks * MEM
    wide = own_rows + 2 * MEM
    rows = 4 * wide
    short = 4 * own_rows
    swap = lat_count == 2
    slots = 1 if swap else 2

    def bf(*dims):
        return jax.ShapeDtypeStruct(dims, BF)

    def vm(dims, dtype=BF):
        return pltpu.VMEM(dims, dtype)

    def send(x, lat_step, lon_step):
        pairs = []
        for i in range(lat_count):
            to = 1 - i if swap and lat_step else i + lat_step
            if 0 <= to < lat_count:
                for j in range(lon_count):
                    pairs.append((i * lon_count + j, to * lon_count + (j + lon_step) % lon_count))
        return lax.ppermute(x, ("lat", "lon"), pairs)

    def across(xs, lon_step=0):
        if swap:
            return [send(xs[0], 1, lon_step)]
        return [send(xs[1], 1, lon_step), send(xs[0], -1, lon_step)]

    row = ((1 - lat_at if swap else lat_at * 0).reshape(1), SM)
    small = [(region_band, VM), (coupling_index.transpose(0, 2, 1), VM), (input_index, VM)]
    band, _, iidx = small
    flops = 2 * rows * units * (3 * BLK + outs)

    mail = call(
        functools.partial(message_kernel, slots),
        [bf(4, 2 * MEM, 2 * HALF + PAD), bf(4, 2 * MEM, 2 * HALF), bf(8, own_rows, CHUNK)]
        + [bf(4, 2 * MEM, 2 * HALF + PAD), bf(2, own_rows, 4 * HALF * 2 * MEM // own_rows), bf(2 * MEM, HALF)] * slots,
        [VM] * (3 + 3 * slots),
        [vm(field_state.shape), vm((2, region_rows, 2, MEM, units)), pltpu.SemaphoreType.DMA((3,))],
        [row, (field_state, HB), (reservoir_state, HB)],
        AHEAD,
    )
    from_left = send(mail[0], 0, 1)
    from_dleft = across(mail[3::3], 1)
    from_lat = across(mail[4::3])
    from_right = send(mail[1], 0, -1)
    from_dright = across(mail[5::3], -1)
    own = (mail[2], VM)
    s0, s1 = call(own_kernel, [bf(short, units)] * 2, [VM] * 2, [], [row, (reservoir_state, VM)], flops)
    weights = [(x, VM) for x in (coupling_blocks, input_blocks, readout[0])]
    states_shape = bf(region_rows, regions, MEM, units)
    stage = [vm((regions, MEM, units)), pltpu.SemaphoreType.DMA]
    padded = vm((12, wide, CHUNK), F32)
    send_out = [bf(2, own_rows, CHUNK + NEAR // 2), bf(2, wide, CHUNK), bf(rows, units)]

    sent, edges, states, far = [None] * slots, [None] * slots, [None] * slots, []
    for slot in (1, 0):
        edge = slot < slots
        operands = [row] + small + weights + [own, ((s0, s1)[slot], VM), (from_left, VM)]
        if edge:
            operands.append((from_dleft[slot], VM))
        operands.append((from_lat[slot if edge else 0], VM))
        operands.append((from_right, VM))
        if edge:
            operands.append((from_dright[slot], VM))
            operands += [(x, VM) for x in far[1:]]
        got = call(
            functools.partial(first_kernel, slot, edge, len(far[1:])),
            send_out if edge else [bf(4, wide, CHUNK), bf(rows, units)],
            [VM] * (3 if edge else 2),
            [padded, vm((rows, units)), vm((rows, 16 * CELL))],
            operands,
            flops if edge else 0,
        )
        if edge:
            sent[slot], edges[slot], states[slot] = got
        else:
            far = list(got)

    for step in range(1, STEPS):
        last = step == STEPS - 1
        got = across(sent)
        pre_rows = short if last else rows
        out = [jax.ShapeDtypeStruct((pre_rows, units), F32)] * slots
        specs = [VM] * slots
        scratch = [padded, vm((pre_rows, 16 * CELL))] + [vm((short, units))] * (2 if last else 0)
        if swap:
            out += [bf(4, own_rows if last else wide, CHUNK), states_shape if last else bf(rows, units)]
            specs += [VM, HB if last else VM]
            scratch += stage if last else []
        shadow = call(
            functools.partial(shadow_kernel, last, slots),
            out,
            specs,
            scratch,
            [row] + small + weights + [(x, VM) for x in edges + states + far],
            2 * flops,
        )
        far = list(shadow[slots:])
        for slot in reversed(range(slots)):
            operands = [row, band, iidx] + weights[1:] + [(shadow[slot], VM), (got[slot], VM)]
            inputs = [vm((pre_rows, 4 * CELL))]
            if not last:
                sent[slot], edges[slot], states[slot] = call(
                    functools.partial(late_kernel, slot, False, False), send_out, [VM] * 3, inputs, operands, flops
                )
            elif slot == 1:
                far = call(
                    functools.partial(late_kernel, slot, True, False),
                    [bf(4, own_rows, CHUNK), states_shape],
                    [VM, HB],
                    stage + inputs,
                    operands,
                    flops,
                )
            else:
                return call(
                    functools.partial(late_kernel, slot, True, True),
                    [bf(MEM, 8, regions * CELL), states_shape],
                    [HB, HB],
                    stage + [vm((MEM, 8, regions * CELL)), pltpu.SemaphoreType.DMA] + inputs,
                    operands + [(far[0], VM), (far[1], HB)],
                    flops,
                    {len(operands) + 1: 1},
                )


def solution(mesh):
    return jax.shard_map(
        per_device,
        mesh=mesh,
        in_specs=(
            P(None, "lat", "lon"),
            P("lat", "lon", None, None),
            P("lat", None, None),
            P("lat", None, None),
            P("lat", None, None),
            P("lat", None),
            P("lat", None, None),
            P("lat"),
        ),
        out_specs=(P(None, "lat", "lon"), P("lat", "lon", None, None)),
        check_vma=False,
    )
```

```python
import functools

import jax
import jax.numpy as jnp
from jax import lax
from jax.experimental import pallas as pl
from jax.experimental.pallas import tpu as pltpu
from jax.sharding import PartitionSpec as P

VARS = 40
STEPS = 3
CELL = 4 * VARS
CHUNK = 4 * CELL
HALF = 512
NEAR = 256
MEM = 4
BLK = 128
AHEAD = 10**10
ORDER = (3 * 10**8, 3 * 10**8)
BF = jnp.bfloat16
F32 = jnp.float32
VM = pl.BlockSpec(memory_space=pltpu.VMEM)
SM = pl.BlockSpec(memory_space=pltpu.SMEM)
HB = pl.BlockSpec(memory_space=pltpu.HBM)
NT = (((1,), (1,)), ((), ()))


def row_of(slot, row_ref):
    return row_ref[0] if slot == 0 else 1 - row_ref[0]


def message_kernel(slots, row_ref, field_hbm, state_hbm, right_ref, left_ref, own_ref, *rest):
    field_ref, state_ref, sems = rest[3 * slots :]
    regions = state_hbm.shape[1]
    copies = [
        pltpu.make_async_copy(field_hbm, field_ref, sems.at[0]),
        pltpu.make_async_copy(state_hbm.at[:, pl.ds(regions - 2, 2)], state_ref.at[0], sems.at[1]),
        pltpu.make_async_copy(state_hbm.at[:, pl.ds(0, 2)], state_ref.at[1], sems.at[2]),
    ]
    for c in copies:
        c.start()
    chunks = field_ref.shape[2] // CHUNK
    copies[0].wait()
    tiles = []
    for q in range(chunks):
        for m in range(MEM):
            tiles.append(field_ref[m, :, q * CHUNK : (q + 1) * CHUNK].astype(F32)[None])
    rows = jnp.transpose(jnp.concatenate(tiles, axis=0), (1, 0, 2)).astype(BF)
    own_ref[...] = rows
    last = (chunks - 1) * MEM
    for c in copies[1:]:
        c.wait()
    for k, out in enumerate((right_ref, left_ref)):
        for r in range(2):
            for j in range(2):
                out[r, j * MEM : (j + 1) * MEM, : 2 * HALF] = state_ref[k, r, j]
        for d in range(8):
            at, lane = (d % 2) * MEM, (d // 2 % 2) * HALF
            out[2 + d // 4, at : at + MEM, lane : lane + HALF] = rows[d, last:, CHUNK - HALF :] if k == 0 else rows[d, :MEM, :HALF]
    for slot in range(slots):
        low = row_of(slot, row_ref) == 0
        dright_ref, edge_ref, dleft_ref = rest[3 * slot : 3 * slot + 3]
        for k in range(2):
            row = jnp.where(low, rows[k], rows[6 + k])
            edge_ref[k] = row
            dright_ref[k * MEM : (k + 1) * MEM, :HALF] = row[last:, CHUNK - HALF :]
            dleft_ref[k * MEM : (k + 1) * MEM] = row[:MEM, :HALF]


def own_kernel(slot, row_ref, state_ref, *rest):
    r = row_of(slot, row_ref)
    rows = [state_ref[r, 4 * q + res].astype(F32) for res in range(4) for q in range(state_ref.shape[1] // 4)]
    rest[-1][...] = jnp.concatenate(rows, axis=0).astype(BF)


def pack(row, out_ref, k):
    last = row.shape[0] - MEM
    out_ref[k, :, :CHUNK] = row[MEM:last].astype(BF)
    half = NEAR // 2
    ends = [row[:MEM, CHUNK - NEAR : CHUNK - half], row[:MEM, CHUNK - half :], row[last:, :half], row[last:, half:NEAR]]
    out_ref[k, :, CHUNK:] = jnp.concatenate(ends, axis=0).astype(BF)


def unpack(msg):
    x = msg.astype(F32)
    own, ends = x[:, :CHUNK], x[:, CHUNK:]
    fill = jnp.zeros((MEM, CHUNK - 2 * ends.shape[1]), F32)
    before = jnp.concatenate([fill, ends[:MEM], ends[MEM : 2 * MEM]], axis=1)
    after = jnp.concatenate([ends[2 * MEM : 3 * MEM], ends[3 * MEM :], fill], axis=1)
    return jnp.concatenate([before, own, after], axis=0)


def windows(lats, narrow):
    parts = [[] for _ in range(4)]
    side = 2 * VARS
    for a in lats:
        rows = a.shape[0]
        before = jnp.concatenate([a[rows - MEM :, CHUNK - side :], a[: rows - MEM, CHUNK - side :]], axis=0)
        after = jnp.concatenate([a[MEM:, :side], a[:MEM, :side]], axis=0)
        parts[0] += [before, a[:, : 3 * side]]
        parts[1].append(a[:, side : 5 * side])
        parts[2].append(a[:, 3 * side : 7 * side])
        parts[3] += [a[:, 5 * side :], after]
    if narrow:
        parts = [[x[MEM : x.shape[0] - MEM] for x in p] for p in parts]
    return jnp.concatenate([jnp.concatenate(p, axis=1) for p in parts], axis=0).astype(BF)


def latitude(pred, d):
    per = pred.shape[0] // 4
    return jnp.concatenate([pred[res * per : (res + 1) * per, d * CELL : (d + 1) * CELL] for res in range(4)], axis=1)


def of_band(band, values, *at):
    got = values[(0, *at)]
    for g in range(1, values.shape[0]):
        got = jnp.where(band == g, values[(g, *at)], got)
    return got


def block_at(index, ref):
    return pl.multiple_of(jnp.clip(index, 0, ref.shape[1] // BLK - 1) * BLK, BLK)


def block_pre(b, band, s_ref, in_ref, cidx, iidx, coup_ref, inp_ref):
    pieces = []
    mats = [coup_ref[band, (2 * b + k) * BLK : (2 * b + k + 1) * BLK, :] for k in range(2)]
    mats.append(inp_ref[band, b * BLK : (b + 1) * BLK, :])
    for k in range(2):
        pieces.append(s_ref[:, pl.ds(block_at(of_band(band, cidx, k, b), s_ref), BLK)])
    pieces.append(in_ref[:, pl.ds(block_at(of_band(band, iidx, b), in_ref), BLK)])
    return lax.dot_general(jnp.concatenate(pieces, axis=1), jnp.concatenate(mats, axis=1), NT, preferred_element_type=F32)


def half_of(r, rest_lats):
    return pl.ds(pl.multiple_of((1 - r if rest_lats else r) * 2 * CELL, 2 * CELL), 2 * CELL)


def send_edge(r, state, read_ref, msg_ref, edge_ref, s_ref):
    s_ref[...] = state
    pred = lax.dot_general(state, read_ref[half_of(r, False), :], NT, preferred_element_type=F32)
    for d in range(2):
        row = latitude(pred, d)
        pack(row, msg_ref, d)
        edge_ref[d] = row.astype(BF)


def first_kernel(slot, edge, behind, row_ref, band_ref, cidx_ref, iidx_ref, coup_ref, inp_ref, read_ref, own_ref, s0_ref, fl_ref, *rest):
    rest = list(rest)
    r = row_of(slot, row_ref)
    if edge:
        dl_ref, lat_ref, fr_ref, dr_ref = rest[:4]
        del rest[: 4 + behind]
    else:
        fr_ref = rest[1]
        del rest[:2]
    outs, (xs_ref, s_ref, in_ref) = rest[:-3], rest[-3:]
    fill = jnp.zeros((MEM, CHUNK - HALF), F32)

    def widen(own, left, right):
        left = jnp.concatenate([fill, left.astype(F32)], axis=1)
        right = jnp.concatenate([right.astype(F32), fill], axis=1)
        return jnp.concatenate([left, own.astype(F32), right], axis=0)

    for d in range(8):
        at, lane = (d % 2) * MEM, (d // 2 % 2) * HALF
        left = fl_ref[2 + d // 4, at : at + MEM, lane : lane + HALF]
        right = fr_ref[2 + d // 4, at : at + MEM, lane : lane + HALF]
        xs_ref[2 + d] = widen(own_ref[d], left, right)
    for k in range(2):
        at = k * MEM
        if edge:
            xs_ref[10 * r + k] = widen(lat_ref[k], dl_ref[at : at + MEM, :HALF], dr_ref[at : at + MEM])
        else:
            xs_ref[10 * r + k] = jnp.zeros(xs_ref.shape[1:], F32)
    empty = jnp.zeros((MEM, s0_ref.shape[1]), F32)
    per = s0_ref.shape[0] // 4
    rows = []
    for res in range(4):
        rows.append(fl_ref[r, (res - 2) * MEM : (res - 1) * MEM, : 2 * HALF].astype(F32) if res >= 2 else empty)
        rows.append(s0_ref[res * per : (res + 1) * per].astype(F32))
        rows.append(fr_ref[r, res * MEM : (res + 1) * MEM].astype(F32) if res < 2 else empty)
    s_ref[...] = jnp.concatenate(rows, axis=0).astype(BF)
    in_ref[...] = windows([xs_ref[4 * r + d] for d in range(8)], False)
    bands, cidx, iidx = band_ref[...], cidx_ref[...], iidx_ref[...]
    band = jnp.where(r == 0, bands[0], bands[1])
    pres = [block_pre(b, band, s_ref, in_ref, cidx, iidx, coup_ref, inp_ref) for b in range(iidx_ref.shape[1])]
    state = jnp.concatenate([jnp.tanh(p).astype(BF) for p in pres], axis=1)
    if edge:
        send_edge(r, state, read_ref, *outs)
        return
    outs[1][...] = state
    pred = lax.dot_general(state, read_ref[...], NT, preferred_element_type=F32)
    for d in range(4):
        outs[0][d] = latitude(pred, d).astype(BF)


def narrowed(s):
    per = s.shape[0] // 4
    return jnp.concatenate([s[res * per + MEM : (res + 1) * per - MEM] for res in range(4)], axis=0)


def shadow_kernel(last, slots, row_ref, band_ref, cidx_ref, iidx_ref, coup_ref, inp_ref, read_ref, *rest):
    rest = list(rest)

    def take(n):
        got = rest[:n]
        del rest[:n]
        return got

    edge_refs, s_refs = take(slots), take(slots)
    far_refs = take(2 * (2 - slots))
    pre_refs = take(slots)
    out_far = take(2 * (2 - slots))
    xs_ref, in_ref = take(2)
    rows_at = [row_of(0, row_ref), row_of(1, row_ref)]
    for k in range(2):
        xs_ref[k] = jnp.zeros(xs_ref.shape[1:], F32)
        xs_ref[10 + k] = jnp.zeros(xs_ref.shape[1:], F32)
    for slot in range(slots):
        r = rows_at[slot]
        pred = lax.dot_general(s_refs[slot][...], read_ref[half_of(r, True), :], NT, preferred_element_type=F32)
        for d in range(2):
            xs_ref[2 + 4 * r + 2 * r + d] = edge_refs[slot][d].astype(F32)
            xs_ref[2 + 4 * r + 2 * (1 - r) + d] = latitude(pred, d).astype(BF).astype(F32)
    if far_refs:
        for d in range(4):
            xs_ref[2 + 4 * rows_at[1] + d] = far_refs[0][d].astype(F32)
        s_refs = [s_refs[0], far_refs[1]]
    if last:
        short_refs = take(2)
        for slot in range(2):
            short_refs[slot][...] = narrowed(s_refs[slot][...].astype(F32)).astype(BF)
        s_refs = short_refs

    bands, cidx, iidx = band_ref[...], cidx_ref[...], iidx_ref[...]
    copy = None
    for slot in (1, 0):
        r = rows_at[slot]
        band = jnp.where(r == 0, bands[0], bands[1])
        in_ref[...] = windows([xs_ref[4 * r + d] for d in range(8)], last)
        blocks = iidx_ref.shape[1]
        pres = [block_pre(b, band, s_refs[slot], in_ref, cidx, iidx, coup_ref, inp_ref) for b in range(blocks)]
        if slot < slots:
            for b in range(blocks):
                pre_refs[slot][:, b * BLK : (b + 1) * BLK] = pres[b]
            continue
        state = jnp.concatenate([jnp.tanh(p).astype(BF) for p in pres], axis=1)
        if last:
            stage_ref, sem = take(2)
            copy = put_states(r, state, stage_ref, out_far[1], sem)
        else:
            out_far[1][...] = state
        pred = lax.dot_general(state, read_ref[...], NT, preferred_element_type=F32)
        for d in range(4):
            out_far[0][d] = latitude(pred, d).astype(BF)
    if copy is not None:
        copy.wait()


def put_states(r, state, stage_ref, states_hbm, sem):
    per = state.shape[0] // 4
    for res in range(4):
        for q in range(per // MEM):
            at = res * per + q * MEM
            stage_ref[4 * q + res] = state[at : at + MEM]
    copy = pltpu.make_async_copy(stage_ref, states_hbm.at[r], sem)
    copy.start()
    return copy


def late_kernel(slot, last, final, row_ref, band_ref, iidx_ref, inp_ref, read_ref, pre_ref, got_ref, *rest):
    r = row_of(slot, row_ref)
    bands, iidx = band_ref[...], iidx_ref[...]
    band = jnp.where(r == 0, bands[0], bands[1])
    in_ref = rest[-1]
    in_ref[...] = windows([unpack(got_ref[k]) for k in range(2)], last)
    parts = []
    for b in range(iidx_ref.shape[1]):
        k = of_band(band, iidx, b) - 15 * r
        used = jnp.logical_and(k >= 0, k < 5)
        at = pl.multiple_of(jnp.where(used, k, 0) * BLK, BLK)
        term = lax.dot_general(in_ref[:, pl.ds(at, BLK)], inp_ref[band, b * BLK : (b + 1) * BLK, :], NT, preferred_element_type=F32)
        pre = pre_ref[:, b * BLK : (b + 1) * BLK] + jnp.where(used, term, 0.0)
        parts.append(jnp.tanh(pre).astype(BF))
    state = jnp.concatenate(parts, axis=1)
    if not last:
        send_edge(r, state, read_ref, *rest[:3])
        return
    if not final:
        lats_ref, states_hbm, stage_ref, sem = rest[:4]
    else:
        other_ref, _, field_hbm, states_hbm, stage_ref, sem, field_ref, field_sem = rest[:8]
    copy = put_states(r, state, stage_ref, states_hbm, sem)
    pred = lax.dot_general(state, read_ref[...], NT, preferred_element_type=F32)
    mine = [latitude(pred, d) for d in range(4)]
    if not final:
        for d in range(4):
            lats_ref[d] = mine[d].astype(BF)
        copy.wait()
        return
    other = [other_ref[d].astype(F32) for d in range(4)]
    low = r == 0
    rows = [jnp.where(low, mine[d], other[d])[None] for d in range(4)]
    rows += [jnp.where(low, other[d], mine[d])[None] for d in range(4)]
    tiles = jnp.transpose(jnp.concatenate(rows, axis=0), (1, 0, 2)).astype(BF)
    for q in range(field_ref.shape[2] // CHUNK):
        for m in range(MEM):
            field_ref[m, :, q * CHUNK : (q + 1) * CHUNK] = tiles[q * MEM + m]
    out = pltpu.make_async_copy(field_ref, field_hbm, field_sem)
    out.start()
    copy.wait()
    out.wait()


def call(kernel, out_shape, out_specs, scratch, operands, flops=0, aliases=None):
    arrays = [pltpu.with_memory_space_constraint(x, pltpu.HBM) if s is HB else x for x, s in operands]
    size = sum(x.size * x.dtype.itemsize for x, _ in operands)
    return pl.pallas_call(
        kernel,
        out_shape=out_shape,
        in_specs=[s for _, s in operands],
        out_specs=out_specs,
        scratch_shapes=scratch,
        input_output_aliases=aliases or {},
        compiler_params=pltpu.CompilerParams(vmem_limit_bytes=40 * 1024 * 1024),
        cost_estimate=pl.CostEstimate(flops=flops, bytes_accessed=size, transcendentals=0),
    )(*arrays)


def per_device(field_state, reservoir_state, coupling_blocks, coupling_index, input_blocks, input_index, readout, region_band):
    lat_count, lon_count = lax.axis_size("lat"), lax.axis_size("lon")
    lat_at = lax.axis_index("lat").astype(jnp.int32)
    region_rows, regions, members, units = reservoir_state.shape
    outs = readout.shape[1]
    assert region_rows == 2 and members == MEM and regions % 4 == 0
    chunks = regions // 4
    own_rows = chunks * MEM
    wide = own_rows + 2 * MEM
    rows = 4 * wide
    short = 4 * own_rows
    swap = lat_count == 2
    slots = 1 if swap else 2

    def bf(*dims):
        return jax.ShapeDtypeStruct(dims, BF)

    def vm(dims, dtype=BF):
        return pltpu.VMEM(dims, dtype)

    def send(x, lat_step, lon_step):
        pairs = []
        for i in range(lat_count):
            to = 1 - i if swap and lat_step else i + lat_step
            if 0 <= to < lat_count:
                for j in range(lon_count):
                    pairs.append((i * lon_count + j, to * lon_count + (j + lon_step) % lon_count))
        return lax.ppermute(x, ("lat", "lon"), pairs)

    def across(xs, lon_step=0):
        if swap:
            return [send(xs[0], 1, lon_step)]
        return [send(xs[1], 1, lon_step), send(xs[0], -1, lon_step)]

    row = ((1 - lat_at if swap else lat_at * 0).reshape(1), SM)
    small = [(region_band, VM), (coupling_index.transpose(0, 2, 1), VM), (input_index, VM)]
    band, _, iidx = small
    flops = 2 * rows * units * (3 * BLK + outs)

    mail = call(
        functools.partial(message_kernel, slots),
        [bf(4, 2 * MEM, 2 * HALF)] * 2 + [bf(8, own_rows, CHUNK)] + [bf(2 * MEM, 1536), bf(2, own_rows, CHUNK), bf(2 * MEM, HALF)] * slots,
        [VM] * (3 + 3 * slots),
        [vm(field_state.shape), vm((2, region_rows, 2, MEM, units)), pltpu.SemaphoreType.DMA((3,))],
        [row, (field_state, HB), (reservoir_state, HB)],
        AHEAD,
    )
    from_left = send(mail[0], 0, 1)
    from_dleft = across(mail[3::3], 1)
    from_lat = across(mail[4::3])
    from_right = send(mail[1], 0, -1)
    from_dright = across(mail[5::3], -1)
    own = (mail[2], VM)
    waits = [from_left] + from_dleft
    s0s1 = []
    for slot in range(2):
        operands = [row, (reservoir_state, VM)] + [(x, VM) for x in waits]
        s0s1.append(call(functools.partial(own_kernel, slot), bf(short, units), VM, [], operands, ORDER[slot]))
        waits = from_lat + s0s1
    s0, s1 = s0s1
    weights = [(x, VM) for x in (coupling_blocks, input_blocks, readout[0])]
    states_shape = bf(region_rows, regions, MEM, units)
    stage = [vm((regions, MEM, units)), pltpu.SemaphoreType.DMA]
    padded = vm((12, wide, CHUNK), F32)
    send_out = [bf(2, own_rows, CHUNK + NEAR // 2), bf(2, wide, CHUNK), bf(rows, units)]

    sent, edges, states, far = [None] * slots, [None] * slots, [None] * slots, []
    for slot in (1, 0):
        edge = slot < slots
        operands = [row] + small + weights + [own, ((s0, s1)[slot], VM), (from_left, VM)]
        if edge:
            operands.append((from_dleft[slot], VM))
        operands.append((from_lat[slot if edge else 0], VM))
        operands.append((from_right, VM))
        if edge:
            operands.append((from_dright[slot], VM))
            operands += [(x, VM) for x in far[1:]]
        got = call(
            functools.partial(first_kernel, slot, edge, len(far[1:])),
            send_out if edge else [bf(4, wide, CHUNK), bf(rows, units)],
            [VM] * (3 if edge else 2),
            [padded, vm((rows, units)), vm((rows, 16 * CELL))],
            operands,
            flops if edge else 0,
        )
        if edge:
            sent[slot], edges[slot], states[slot] = got
        else:
            far = list(got)

    for step in range(1, STEPS):
        last = step == STEPS - 1
        got = across(sent)
        pre_rows = short if last else rows
        out = [jax.ShapeDtypeStruct((pre_rows, units), F32)] * slots
        specs = [VM] * slots
        scratch = [padded, vm((pre_rows, 16 * CELL))] + [vm((short, units))] * (2 if last else 0)
        if swap:
            out += [bf(4, own_rows if last else wide, CHUNK), states_shape if last else bf(rows, units)]
            specs += [VM, HB if last else VM]
            scratch += stage if last else []
        shadow = call(
            functools.partial(shadow_kernel, last, slots),
            out,
            specs,
            scratch,
            [row] + small + weights + [(x, VM) for x in edges + states + far],
            2 * flops,
        )
        far = list(shadow[slots:])
        for slot in reversed(range(slots)):
            operands = [row, band, iidx] + weights[1:] + [(shadow[slot], VM), (got[slot], VM)]
            inputs = [vm((pre_rows, 4 * CELL))]
            if not last:
                sent[slot], edges[slot], states[slot] = call(
                    functools.partial(late_kernel, slot, False, False), send_out, [VM] * 3, inputs, operands, flops
                )
            elif slot == 1:
                far = call(
                    functools.partial(late_kernel, slot, True, False),
                    [bf(4, own_rows, CHUNK), states_shape],
                    [VM, HB],
                    stage + inputs,
                    operands,
                    flops,
                )
            else:
                return call(
                    functools.partial(late_kernel, slot, True, True),
                    [bf(MEM, 8, regions * CELL), states_shape],
                    [HB, HB],
                    stage + [vm((MEM, 8, regions * CELL)), pltpu.SemaphoreType.DMA] + inputs,
                    operands + [(far[0], VM), (far[1], HB)],
                    flops,
                    {len(operands) + 1: 1},
                )


def solution(mesh):
    return jax.shard_map(
        per_device,
        mesh=mesh,
        in_specs=(
            P(None, "lat", "lon"),
            P("lat", "lon", None, None),
            P("lat", None, None),
            P("lat", None, None),
            P("lat", None, None),
            P("lat", None),
            P("lat", None, None),
            P("lat"),
        ),
        out_specs=(P(None, "lat", "lon"), P("lat", "lon", None, None)),
        check_vma=False,
    )
```

```python
import functools

import jax
import jax.numpy as jnp
from jax import lax
from jax.experimental import pallas as pl
from jax.experimental.pallas import tpu as pltpu
from jax.sharding import PartitionSpec as P

VARS = 40
STEPS = 3
CELL = 4 * VARS
CHUNK = 4 * CELL
HALF = 512
NEAR = 256
MEM = 4
BLK = 128
AHEAD = 10**10
ORDER = (3 * 10**8, 3 * 10**8)
BF = jnp.bfloat16
F32 = jnp.float32
VM = pl.BlockSpec(memory_space=pltpu.VMEM)
SM = pl.BlockSpec(memory_space=pltpu.SMEM)
HB = pl.BlockSpec(memory_space=pltpu.HBM)
NT = (((1,), (1,)), ((), ()))


def row_of(slot, row_ref):
    return row_ref[0] if slot == 0 else 1 - row_ref[0]


def message_kernel(slots, row_ref, field_hbm, state_hbm, right_ref, left_ref, own_ref, *rest):
    field_ref, state_ref, sems = rest[3 * slots :]
    regions = state_hbm.shape[1]
    copies = [
        pltpu.make_async_copy(field_hbm, field_ref, sems.at[0]),
        pltpu.make_async_copy(state_hbm.at[:, pl.ds(regions - 2, 2)], state_ref.at[0], sems.at[1]),
        pltpu.make_async_copy(state_hbm.at[:, pl.ds(0, 2)], state_ref.at[1], sems.at[2]),
    ]
    for c in copies:
        c.start()
    chunks = field_ref.shape[2] // CHUNK
    copies[0].wait()
    tiles = []
    for q in range(chunks):
        for m in range(MEM):
            tiles.append(field_ref[m, :, q * CHUNK : (q + 1) * CHUNK].astype(F32)[None])
    rows = jnp.transpose(jnp.concatenate(tiles, axis=0), (1, 0, 2)).astype(BF)
    own_ref[...] = rows
    last = (chunks - 1) * MEM
    for c in copies[1:]:
        c.wait()
    for k, out in enumerate((right_ref, left_ref)):
        for r in range(2):
            for j in range(2):
                out[r, j * MEM : (j + 1) * MEM, : 2 * HALF] = state_ref[k, r, j]
        for d in range(8):
            at, lane = (d % 2) * MEM, (d // 2 % 2) * HALF
            out[2 + d // 4, at : at + MEM, lane : lane + HALF] = rows[d, last:, CHUNK - HALF :] if k == 0 else rows[d, :MEM, :HALF]
    for slot in range(slots):
        low = row_of(slot, row_ref) == 0
        dright_ref, edge_ref, dleft_ref = rest[3 * slot : 3 * slot + 3]
        for k in range(2):
            row = jnp.where(low, rows[k], rows[6 + k])
            edge_ref[k] = row
            dright_ref[k * MEM : (k + 1) * MEM, :HALF] = row[last:, CHUNK - HALF :]
            dleft_ref[k * MEM : (k + 1) * MEM] = row[:MEM, :HALF]


def own_kernel(slot, row_ref, state_ref, band_ref, cidx_ref, iidx_ref, *rest):
    s_ref, code_ref = rest[-2:]
    r = row_of(slot, row_ref)
    rows = [state_ref[r, 4 * q + res].astype(F32) for res in range(4) for q in range(state_ref.shape[1] // 4)]
    s_ref[...] = jnp.concatenate(rows, axis=0).astype(BF)
    bands = band_ref[...]
    band = jnp.where(r == 0, bands[0], bands[1])

    def chosen(values):
        got = values[0]
        for g in range(1, values.shape[0]):
            got = jnp.where(band == g, values[g], got)
        return got.astype(F32)

    blocks = iidx_ref.shape[1]
    at = lax.broadcasted_iota(jnp.int32, (1, blocks), 1)
    weights = [sum(jnp.where(at == b, 2.0 ** (3 * b), 0.0) for b in range(blocks))]
    for half in range(2):
        weights.append(sum(jnp.where(at == b, 2.0 ** (5 * (b % 4)), 0.0) for b in range(4 * half, 4 * half + 4)))
    columns, inputs = chosen(cidx_ref[...]), chosen(iidx_ref[...])
    words = [jnp.sum(columns[k : k + 1] * weights[0]) for k in range(2)]
    words += [jnp.sum(inputs.reshape(1, blocks) * weights[1 + half]) for half in range(2)]
    lane = lax.broadcasted_iota(jnp.int32, code_ref.shape, 1)
    code = jnp.where(lane == 0, band.astype(F32), 0.0)
    for k, word in enumerate(words):
        code = jnp.where(lane == k + 1, word, code)
    code_ref[...] = code.astype(jnp.int32)


def decode(code_ref):
    code = code_ref[...]
    band, columns, inputs = code[0, 0], [code[0, 1 + k] for k in range(2)], [code[0, 3 + k] for k in range(2)]

    def column(k, b):
        return (columns[k] >> (3 * b)) & 7

    def source(b):
        return (inputs[b // 4] >> (5 * (b % 4))) & 31

    return band, column, source


def pack(row, out_ref, k):
    last = row.shape[0] - MEM
    out_ref[k, :, :CHUNK] = row[MEM:last].astype(BF)
    half = NEAR // 2
    ends = [row[:MEM, CHUNK - NEAR : CHUNK - half], row[:MEM, CHUNK - half :], row[last:, :half], row[last:, half:NEAR]]
    out_ref[k, :, CHUNK:] = jnp.concatenate(ends, axis=0).astype(BF)


def unpack(msg):
    x = msg.astype(F32)
    own, ends = x[:, :CHUNK], x[:, CHUNK:]
    fill = jnp.zeros((MEM, CHUNK - 2 * ends.shape[1]), F32)
    before = jnp.concatenate([fill, ends[:MEM], ends[MEM : 2 * MEM]], axis=1)
    after = jnp.concatenate([ends[2 * MEM : 3 * MEM], ends[3 * MEM :], fill], axis=1)
    return jnp.concatenate([before, own, after], axis=0)


def windows(lats, narrow):
    parts = [[] for _ in range(4)]
    side = 2 * VARS
    for a in lats:
        rows = a.shape[0]
        before = jnp.concatenate([a[rows - MEM :, CHUNK - side :], a[: rows - MEM, CHUNK - side :]], axis=0)
        after = jnp.concatenate([a[MEM:, :side], a[:MEM, :side]], axis=0)
        parts[0] += [before, a[:, : 3 * side]]
        parts[1].append(a[:, side : 5 * side])
        parts[2].append(a[:, 3 * side : 7 * side])
        parts[3] += [a[:, 5 * side :], after]
    if narrow:
        parts = [[x[MEM : x.shape[0] - MEM] for x in p] for p in parts]
    return jnp.concatenate([jnp.concatenate(p, axis=1) for p in parts], axis=0).astype(BF)


def latitude(pred, d):
    per = pred.shape[0] // 4
    return jnp.concatenate([pred[res * per : (res + 1) * per, d * CELL : (d + 1) * CELL] for res in range(4)], axis=1)


def block_at(index, ref):
    return pl.multiple_of(jnp.clip(index, 0, ref.shape[1] // BLK - 1) * BLK, BLK)


def block_pre(b, codes, s_ref, in_ref, coup_ref, inp_ref):
    band, column, source = codes
    pieces = []
    mats = [coup_ref[band, (2 * b + k) * BLK : (2 * b + k + 1) * BLK, :] for k in range(2)]
    mats.append(inp_ref[band, b * BLK : (b + 1) * BLK, :])
    for k in range(2):
        pieces.append(s_ref[:, pl.ds(block_at(column(k, b), s_ref), BLK)])
    pieces.append(in_ref[:, pl.ds(block_at(source(b), in_ref), BLK)])
    return lax.dot_general(jnp.concatenate(pieces, axis=1), jnp.concatenate(mats, axis=1), NT, preferred_element_type=F32)


def half_of(r, rest_lats):
    return pl.ds(pl.multiple_of((1 - r if rest_lats else r) * 2 * CELL, 2 * CELL), 2 * CELL)


def send_edge(r, state, read_ref, msg_ref, edge_ref, s_ref):
    s_ref[...] = state
    pred = lax.dot_general(state, read_ref[half_of(r, False), :], NT, preferred_element_type=F32)
    for d in range(2):
        row = latitude(pred, d)
        pack(row, msg_ref, d)
        edge_ref[d] = row.astype(BF)


def first_kernel(slot, edge, behind, row_ref, code_ref, coup_ref, inp_ref, read_ref, own_ref, s0_ref, fl_ref, *rest):
    rest = list(rest)
    r = row_of(slot, row_ref)
    if edge:
        dl_ref, lat_ref, fr_ref, dr_ref = rest[:4]
        del rest[: 4 + behind]
    else:
        fr_ref = rest[1]
        del rest[:2]
    outs, (xs_ref, s_ref, in_ref) = rest[:-3], rest[-3:]
    fill = jnp.zeros((MEM, CHUNK - HALF), F32)

    def widen(own, left, right):
        left = jnp.concatenate([fill, left.astype(F32)], axis=1)
        right = jnp.concatenate([right.astype(F32), fill], axis=1)
        return jnp.concatenate([left, own.astype(F32), right], axis=0)

    for d in range(8):
        at, lane = (d % 2) * MEM, (d // 2 % 2) * HALF
        left = fl_ref[2 + d // 4, at : at + MEM, lane : lane + HALF]
        right = fr_ref[2 + d // 4, at : at + MEM, lane : lane + HALF]
        xs_ref[2 + d] = widen(own_ref[d], left, right)
    for k in range(2):
        at = k * MEM
        if edge:
            xs_ref[10 * r + k] = widen(lat_ref[k], dl_ref[at : at + MEM, :HALF], dr_ref[at : at + MEM])
        else:
            xs_ref[10 * r + k] = jnp.zeros(xs_ref.shape[1:], F32)
    empty = jnp.zeros((MEM, s0_ref.shape[1]), F32)
    per = s0_ref.shape[0] // 4
    rows = []
    for res in range(4):
        rows.append(fl_ref[r, (res - 2) * MEM : (res - 1) * MEM, : 2 * HALF].astype(F32) if res >= 2 else empty)
        rows.append(s0_ref[res * per : (res + 1) * per].astype(F32))
        rows.append(fr_ref[r, res * MEM : (res + 1) * MEM].astype(F32) if res < 2 else empty)
    s_ref[...] = jnp.concatenate(rows, axis=0).astype(BF)
    in_ref[...] = windows([xs_ref[4 * r + d] for d in range(8)], False)
    codes = decode(code_ref)
    pres = [block_pre(b, codes, s_ref, in_ref, coup_ref, inp_ref) for b in range(s_ref.shape[1] // BLK)]
    state = jnp.concatenate([jnp.tanh(p).astype(BF) for p in pres], axis=1)
    if edge:
        send_edge(r, state, read_ref, *outs)
        return
    outs[1][...] = state
    pred = lax.dot_general(state, read_ref[...], NT, preferred_element_type=F32)
    for d in range(4):
        outs[0][d] = latitude(pred, d).astype(BF)


def narrowed(s):
    per = s.shape[0] // 4
    return jnp.concatenate([s[res * per + MEM : (res + 1) * per - MEM] for res in range(4)], axis=0)


def shadow_kernel(last, slots, row_ref, code0_ref, code1_ref, coup_ref, inp_ref, read_ref, *rest):
    rest = list(rest)

    def take(n):
        got = rest[:n]
        del rest[:n]
        return got

    edge_refs, s_refs = take(slots), take(slots)
    far_refs = take(2 * (2 - slots))
    pre_refs = take(slots)
    out_far = take(2 * (2 - slots))
    xs_ref, in_ref = take(2)
    rows_at = [row_of(0, row_ref), row_of(1, row_ref)]
    for k in range(2):
        xs_ref[k] = jnp.zeros(xs_ref.shape[1:], F32)
        xs_ref[10 + k] = jnp.zeros(xs_ref.shape[1:], F32)
    for slot in range(slots):
        r = rows_at[slot]
        pred = lax.dot_general(s_refs[slot][...], read_ref[half_of(r, True), :], NT, preferred_element_type=F32)
        for d in range(2):
            xs_ref[2 + 4 * r + 2 * r + d] = edge_refs[slot][d].astype(F32)
            xs_ref[2 + 4 * r + 2 * (1 - r) + d] = latitude(pred, d).astype(BF).astype(F32)
    if far_refs:
        for d in range(4):
            xs_ref[2 + 4 * rows_at[1] + d] = far_refs[0][d].astype(F32)
        s_refs = [s_refs[0], far_refs[1]]
    if last:
        short_refs = take(2)
        for slot in range(2):
            short_refs[slot][...] = narrowed(s_refs[slot][...].astype(F32)).astype(BF)
        s_refs = short_refs

    copy = None
    for slot in (1, 0):
        r = rows_at[slot]
        codes = decode((code0_ref, code1_ref)[slot])
        in_ref[...] = windows([xs_ref[4 * r + d] for d in range(8)], last)
        blocks = s_refs[slot].shape[1] // BLK
        pres = [block_pre(b, codes, s_refs[slot], in_ref, coup_ref, inp_ref) for b in range(blocks)]
        if slot < slots:
            for b in range(blocks):
                pre_refs[slot][:, b * BLK : (b + 1) * BLK] = pres[b]
            continue
        state = jnp.concatenate([jnp.tanh(p).astype(BF) for p in pres], axis=1)
        if last:
            stage_ref, sem = take(2)
            copy = put_states(r, state, stage_ref, out_far[1], sem)
        else:
            out_far[1][...] = state
        pred = lax.dot_general(state, read_ref[...], NT, preferred_element_type=F32)
        for d in range(4):
            out_far[0][d] = latitude(pred, d).astype(BF)
    if copy is not None:
        copy.wait()


def put_states(r, state, stage_ref, states_hbm, sem):
    per = state.shape[0] // 4
    for res in range(4):
        for q in range(per // MEM):
            at = res * per + q * MEM
            stage_ref[4 * q + res] = state[at : at + MEM]
    copy = pltpu.make_async_copy(stage_ref, states_hbm.at[r], sem)
    copy.start()
    return copy


def late_kernel(slot, last, final, row_ref, code_ref, inp_ref, read_ref, pre_ref, got_ref, *rest):
    r = row_of(slot, row_ref)
    band, _, source = decode(code_ref)
    in_ref = rest[-1]
    in_ref[...] = windows([unpack(got_ref[k]) for k in range(2)], last)
    parts = []
    for b in range(pre_ref.shape[1] // BLK):
        k = source(b) - 15 * r
        used = jnp.logical_and(k >= 0, k < 5)
        at = pl.multiple_of(jnp.where(used, k, 0) * BLK, BLK)
        term = lax.dot_general(in_ref[:, pl.ds(at, BLK)], inp_ref[band, b * BLK : (b + 1) * BLK, :], NT, preferred_element_type=F32)
        pre = pre_ref[:, b * BLK : (b + 1) * BLK] + jnp.where(used, term, 0.0)
        parts.append(jnp.tanh(pre).astype(BF))
    state = jnp.concatenate(parts, axis=1)
    if not last:
        send_edge(r, state, read_ref, *rest[:3])
        return
    if not final:
        lats_ref, states_hbm, stage_ref, sem = rest[:4]
    else:
        other_ref, _, field_hbm, states_hbm, stage_ref, sem, field_ref, field_sem = rest[:8]
    copy = put_states(r, state, stage_ref, states_hbm, sem)
    pred = lax.dot_general(state, read_ref[...], NT, preferred_element_type=F32)
    mine = [latitude(pred, d) for d in range(4)]
    if not final:
        for d in range(4):
            lats_ref[d] = mine[d].astype(BF)
        copy.wait()
        return
    other = [other_ref[d].astype(F32) for d in range(4)]
    low = r == 0
    rows = [jnp.where(low, mine[d], other[d])[None] for d in range(4)]
    rows += [jnp.where(low, other[d], mine[d])[None] for d in range(4)]
    tiles = jnp.transpose(jnp.concatenate(rows, axis=0), (1, 0, 2)).astype(BF)
    for q in range(field_ref.shape[2] // CHUNK):
        for m in range(MEM):
            field_ref[m, :, q * CHUNK : (q + 1) * CHUNK] = tiles[q * MEM + m]
    out = pltpu.make_async_copy(field_ref, field_hbm, field_sem)
    out.start()
    copy.wait()
    out.wait()


def call(kernel, out_shape, out_specs, scratch, operands, flops=0, aliases=None):
    arrays = [pltpu.with_memory_space_constraint(x, pltpu.HBM) if s is HB else x for x, s in operands]
    size = sum(x.size * x.dtype.itemsize for x, _ in operands)
    return pl.pallas_call(
        kernel,
        out_shape=out_shape,
        in_specs=[s for _, s in operands],
        out_specs=out_specs,
        scratch_shapes=scratch,
        input_output_aliases=aliases or {},
        compiler_params=pltpu.CompilerParams(vmem_limit_bytes=40 * 1024 * 1024),
        cost_estimate=pl.CostEstimate(flops=flops, bytes_accessed=size, transcendentals=0),
    )(*arrays)


def per_device(field_state, reservoir_state, coupling_blocks, coupling_index, input_blocks, input_index, readout, region_band):
    lat_count, lon_count = lax.axis_size("lat"), lax.axis_size("lon")
    lat_at = lax.axis_index("lat").astype(jnp.int32)
    region_rows, regions, members, units = reservoir_state.shape
    outs = readout.shape[1]
    assert region_rows == 2 and members == MEM and regions % 4 == 0 and units == 8 * BLK
    chunks = regions // 4
    own_rows = chunks * MEM
    wide = own_rows + 2 * MEM
    rows = 4 * wide
    short = 4 * own_rows
    swap = lat_count == 2
    slots = 1 if swap else 2

    def bf(*dims):
        return jax.ShapeDtypeStruct(dims, BF)

    def vm(dims, dtype=BF):
        return pltpu.VMEM(dims, dtype)

    def send(x, lat_step, lon_step):
        pairs = []
        for i in range(lat_count):
            to = 1 - i if swap and lat_step else i + lat_step
            if 0 <= to < lat_count:
                for j in range(lon_count):
                    pairs.append((i * lon_count + j, to * lon_count + (j + lon_step) % lon_count))
        return lax.ppermute(x, ("lat", "lon"), pairs)

    def across(xs, lon_step=0):
        if swap:
            return [send(xs[0], 1, lon_step)]
        return [send(xs[1], 1, lon_step), send(xs[0], -1, lon_step)]

    row = ((1 - lat_at if swap else lat_at * 0).reshape(1), SM)
    small = [(region_band, VM), (coupling_index.transpose(0, 2, 1), VM), (input_index, VM)]
    flops = 2 * rows * units * (3 * BLK + outs)

    mail = call(
        functools.partial(message_kernel, slots),
        [bf(4, 2 * MEM, 2 * HALF)] * 2 + [bf(8, own_rows, CHUNK)] + [bf(2 * MEM, 1536), bf(2, own_rows, CHUNK), bf(2 * MEM, HALF)] * slots,
        [VM] * (3 + 3 * slots),
        [vm(field_state.shape), vm((2, region_rows, 2, MEM, units)), pltpu.SemaphoreType.DMA((3,))],
        [row, (field_state, HB), (reservoir_state, HB)],
        AHEAD,
    )
    from_left = send(mail[0], 0, 1)
    from_dleft = across(mail[3::3], 1)
    from_lat = across(mail[4::3])
    from_right = send(mail[1], 0, -1)
    from_dright = across(mail[5::3], -1)
    own = (mail[2], VM)
    waits = [from_left] + from_dleft
    s0s1 = []
    for slot in range(2):
        operands = [row, (reservoir_state, VM)] + small + [(x, VM) for x in waits]
        words = jax.ShapeDtypeStruct((8, BLK), jnp.int32)
        s0s1.append(call(functools.partial(own_kernel, slot), [bf(short, units), words], [VM] * 2, [], operands, ORDER[slot]))
        waits = from_lat + [s0s1[-1][0]]
    (s0, code0), (s1, code1) = s0s1
    codes = [(code0, VM), (code1, VM)]
    weights = [(x, VM) for x in (coupling_blocks, input_blocks, readout[0])]
    states_shape = bf(region_rows, regions, MEM, units)
    stage = [vm((regions, MEM, units)), pltpu.SemaphoreType.DMA]
    padded = vm((12, wide, CHUNK), F32)
    send_out = [bf(2, own_rows, CHUNK + NEAR // 2), bf(2, wide, CHUNK), bf(rows, units)]

    sent, edges, states, far = [None] * slots, [None] * slots, [None] * slots, []
    for slot in (1, 0):
        edge = slot < slots
        operands = [row, codes[slot]] + weights + [own, ((s0, s1)[slot], VM), (from_left, VM)]
        if edge:
            operands.append((from_dleft[slot], VM))
        operands.append((from_lat[slot if edge else 0], VM))
        operands.append((from_right, VM))
        if edge:
            operands.append((from_dright[slot], VM))
            operands += [(x, VM) for x in far[1:]]
        got = call(
            functools.partial(first_kernel, slot, edge, len(far[1:])),
            send_out if edge else [bf(4, wide, CHUNK), bf(rows, units)],
            [VM] * (3 if edge else 2),
            [padded, vm((rows, units)), vm((rows, 16 * CELL))],
            operands,
            flops if edge else 0,
        )
        if edge:
            sent[slot], edges[slot], states[slot] = got
        else:
            far = list(got)

    for step in range(1, STEPS):
        last = step == STEPS - 1
        got = across(sent)
        pre_rows = short if last else rows
        out = [jax.ShapeDtypeStruct((pre_rows, units), F32)] * slots
        specs = [VM] * slots
        scratch = [padded, vm((pre_rows, 16 * CELL))] + [vm((short, units))] * (2 if last else 0)
        if swap:
            out += [bf(4, own_rows if last else wide, CHUNK), states_shape if last else bf(rows, units)]
            specs += [VM, HB if last else VM]
            scratch += stage if last else []
        shadow = call(
            functools.partial(shadow_kernel, last, slots),
            out,
            specs,
            scratch,
            [row] + codes + weights + [(x, VM) for x in edges + states + far],
            2 * flops,
        )
        far = list(shadow[slots:])
        for slot in reversed(range(slots)):
            operands = [row, codes[slot]] + weights[1:] + [(shadow[slot], VM), (got[slot], VM)]
            inputs = [vm((pre_rows, 4 * CELL))]
            if not last:
                sent[slot], edges[slot], states[slot] = call(
                    functools.partial(late_kernel, slot, False, False), send_out, [VM] * 3, inputs, operands, flops
                )
            elif slot == 1:
                far = call(
                    functools.partial(late_kernel, slot, True, False),
                    [bf(4, own_rows, CHUNK), states_shape],
                    [VM, HB],
                    stage + inputs,
                    operands,
                    flops,
                )
            else:
                return call(
                    functools.partial(late_kernel, slot, True, True),
                    [bf(MEM, 8, regions * CELL), states_shape],
                    [HB, HB],
                    stage + [vm((MEM, 8, regions * CELL)), pltpu.SemaphoreType.DMA] + inputs,
                    operands + [(far[0], VM), (far[1], HB)],
                    flops,
                    {len(operands) + 1: 1},
                )


def solution(mesh):
    return jax.shard_map(
        per_device,
        mesh=mesh,
        in_specs=(
            P(None, "lat", "lon"),
            P("lat", "lon", None, None),
            P("lat", None, None),
            P("lat", None, None),
            P("lat", None, None),
            P("lat", None),
            P("lat", None, None),
            P("lat"),
        ),
        out_specs=(P(None, "lat", "lon"), P("lat", "lon", None, None)),
        check_vma=False,
    )
```

```python
import functools

import jax
import jax.numpy as jnp
from jax import lax
from jax.experimental import pallas as pl
from jax.experimental.pallas import tpu as pltpu
from jax.sharding import PartitionSpec as P

VARS = 40
STEPS = 3
CELL = 4 * VARS
CHUNK = 4 * CELL
HALF = 512
NEAR = 256
MEM = 4
BLK = 128
AHEAD = 10**10
ORDER = (3 * 10**8, 3 * 10**8)
BF = jnp.bfloat16
F32 = jnp.float32
VM = pl.BlockSpec(memory_space=pltpu.VMEM)
SM = pl.BlockSpec(memory_space=pltpu.SMEM)
HB = pl.BlockSpec(memory_space=pltpu.HBM)
NT = (((1,), (1,)), ((), ()))


def row_of(slot, row_ref):
    return row_ref[0] if slot == 0 else 1 - row_ref[0]


def message_kernel(slots, row_ref, field_hbm, state_hbm, right_ref, left_ref, own_ref, *rest):
    field_ref, state_ref, sems = rest[3 * slots :]
    regions = state_hbm.shape[1]
    copies = [
        pltpu.make_async_copy(field_hbm, field_ref, sems.at[0]),
        pltpu.make_async_copy(state_hbm.at[:, pl.ds(regions - 2, 2)], state_ref.at[0], sems.at[1]),
        pltpu.make_async_copy(state_hbm.at[:, pl.ds(0, 2)], state_ref.at[1], sems.at[2]),
    ]
    for c in copies:
        c.start()
    chunks = field_ref.shape[2] // CHUNK
    copies[0].wait()
    tiles = []
    for q in range(chunks):
        for m in range(MEM):
            tiles.append(field_ref[m, :, q * CHUNK : (q + 1) * CHUNK].astype(F32)[None])
    rows = jnp.transpose(jnp.concatenate(tiles, axis=0), (1, 0, 2)).astype(BF)
    own_ref[...] = rows
    last = (chunks - 1) * MEM
    for c in copies[1:]:
        c.wait()
    for k, out in enumerate((right_ref, left_ref)):
        for r in range(2):
            for j in range(2):
                out[r, j * MEM : (j + 1) * MEM, : 2 * HALF] = state_ref[k, r, j]
        for d in range(8):
            at, lane = (d % 2) * MEM, (d // 2 % 2) * HALF
            out[2 + d // 4, at : at + MEM, lane : lane + HALF] = rows[d, last:, CHUNK - HALF :] if k == 0 else rows[d, :MEM, :HALF]
    for slot in range(slots):
        low = row_of(slot, row_ref) == 0
        dright_ref, edge_ref, dleft_ref = rest[3 * slot : 3 * slot + 3]
        for k in range(2):
            row = jnp.where(low, rows[k], rows[6 + k])
            edge_ref[k] = row
            dright_ref[k * MEM : (k + 1) * MEM, :HALF] = row[last:, CHUNK - HALF :]
            dleft_ref[k * MEM : (k + 1) * MEM] = row[:MEM, :HALF]


def own_kernel(slot, row_ref, state_ref, *rest):
    r = row_of(slot, row_ref)
    rows = [state_ref[r, 4 * q + res].astype(F32) for res in range(4) for q in range(state_ref.shape[1] // 4)]
    rest[-1][...] = jnp.concatenate(rows, axis=0).astype(BF)


def pack(row, out_ref, k):
    last = row.shape[0] - MEM
    out_ref[k, :, :CHUNK] = row[MEM:last].astype(BF)
    half = NEAR // 2
    ends = [row[:MEM, CHUNK - NEAR : CHUNK - half], row[:MEM, CHUNK - half :], row[last:, :half], row[last:, half:NEAR]]
    out_ref[k, :, CHUNK:] = jnp.concatenate(ends, axis=0).astype(BF)


def unpack(msg):
    x = msg.astype(F32)
    own, ends = x[:, :CHUNK], x[:, CHUNK:]
    fill = jnp.zeros((MEM, CHUNK - 2 * ends.shape[1]), F32)
    before = jnp.concatenate([fill, ends[:MEM], ends[MEM : 2 * MEM]], axis=1)
    after = jnp.concatenate([ends[2 * MEM : 3 * MEM], ends[3 * MEM :], fill], axis=1)
    return jnp.concatenate([before, own, after], axis=0)


def windows(lats, narrow):
    parts = [[] for _ in range(4)]
    side = 2 * VARS
    for a in lats:
        rows = a.shape[0]
        before = jnp.concatenate([a[rows - MEM :, CHUNK - side :], a[: rows - MEM, CHUNK - side :]], axis=0)
        after = jnp.concatenate([a[MEM:, :side], a[:MEM, :side]], axis=0)
        parts[0] += [before, a[:, : 3 * side]]
        parts[1].append(a[:, side : 5 * side])
        parts[2].append(a[:, 3 * side : 7 * side])
        parts[3] += [a[:, 5 * side :], after]
    if narrow:
        parts = [[x[MEM : x.shape[0] - MEM] for x in p] for p in parts]
    return jnp.concatenate([jnp.concatenate(p, axis=1) for p in parts], axis=0).astype(BF)


def latitude(pred, d):
    per = pred.shape[0] // 4
    return jnp.concatenate([pred[res * per : (res + 1) * per, d * CELL : (d + 1) * CELL] for res in range(4)], axis=1)


def of_band(band, values, *at):
    got = values[(0, *at)]
    for g in range(1, values.shape[0]):
        got = jnp.where(band == g, values[(g, *at)], got)
    return got


def block_at(index, ref):
    return pl.multiple_of(jnp.clip(index, 0, ref.shape[1] // BLK - 1) * BLK, BLK)


def block_pre(b, band, s_ref, in_ref, cidx, iidx, coup_ref, inp_ref):
    pieces = []
    mats = [coup_ref[band, (2 * b + k) * BLK : (2 * b + k + 1) * BLK, :] for k in range(2)]
    mats.append(inp_ref[band, b * BLK : (b + 1) * BLK, :])
    for k in range(2):
        pieces.append(s_ref[:, pl.ds(block_at(of_band(band, cidx, k, b), s_ref), BLK)])
    pieces.append(in_ref[:, pl.ds(block_at(of_band(band, iidx, b), in_ref), BLK)])
    return lax.dot_general(jnp.concatenate(pieces, axis=1), jnp.concatenate(mats, axis=1), NT, preferred_element_type=F32)


def half_of(r, rest_lats):
    return pl.ds(pl.multiple_of((1 - r if rest_lats else r) * 2 * CELL, 2 * CELL), 2 * CELL)


def send_edge(r, state, read_ref, msg_ref, edge_ref, s_ref):
    s_ref[...] = state
    pred = lax.dot_general(state, read_ref[half_of(r, False), :], NT, preferred_element_type=F32)
    for d in range(2):
        row = latitude(pred, d)
        pack(row, msg_ref, d)
        edge_ref[d] = row.astype(BF)


def first_kernel(slot, edge, behind, row_ref, band_ref, cidx_ref, iidx_ref, coup_ref, inp_ref, read_ref, own_ref, s0_ref, fl_ref, *rest):
    rest = list(rest)
    r = row_of(slot, row_ref)
    if edge:
        dl_ref, lat_ref, fr_ref, dr_ref = rest[:4]
        del rest[: 4 + behind]
    else:
        fr_ref = rest[1]
        del rest[:2]
    outs, (xs_ref, s_ref, in_ref) = rest[:-3], rest[-3:]
    fill = jnp.zeros((MEM, CHUNK - HALF), F32)

    def widen(own, left, right):
        left = jnp.concatenate([fill, left.astype(F32)], axis=1)
        right = jnp.concatenate([right.astype(F32), fill], axis=1)
        return jnp.concatenate([left, own.astype(F32), right], axis=0)

    for d in range(8):
        at, lane = (d % 2) * MEM, (d // 2 % 2) * HALF
        left = fl_ref[2 + d // 4, at : at + MEM, lane : lane + HALF]
        right = fr_ref[2 + d // 4, at : at + MEM, lane : lane + HALF]
        xs_ref[2 + d] = widen(own_ref[d], left, right)
    for k in range(2):
        at = k * MEM
        if edge:
            xs_ref[10 * r + k] = widen(lat_ref[k], dl_ref[at : at + MEM, :HALF], dr_ref[at : at + MEM])
        else:
            xs_ref[10 * r + k] = jnp.zeros(xs_ref.shape[1:], F32)
    empty = jnp.zeros((MEM, s0_ref.shape[1]), F32)
    per = s0_ref.shape[0] // 4
    rows = []
    for res in range(4):
        rows.append(fl_ref[r, (res - 2) * MEM : (res - 1) * MEM, : 2 * HALF].astype(F32) if res >= 2 else empty)
        rows.append(s0_ref[res * per : (res + 1) * per].astype(F32))
        rows.append(fr_ref[r, res * MEM : (res + 1) * MEM].astype(F32) if res < 2 else empty)
    s_ref[...] = jnp.concatenate(rows, axis=0).astype(BF)
    in_ref[...] = windows([xs_ref[4 * r + d] for d in range(8)], False)
    bands, cidx, iidx = band_ref[...], cidx_ref[...], iidx_ref[...]
    band = jnp.where(r == 0, bands[0], bands[1])
    pres = [block_pre(b, band, s_ref, in_ref, cidx, iidx, coup_ref, inp_ref) for b in range(iidx_ref.shape[1])]
    state = jnp.concatenate([jnp.tanh(p).astype(BF) for p in pres], axis=1)
    if edge:
        send_edge(r, state, read_ref, *outs)
        return
    outs[0][...] = state


def narrowed(s):
    per = s.shape[0] // 4
    return jnp.concatenate([s[res * per + MEM : (res + 1) * per - MEM] for res in range(4)], axis=0)


def shadow_kernel(second, last, slots, row_ref, band_ref, cidx_ref, iidx_ref, coup_ref, inp_ref, read_ref, *rest):
    rest = list(rest)

    def take(n):
        got = rest[:n]
        del rest[:n]
        return got

    edge_refs, s_refs = take(slots), take(slots)
    far_refs = take((1 if second else 2) * (2 - slots))
    pre_refs = take(slots)
    out_far = take(2 * (2 - slots))
    xs_ref, in_ref = take(2)
    rows_at = [row_of(0, row_ref), row_of(1, row_ref)]
    for k in range(2):
        xs_ref[k] = jnp.zeros(xs_ref.shape[1:], F32)
        xs_ref[10 + k] = jnp.zeros(xs_ref.shape[1:], F32)
    for slot in range(slots):
        r = rows_at[slot]
        pred = lax.dot_general(s_refs[slot][...], read_ref[half_of(r, True), :], NT, preferred_element_type=F32)
        for d in range(2):
            xs_ref[2 + 4 * r + 2 * r + d] = edge_refs[slot][d].astype(F32)
            xs_ref[2 + 4 * r + 2 * (1 - r) + d] = latitude(pred, d).astype(BF).astype(F32)
    if far_refs:
        s_refs = [s_refs[0], far_refs[-1]]
        if second:
            pred = lax.dot_general(far_refs[0][...], read_ref[...], NT, preferred_element_type=F32)
        for d in range(4):
            lat = latitude(pred, d).astype(BF) if second else far_refs[0][d]
            xs_ref[2 + 4 * rows_at[1] + d] = lat.astype(F32)
    if last:
        short_refs = take(2)
        for slot in range(2):
            short_refs[slot][...] = narrowed(s_refs[slot][...].astype(F32)).astype(BF)
        s_refs = short_refs

    bands, cidx, iidx = band_ref[...], cidx_ref[...], iidx_ref[...]
    copy = None
    for slot in (1, 0):
        r = rows_at[slot]
        band = jnp.where(r == 0, bands[0], bands[1])
        in_ref[...] = windows([xs_ref[4 * r + d] for d in range(8)], last)
        blocks = iidx_ref.shape[1]
        pres = [block_pre(b, band, s_refs[slot], in_ref, cidx, iidx, coup_ref, inp_ref) for b in range(blocks)]
        if slot < slots:
            for b in range(blocks):
                pre_refs[slot][:, b * BLK : (b + 1) * BLK] = pres[b]
            continue
        state = jnp.concatenate([jnp.tanh(p).astype(BF) for p in pres], axis=1)
        if last:
            stage_ref, sem = take(2)
            copy = put_states(r, state, stage_ref, out_far[1], sem)
        else:
            out_far[1][...] = state
        pred = lax.dot_general(state, read_ref[...], NT, preferred_element_type=F32)
        for d in range(4):
            out_far[0][d] = latitude(pred, d).astype(BF)
    if copy is not None:
        copy.wait()


def put_states(r, state, stage_ref, states_hbm, sem):
    per = state.shape[0] // 4
    for res in range(4):
        for q in range(per // MEM):
            at = res * per + q * MEM
            stage_ref[4 * q + res] = state[at : at + MEM]
    copy = pltpu.make_async_copy(stage_ref, states_hbm.at[r], sem)
    copy.start()
    return copy


def late_kernel(slot, last, final, row_ref, band_ref, iidx_ref, inp_ref, read_ref, pre_ref, got_ref, *rest):
    r = row_of(slot, row_ref)
    bands, iidx = band_ref[...], iidx_ref[...]
    band = jnp.where(r == 0, bands[0], bands[1])
    in_ref = rest[-1]
    in_ref[...] = windows([unpack(got_ref[k]) for k in range(2)], last)
    parts = []
    for b in range(iidx_ref.shape[1]):
        k = of_band(band, iidx, b) - 15 * r
        used = jnp.logical_and(k >= 0, k < 5)
        at = pl.multiple_of(jnp.where(used, k, 0) * BLK, BLK)
        term = lax.dot_general(in_ref[:, pl.ds(at, BLK)], inp_ref[band, b * BLK : (b + 1) * BLK, :], NT, preferred_element_type=F32)
        pre = pre_ref[:, b * BLK : (b + 1) * BLK] + jnp.where(used, term, 0.0)
        parts.append(jnp.tanh(pre).astype(BF))
    state = jnp.concatenate(parts, axis=1)
    if not last:
        send_edge(r, state, read_ref, *rest[:3])
        return
    if not final:
        lats_ref, states_hbm, stage_ref, sem = rest[:4]
    else:
        other_ref, _, field_hbm, states_hbm, stage_ref, sem, field_ref, field_sem = rest[:8]
    copy = put_states(r, state, stage_ref, states_hbm, sem)
    pred = lax.dot_general(state, read_ref[...], NT, preferred_element_type=F32)
    mine = [latitude(pred, d) for d in range(4)]
    if not final:
        for d in range(4):
            lats_ref[d] = mine[d].astype(BF)
        copy.wait()
        return
    other = [other_ref[d].astype(F32) for d in range(4)]
    low = r == 0
    rows = [jnp.where(low, mine[d], other[d])[None] for d in range(4)]
    rows += [jnp.where(low, other[d], mine[d])[None] for d in range(4)]
    tiles = jnp.transpose(jnp.concatenate(rows, axis=0), (1, 0, 2)).astype(BF)
    for q in range(field_ref.shape[2] // CHUNK):
        for m in range(MEM):
            field_ref[m, :, q * CHUNK : (q + 1) * CHUNK] = tiles[q * MEM + m]
    out = pltpu.make_async_copy(field_ref, field_hbm, field_sem)
    out.start()
    copy.wait()
    out.wait()


def call(kernel, out_shape, out_specs, scratch, operands, flops=0, aliases=None):
    arrays = [pltpu.with_memory_space_constraint(x, pltpu.HBM) if s is HB else x for x, s in operands]
    size = sum(x.size * x.dtype.itemsize for x, _ in operands)
    return pl.pallas_call(
        kernel,
        out_shape=out_shape,
        in_specs=[s for _, s in operands],
        out_specs=out_specs,
        scratch_shapes=scratch,
        input_output_aliases=aliases or {},
        compiler_params=pltpu.CompilerParams(vmem_limit_bytes=40 * 1024 * 1024),
        cost_estimate=pl.CostEstimate(flops=flops, bytes_accessed=size, transcendentals=0),
    )(*arrays)


def per_device(field_state, reservoir_state, coupling_blocks, coupling_index, input_blocks, input_index, readout, region_band):
    lat_count, lon_count = lax.axis_size("lat"), lax.axis_size("lon")
    lat_at = lax.axis_index("lat").astype(jnp.int32)
    region_rows, regions, members, units = reservoir_state.shape
    outs = readout.shape[1]
    assert region_rows == 2 and members == MEM and regions % 4 == 0
    chunks = regions // 4
    own_rows = chunks * MEM
    wide = own_rows + 2 * MEM
    rows = 4 * wide
    short = 4 * own_rows
    swap = lat_count == 2
    slots = 1 if swap else 2

    def bf(*dims):
        return jax.ShapeDtypeStruct(dims, BF)

    def vm(dims, dtype=BF):
        return pltpu.VMEM(dims, dtype)

    def send(x, lat_step, lon_step):
        pairs = []
        for i in range(lat_count):
            to = 1 - i if swap and lat_step else i + lat_step
            if 0 <= to < lat_count:
                for j in range(lon_count):
                    pairs.append((i * lon_count + j, to * lon_count + (j + lon_step) % lon_count))
        return lax.ppermute(x, ("lat", "lon"), pairs)

    def across(xs, lon_step=0):
        if swap:
            return [send(xs[0], 1, lon_step)]
        return [send(xs[1], 1, lon_step), send(xs[0], -1, lon_step)]

    row = ((1 - lat_at if swap else lat_at * 0).reshape(1), SM)
    small = [(region_band, VM), (coupling_index.transpose(0, 2, 1), VM), (input_index, VM)]
    band, _, iidx = small
    flops = 2 * rows * units * (3 * BLK + outs)

    mail = call(
        functools.partial(message_kernel, slots),
        [bf(4, 2 * MEM, 2 * HALF)] * 2 + [bf(8, own_rows, CHUNK)] + [bf(2 * MEM, 1536), bf(2, own_rows, CHUNK), bf(2 * MEM, HALF)] * slots,
        [VM] * (3 + 3 * slots),
        [vm(field_state.shape), vm((2, region_rows, 2, MEM, units)), pltpu.SemaphoreType.DMA((3,))],
        [row, (field_state, HB), (reservoir_state, HB)],
        AHEAD,
    )
    from_left = send(mail[0], 0, 1)
    from_dleft = across(mail[3::3], 1)
    from_lat = across(mail[4::3])
    from_right = send(mail[1], 0, -1)
    from_dright = across(mail[5::3], -1)
    own = (mail[2], VM)
    waits = [from_left] + from_dleft
    s0s1 = []
    for slot in range(2):
        operands = [row, (reservoir_state, VM)] + [(x, VM) for x in waits]
        s0s1.append(call(functools.partial(own_kernel, slot), bf(short, units), VM, [], operands, ORDER[slot]))
        waits = from_lat + s0s1
    s0, s1 = s0s1
    weights = [(x, VM) for x in (coupling_blocks, input_blocks, readout[0])]
    states_shape = bf(region_rows, regions, MEM, units)
    stage = [vm((regions, MEM, units)), pltpu.SemaphoreType.DMA]
    padded = vm((12, wide, CHUNK), F32)
    send_out = [bf(2, own_rows, CHUNK + NEAR // 2), bf(2, wide, CHUNK), bf(rows, units)]

    sent, edges, states, far = [None] * slots, [None] * slots, [None] * slots, []
    for slot in (1, 0):
        edge = slot < slots
        operands = [row] + small + weights + [own, ((s0, s1)[slot], VM), (from_left, VM)]
        if edge:
            operands.append((from_dleft[slot], VM))
        operands.append((from_lat[slot if edge else 0], VM))
        operands.append((from_right, VM))
        if edge:
            operands.append((from_dright[slot], VM))
            operands += [(x, VM) for x in far]
        got = call(
            functools.partial(first_kernel, slot, edge, len(far)),
            send_out if edge else [bf(rows, units)],
            [VM] * (3 if edge else 1),
            [padded, vm((rows, units)), vm((rows, 16 * CELL))],
            operands,
            flops if edge else 0,
        )
        if edge:
            sent[slot], edges[slot], states[slot] = got
        else:
            far = list(got)

    for step in range(1, STEPS):
        last = step == STEPS - 1
        got = across(sent)
        pre_rows = short if last else rows
        out = [jax.ShapeDtypeStruct((pre_rows, units), F32)] * slots
        specs = [VM] * slots
        scratch = [padded, vm((pre_rows, 16 * CELL))] + [vm((short, units))] * (2 if last else 0)
        if swap:
            out += [bf(4, own_rows if last else wide, CHUNK), states_shape if last else bf(rows, units)]
            specs += [VM, HB if last else VM]
            scratch += stage if last else []
        shadow = call(
            functools.partial(shadow_kernel, step == 1, last, slots),
            out,
            specs,
            scratch,
            [row] + small + weights + [(x, VM) for x in edges + states + far],
            2 * flops,
        )
        far = list(shadow[slots:])
        for slot in reversed(range(slots)):
            operands = [row, band, iidx] + weights[1:] + [(shadow[slot], VM), (got[slot], VM)]
            inputs = [vm((pre_rows, 4 * CELL))]
            if not last:
                sent[slot], edges[slot], states[slot] = call(
                    functools.partial(late_kernel, slot, False, False), send_out, [VM] * 3, inputs, operands, flops
                )
            elif slot == 1:
                far = call(
                    functools.partial(late_kernel, slot, True, False),
                    [bf(4, own_rows, CHUNK), states_shape],
                    [VM, HB],
                    stage + inputs,
                    operands,
                    flops,
                )
            else:
                return call(
                    functools.partial(late_kernel, slot, True, True),
                    [bf(MEM, 8, regions * CELL), states_shape],
                    [HB, HB],
                    stage + [vm((MEM, 8, regions * CELL)), pltpu.SemaphoreType.DMA] + inputs,
                    operands + [(far[0], VM), (far[1], HB)],
                    flops,
                    {len(operands) + 1: 1},
                )


def solution(mesh):
    return jax.shard_map(
        per_device,
        mesh=mesh,
        in_specs=(
            P(None, "lat", "lon"),
            P("lat", "lon", None, None),
            P("lat", None, None),
            P("lat", None, None),
            P("lat", None, None),
            P("lat", None),
            P("lat", None, None),
            P("lat"),
        ),
        out_specs=(P(None, "lat", "lon"), P("lat", "lon", None, None)),
        check_vma=False,
    )
```

```python
import functools

import jax
import jax.numpy as jnp
from jax import lax
from jax.experimental import pallas as pl
from jax.experimental.pallas import tpu as pltpu
from jax.sharding import PartitionSpec as P

VARS = 40
STEPS = 3
CELL = 4 * VARS
CHUNK = 4 * CELL
HALF = 512
NEAR = 256
MEM = 4
BLK = 128
AHEAD = 10**10
ORDER = (3 * 10**8, 3 * 10**8)
BF = jnp.bfloat16
F32 = jnp.float32
VM = pl.BlockSpec(memory_space=pltpu.VMEM)
SM = pl.BlockSpec(memory_space=pltpu.SMEM)
HB = pl.BlockSpec(memory_space=pltpu.HBM)
NT = (((1,), (1,)), ((), ()))


def row_of(slot, row_ref):
    return row_ref[0] if slot == 0 else 1 - row_ref[0]


def message_kernel(slots, row_ref, field_hbm, state_hbm, right_ref, left_ref, own_ref, *rest):
    field_ref, state_ref, sems = rest[3 * slots :]
    regions = state_hbm.shape[1]
    copies = [
        pltpu.make_async_copy(field_hbm, field_ref, sems.at[0]),
        pltpu.make_async_copy(state_hbm.at[:, pl.ds(regions - 2, 2)], state_ref.at[0], sems.at[1]),
        pltpu.make_async_copy(state_hbm.at[:, pl.ds(0, 2)], state_ref.at[1], sems.at[2]),
    ]
    for c in copies:
        c.start()
    chunks = field_ref.shape[2] // CHUNK
    copies[0].wait()
    tiles = []
    for q in range(chunks):
        for m in range(MEM):
            tiles.append(field_ref[m, :, q * CHUNK : (q + 1) * CHUNK].astype(F32)[None])
    rows = jnp.transpose(jnp.concatenate(tiles, axis=0), (1, 0, 2)).astype(BF)
    own_ref[...] = rows
    last = (chunks - 1) * MEM
    for c in copies[1:]:
        c.wait()
    for k, out in enumerate((right_ref, left_ref)):
        for r in range(2):
            for j in range(2):
                out[r, j * MEM : (j + 1) * MEM, : 2 * HALF] = state_ref[k, r, j]
        for d in range(8):
            at, lane = (d % 2) * MEM, (d // 2 % 2) * HALF
            out[2 + d // 4, at : at + MEM, lane : lane + HALF] = rows[d, last:, CHUNK - HALF :] if k == 0 else rows[d, :MEM, :HALF]
    for slot in range(slots):
        low = row_of(slot, row_ref) == 0
        dright_ref, edge_ref, dleft_ref = rest[3 * slot : 3 * slot + 3]
        for k in range(2):
            row = jnp.where(low, rows[k], rows[6 + k])
            edge_ref[k] = row
            dright_ref[k * MEM : (k + 1) * MEM, :HALF] = row[last:, CHUNK - HALF :]
            dleft_ref[k * MEM : (k + 1) * MEM] = row[:MEM, :HALF]


def own_kernel(slot, row_ref, state_ref, *rest):
    r = row_of(slot, row_ref)
    rows = [state_ref[r, 4 * q + res].astype(F32) for res in range(4) for q in range(state_ref.shape[1] // 4)]
    rest[-1][...] = jnp.concatenate(rows, axis=0).astype(BF)


def pack(row, out_ref, k):
    last = row.shape[0] - MEM
    out_ref[k, :, :CHUNK] = row[MEM:last].astype(BF)
    half = NEAR // 2
    ends = [row[:MEM, CHUNK - NEAR : CHUNK - half], row[:MEM, CHUNK - half :], row[last:, :half], row[last:, half:NEAR]]
    out_ref[k, :, CHUNK:] = jnp.concatenate(ends, axis=0).astype(BF)


def unpack(msg):
    x = msg.astype(F32)
    own, ends = x[:, :CHUNK], x[:, CHUNK:]
    fill = jnp.zeros((MEM, CHUNK - 2 * ends.shape[1]), F32)
    before = jnp.concatenate([fill, ends[:MEM], ends[MEM : 2 * MEM]], axis=1)
    after = jnp.concatenate([ends[2 * MEM : 3 * MEM], ends[3 * MEM :], fill], axis=1)
    return jnp.concatenate([before, own, after], axis=0)


def windows(lats, narrow):
    parts = [[] for _ in range(4)]
    side = 2 * VARS
    for a in lats:
        rows = a.shape[0]
        before = jnp.concatenate([a[rows - MEM :, CHUNK - side :], a[: rows - MEM, CHUNK - side :]], axis=0)
        after = jnp.concatenate([a[MEM:, :side], a[:MEM, :side]], axis=0)
        parts[0] += [before, a[:, : 3 * side]]
        parts[1].append(a[:, side : 5 * side])
        parts[2].append(a[:, 3 * side : 7 * side])
        parts[3] += [a[:, 5 * side :], after]
    if narrow:
        parts = [[x[MEM : x.shape[0] - MEM] for x in p] for p in parts]
    return jnp.concatenate([jnp.concatenate(p, axis=1) for p in parts], axis=0).astype(BF)


def latitude(pred, d):
    per = pred.shape[0] // 4
    return jnp.concatenate([pred[res * per : (res + 1) * per, d * CELL : (d + 1) * CELL] for res in range(4)], axis=1)


def of_band(band, values, *at):
    got = values[(0, *at)]
    for g in range(1, values.shape[0]):
        got = jnp.where(band == g, values[(g, *at)], got)
    return got


def block_at(index, ref):
    return pl.multiple_of(jnp.clip(index, 0, ref.shape[1] // BLK - 1) * BLK, BLK)


def block_pre(b, band, s_ref, in_ref, cidx, iidx, coup_ref, inp_ref, other=None):
    pieces = []
    mats = [coup_ref[band, (2 * b + k) * BLK : (2 * b + k + 1) * BLK, :] for k in range(2)]
    mats.append(inp_ref[band, b * BLK : (b + 1) * BLK, :])
    for k in range(2):
        pieces.append(s_ref[:, pl.ds(block_at(of_band(band, cidx, k, b), s_ref), BLK)])
    pieces.append(in_ref[:, pl.ds(block_at(of_band(band, iidx, b), in_ref), BLK)])
    if other is not None:
        used, ref, at = other
        pieces[2] = jnp.where(used, ref[:, pl.ds(at, BLK)], pieces[2])
    return lax.dot_general(jnp.concatenate(pieces, axis=1), jnp.concatenate(mats, axis=1), NT, preferred_element_type=F32)


def half_of(r, rest_lats):
    return pl.ds(pl.multiple_of((1 - r if rest_lats else r) * 2 * CELL, 2 * CELL), 2 * CELL)


def send_edge(r, state, read_ref, msg_ref, edge_ref, s_ref):
    s_ref[...] = state
    pred = lax.dot_general(state, read_ref[half_of(r, False), :], NT, preferred_element_type=F32)
    for d in range(2):
        row = latitude(pred, d)
        pack(row, msg_ref, d)
        edge_ref[d] = row.astype(BF)


def widen(own, left, right):
    fill = jnp.zeros((MEM, CHUNK - HALF), F32)
    left = jnp.concatenate([fill, left.astype(F32)], axis=1)
    right = jnp.concatenate([right.astype(F32), fill], axis=1)
    return jnp.concatenate([left, own.astype(F32), right], axis=0)


def first_kernel(slots, row_ref, band_ref, cidx_ref, iidx_ref, coup_ref, inp_ref, own_ref, s0_ref, s1_ref, fl_ref, *rest):
    fr_ref = rest[slots]
    outs = rest[slots + 1 : -3]
    xs_ref, s_ref, in_ref = rest[-3:]
    for k in range(2):
        xs_ref[k] = jnp.zeros(xs_ref.shape[1:], F32)
        xs_ref[10 + k] = jnp.zeros(xs_ref.shape[1:], F32)
    for d in range(8):
        at, lane = (d % 2) * MEM, (d // 2 % 2) * HALF
        left = fl_ref[2 + d // 4, at : at + MEM, lane : lane + HALF]
        right = fr_ref[2 + d // 4, at : at + MEM, lane : lane + HALF]
        xs_ref[2 + d] = widen(own_ref[d], left, right)
    empty = jnp.zeros((MEM, s_ref.shape[1]), F32)
    bands, cidx, iidx = band_ref[...], cidx_ref[...], iidx_ref[...]
    for slot, src in ((1, s1_ref), (0, s0_ref)):
        r = row_of(slot, row_ref)
        per = src.shape[0] // 4
        rows = []
        for res in range(4):
            rows.append(fl_ref[r, (res - 2) * MEM : (res - 1) * MEM].astype(F32) if res >= 2 else empty)
            rows.append(src[res * per : (res + 1) * per].astype(F32))
            rows.append(fr_ref[r, res * MEM : (res + 1) * MEM].astype(F32) if res < 2 else empty)
        states = jnp.concatenate(rows, axis=0).astype(BF)
        inputs = windows([xs_ref[4 * r + d] for d in range(8)], False)
        if slot < slots:
            outs[2 * slot][...] = states
            outs[2 * slot + 1][...] = inputs
            continue
        s_ref[...] = states
        in_ref[...] = inputs
        band = jnp.where(r == 0, bands[0], bands[1])
        pres = [block_pre(b, band, s_ref, in_ref, cidx, iidx, coup_ref, inp_ref) for b in range(iidx_ref.shape[1])]
        outs[2 * slots][...] = jnp.concatenate([jnp.tanh(p).astype(BF) for p in pres], axis=1)


def first_edge_kernel(slot, row_ref, band_ref, cidx_ref, iidx_ref, coup_ref, inp_ref, read_ref, s_ref, in_ref, dl_ref, lat_ref, dr_ref, *rest):
    got_ref = rest[-1]
    r = row_of(slot, row_ref)
    lats = []
    for k in range(2):
        at = k * MEM
        lats.append(widen(lat_ref[k], dl_ref[at : at + MEM, :HALF], dr_ref[at : at + MEM]))
    got_ref[...] = windows(lats, False)
    bands, cidx, iidx = band_ref[...], cidx_ref[...], iidx_ref[...]
    band = jnp.where(r == 0, bands[0], bands[1])
    parts = []
    for b in range(iidx_ref.shape[1]):
        k = of_band(band, iidx, b) - 15 * r
        used = jnp.logical_and(k >= 0, k < 5)
        pre = block_pre(b, band, s_ref, in_ref, cidx, iidx, coup_ref, inp_ref, (used, got_ref, block_at(k, got_ref)))
        parts.append(jnp.tanh(pre).astype(BF))
    send_edge(r, jnp.concatenate(parts, axis=1), read_ref, *rest[:3])


def narrowed(s):
    per = s.shape[0] // 4
    return jnp.concatenate([s[res * per + MEM : (res + 1) * per - MEM] for res in range(4)], axis=0)


def shadow_kernel(second, last, slots, row_ref, band_ref, cidx_ref, iidx_ref, coup_ref, inp_ref, read_ref, *rest):
    rest = list(rest)

    def take(n):
        got = rest[:n]
        del rest[:n]
        return got

    edge_refs, s_refs = take(slots), take(slots)
    far_refs = take((1 if second else 2) * (2 - slots))
    pre_refs = take(slots)
    out_far = take(2 * (2 - slots))
    xs_ref, in_ref = take(2)
    rows_at = [row_of(0, row_ref), row_of(1, row_ref)]
    for k in range(2):
        xs_ref[k] = jnp.zeros(xs_ref.shape[1:], F32)
        xs_ref[10 + k] = jnp.zeros(xs_ref.shape[1:], F32)
    for slot in range(slots):
        r = rows_at[slot]
        pred = lax.dot_general(s_refs[slot][...], read_ref[half_of(r, True), :], NT, preferred_element_type=F32)
        for d in range(2):
            xs_ref[2 + 4 * r + 2 * r + d] = edge_refs[slot][d].astype(F32)
            xs_ref[2 + 4 * r + 2 * (1 - r) + d] = latitude(pred, d).astype(BF).astype(F32)
    if far_refs:
        s_refs = [s_refs[0], far_refs[-1]]
        if second:
            pred = lax.dot_general(far_refs[0][...], read_ref[...], NT, preferred_element_type=F32)
        for d in range(4):
            lat = latitude(pred, d).astype(BF) if second else far_refs[0][d]
            xs_ref[2 + 4 * rows_at[1] + d] = lat.astype(F32)
    if last:
        short_refs = take(2)
        for slot in range(2):
            short_refs[slot][...] = narrowed(s_refs[slot][...].astype(F32)).astype(BF)
        s_refs = short_refs

    bands, cidx, iidx = band_ref[...], cidx_ref[...], iidx_ref[...]
    copy = None
    for slot in (1, 0):
        r = rows_at[slot]
        band = jnp.where(r == 0, bands[0], bands[1])
        in_ref[...] = windows([xs_ref[4 * r + d] for d in range(8)], last)
        blocks = iidx_ref.shape[1]
        pres = [block_pre(b, band, s_refs[slot], in_ref, cidx, iidx, coup_ref, inp_ref) for b in range(blocks)]
        if slot < slots:
            for b in range(blocks):
                pre_refs[slot][:, b * BLK : (b + 1) * BLK] = pres[b]
            continue
        state = jnp.concatenate([jnp.tanh(p).astype(BF) for p in pres], axis=1)
        if last:
            stage_ref, sem = take(2)
            copy = put_states(r, state, stage_ref, out_far[1], sem)
        else:
            out_far[1][...] = state
        pred = lax.dot_general(state, read_ref[...], NT, preferred_element_type=F32)
        for d in range(4):
            out_far[0][d] = latitude(pred, d).astype(BF)
    if copy is not None:
        copy.wait()


def put_states(r, state, stage_ref, states_hbm, sem):
    per = state.shape[0] // 4
    for res in range(4):
        for q in range(per // MEM):
            at = res * per + q * MEM
            stage_ref[4 * q + res] = state[at : at + MEM]
    copy = pltpu.make_async_copy(stage_ref, states_hbm.at[r], sem)
    copy.start()
    return copy


def late_kernel(slot, last, final, row_ref, band_ref, iidx_ref, inp_ref, read_ref, pre_ref, got_ref, *rest):
    r = row_of(slot, row_ref)
    bands, iidx = band_ref[...], iidx_ref[...]
    band = jnp.where(r == 0, bands[0], bands[1])
    in_ref = rest[-1]
    in_ref[...] = windows([unpack(got_ref[k]) for k in range(2)], last)
    parts = []
    for b in range(iidx_ref.shape[1]):
        k = of_band(band, iidx, b) - 15 * r
        used = jnp.logical_and(k >= 0, k < 5)
        at = pl.multiple_of(jnp.where(used, k, 0) * BLK, BLK)
        term = lax.dot_general(in_ref[:, pl.ds(at, BLK)], inp_ref[band, b * BLK : (b + 1) * BLK, :], NT, preferred_element_type=F32)
        pre = pre_ref[:, b * BLK : (b + 1) * BLK] + jnp.where(used, term, 0.0)
        parts.append(jnp.tanh(pre).astype(BF))
    state = jnp.concatenate(parts, axis=1)
    if not last:
        send_edge(r, state, read_ref, *rest[:3])
        return
    if not final:
        lats_ref, states_hbm, stage_ref, sem = rest[:4]
    else:
        other_ref, _, field_hbm, states_hbm, stage_ref, sem, field_ref, field_sem = rest[:8]
    copy = put_states(r, state, stage_ref, states_hbm, sem)
    pred = lax.dot_general(state, read_ref[...], NT, preferred_element_type=F32)
    mine = [latitude(pred, d) for d in range(4)]
    if not final:
        for d in range(4):
            lats_ref[d] = mine[d].astype(BF)
        copy.wait()
        return
    other = [other_ref[d].astype(F32) for d in range(4)]
    low = r == 0
    rows = [jnp.where(low, mine[d], other[d])[None] for d in range(4)]
    rows += [jnp.where(low, other[d], mine[d])[None] for d in range(4)]
    tiles = jnp.transpose(jnp.concatenate(rows, axis=0), (1, 0, 2)).astype(BF)
    for q in range(field_ref.shape[2] // CHUNK):
        for m in range(MEM):
            field_ref[m, :, q * CHUNK : (q + 1) * CHUNK] = tiles[q * MEM + m]
    out = pltpu.make_async_copy(field_ref, field_hbm, field_sem)
    out.start()
    copy.wait()
    out.wait()


def call(kernel, out_shape, out_specs, scratch, operands, flops=0, aliases=None):
    arrays = [pltpu.with_memory_space_constraint(x, pltpu.HBM) if s is HB else x for x, s in operands]
    size = sum(x.size * x.dtype.itemsize for x, _ in operands)
    return pl.pallas_call(
        kernel,
        out_shape=out_shape,
        in_specs=[s for _, s in operands],
        out_specs=out_specs,
        scratch_shapes=scratch,
        input_output_aliases=aliases or {},
        compiler_params=pltpu.CompilerParams(vmem_limit_bytes=40 * 1024 * 1024),
        cost_estimate=pl.CostEstimate(flops=flops, bytes_accessed=size, transcendentals=0),
    )(*arrays)


def per_device(field_state, reservoir_state, coupling_blocks, coupling_index, input_blocks, input_index, readout, region_band):
    lat_count, lon_count = lax.axis_size("lat"), lax.axis_size("lon")
    lat_at = lax.axis_index("lat").astype(jnp.int32)
    region_rows, regions, members, units = reservoir_state.shape
    outs = readout.shape[1]
    assert region_rows == 2 and members == MEM and regions % 4 == 0
    chunks = regions // 4
    own_rows = chunks * MEM
    wide = own_rows + 2 * MEM
    rows = 4 * wide
    short = 4 * own_rows
    swap = lat_count == 2
    slots = 1 if swap else 2

    def bf(*dims):
        return jax.ShapeDtypeStruct(dims, BF)

    def vm(dims, dtype=BF):
        return pltpu.VMEM(dims, dtype)

    def send(x, lat_step, lon_step):
        pairs = []
        for i in range(lat_count):
            to = 1 - i if swap and lat_step else i + lat_step
            if 0 <= to < lat_count:
                for j in range(lon_count):
                    pairs.append((i * lon_count + j, to * lon_count + (j + lon_step) % lon_count))
        return lax.ppermute(x, ("lat", "lon"), pairs)

    def across(xs, lon_step=0):
        if swap:
            return [send(xs[0], 1, lon_step)]
        return [send(xs[1], 1, lon_step), send(xs[0], -1, lon_step)]

    row = ((1 - lat_at if swap else lat_at * 0).reshape(1), SM)
    small = [(region_band, VM), (coupling_index.transpose(0, 2, 1), VM), (input_index, VM)]
    band, _, iidx = small
    flops = 2 * rows * units * (3 * BLK + outs)

    mail = call(
        functools.partial(message_kernel, slots),
        [bf(4, 2 * MEM, 2 * HALF)] * 2 + [bf(8, own_rows, CHUNK)] + [bf(2 * MEM, 1536), bf(2, own_rows, CHUNK), bf(2 * MEM, HALF)] * slots,
        [VM] * (3 + 3 * slots),
        [vm(field_state.shape), vm((2, region_rows, 2, MEM, units)), pltpu.SemaphoreType.DMA((3,))],
        [row, (field_state, HB), (reservoir_state, HB)],
        AHEAD,
    )
    from_left = send(mail[0], 0, 1)
    from_dleft = across(mail[3::3], 1)
    from_lat = across(mail[4::3])
    from_right = send(mail[1], 0, -1)
    from_dright = across(mail[5::3], -1)
    own = (mail[2], VM)
    waits = [from_left] + from_dleft
    s0s1 = []
    for slot in range(2):
        operands = [row, (reservoir_state, VM)] + [(x, VM) for x in waits]
        s0s1.append(call(functools.partial(own_kernel, slot), bf(short, units), VM, [], operands, ORDER[slot]))
        waits = from_lat + s0s1
    s0, s1 = s0s1
    weights = [(x, VM) for x in (coupling_blocks, input_blocks, readout[0])]
    states_shape = bf(region_rows, regions, MEM, units)
    stage = [vm((regions, MEM, units)), pltpu.SemaphoreType.DMA]
    padded = vm((12, wide, CHUNK), F32)
    send_out = [bf(2, own_rows, CHUNK + NEAR // 2), bf(2, wide, CHUNK), bf(rows, units)]

    first = call(
        functools.partial(first_kernel, slots),
        [bf(rows, units), bf(rows, 16 * CELL)] * slots + [bf(rows, units)] * (2 - slots),
        [VM] * (2 + slots),
        [padded, vm((rows, units)), vm((rows, 16 * CELL))],
        [row] + small + weights[:2] + [own, (s0, VM), (s1, VM), (from_left, VM)] + [(x, VM) for x in from_lat] + [(from_right, VM)],
    )
    far = list(first[2 * slots :])
    sent, edges, states = [None] * slots, [None] * slots, [None] * slots
    for slot in range(slots):
        known = [(x, VM) for x in first[2 * slot : 2 * slot + 2]]
        corners = [(x[slot], VM) for x in (from_dleft, from_lat, from_dright)]
        sent[slot], edges[slot], states[slot] = call(
            functools.partial(first_edge_kernel, slot),
            send_out,
            [VM] * 3,
            [vm((rows, 4 * CELL))],
            [row] + small + weights + known + corners,
            flops,
        )

    for step in range(1, STEPS):
        last = step == STEPS - 1
        got = across(sent)
        pre_rows = short if last else rows
        out = [jax.ShapeDtypeStruct((pre_rows, units), F32)] * slots
        specs = [VM] * slots
        scratch = [padded, vm((pre_rows, 16 * CELL))] + [vm((short, units))] * (2 if last else 0)
        if swap:
            out += [bf(4, own_rows if last else wide, CHUNK), states_shape if last else bf(rows, units)]
            specs += [VM, HB if last else VM]
            scratch += stage if last else []
        shadow = call(
            functools.partial(shadow_kernel, step == 1, last, slots),
            out,
            specs,
            scratch,
            [row] + small + weights + [(x, VM) for x in edges + states + far],
            2 * flops,
        )
        far = list(shadow[slots:])
        for slot in reversed(range(slots)):
            operands = [row, band, iidx] + weights[1:] + [(shadow[slot], VM), (got[slot], VM)]
            inputs = [vm((pre_rows, 4 * CELL))]
            if not last:
                sent[slot], edges[slot], states[slot] = call(
                    functools.partial(late_kernel, slot, False, False), send_out, [VM] * 3, inputs, operands, flops
                )
            elif slot == 1:
                far = call(
                    functools.partial(late_kernel, slot, True, False),
                    [bf(4, own_rows, CHUNK), states_shape],
                    [VM, HB],
                    stage + inputs,
                    operands,
                    flops,
                )
            else:
                return call(
                    functools.partial(late_kernel, slot, True, True),
                    [bf(MEM, 8, regions * CELL), states_shape],
                    [HB, HB],
                    stage + [vm((MEM, 8, regions * CELL)), pltpu.SemaphoreType.DMA] + inputs,
                    operands + [(far[0], VM), (far[1], HB)],
                    flops,
                    {len(operands) + 1: 1},
                )


def solution(mesh):
    return jax.shard_map(
        per_device,
        mesh=mesh,
        in_specs=(
            P(None, "lat", "lon"),
            P("lat", "lon", None, None),
            P("lat", None, None),
            P("lat", None, None),
            P("lat", None, None),
            P("lat", None),
            P("lat", None, None),
            P("lat"),
        ),
        out_specs=(P(None, "lat", "lon"), P("lat", "lon", None, None)),
        check_vma=False,
    )
```

```python
import functools

import jax
import jax.numpy as jnp
from jax import lax
from jax.experimental import pallas as pl
from jax.experimental.pallas import tpu as pltpu
from jax.sharding import PartitionSpec as P

VARS = 40
STEPS = 3
CELL = 4 * VARS
CHUNK = 4 * CELL
HALF = 512
NEAR = 256
MEM = 4
BLK = 128
AHEAD = 10**10
ORDER = (3 * 10**8, 3 * 10**8)
BF = jnp.bfloat16
F32 = jnp.float32
VM = pl.BlockSpec(memory_space=pltpu.VMEM)
SM = pl.BlockSpec(memory_space=pltpu.SMEM)
HB = pl.BlockSpec(memory_space=pltpu.HBM)
NT = (((1,), (1,)), ((), ()))


def row_of(slot, row_ref):
    return row_ref[0] if slot == 0 else 1 - row_ref[0]


def message_kernel(slots, row_ref, field_hbm, state_hbm, right_ref, left_ref, own_ref, *rest):
    field_ref, state_ref, sems = rest[3 * slots :]
    regions = state_hbm.shape[1]
    copies = [
        pltpu.make_async_copy(field_hbm, field_ref, sems.at[0]),
        pltpu.make_async_copy(state_hbm.at[:, pl.ds(regions - 2, 2)], state_ref.at[0], sems.at[1]),
        pltpu.make_async_copy(state_hbm.at[:, pl.ds(0, 2)], state_ref.at[1], sems.at[2]),
    ]
    for c in copies:
        c.start()
    chunks = field_ref.shape[2] // CHUNK
    copies[0].wait()
    tiles = []
    for q in range(chunks):
        for m in range(MEM):
            tiles.append(field_ref[m, :, q * CHUNK : (q + 1) * CHUNK].astype(F32)[None])
    rows = jnp.transpose(jnp.concatenate(tiles, axis=0), (1, 0, 2)).astype(BF)
    own_ref[...] = rows
    last = (chunks - 1) * MEM
    for c in copies[1:]:
        c.wait()
    for k, out in enumerate((right_ref, left_ref)):
        for r in range(2):
            for j in range(2):
                out[r, j * MEM : (j + 1) * MEM, : 2 * HALF] = state_ref[k, r, j]
        for d in range(8):
            at, lane = (d % 2) * MEM, (d // 2 % 2) * HALF
            out[2 + d // 4, at : at + MEM, lane : lane + HALF] = rows[d, last:, CHUNK - HALF :] if k == 0 else rows[d, :MEM, :HALF]
    for slot in range(slots):
        low = row_of(slot, row_ref) == 0
        dright_ref, edge_ref, dleft_ref = rest[3 * slot : 3 * slot + 3]
        for k in range(2):
            row = jnp.where(low, rows[k], rows[6 + k])
            edge_ref[k] = row
            dright_ref[k * MEM : (k + 1) * MEM, :HALF] = row[last:, CHUNK - HALF :]
            dleft_ref[k * MEM : (k + 1) * MEM] = row[:MEM, :HALF]


def own_kernel(slot, row_ref, state_ref, *rest):
    r = row_of(slot, row_ref)
    rows = [state_ref[r, 4 * q + res].astype(F32) for res in range(4) for q in range(state_ref.shape[1] // 4)]
    rest[-1][...] = jnp.concatenate(rows, axis=0).astype(BF)


def pack(row, out_ref, k):
    last = row.shape[0] - MEM
    out_ref[k, :, :CHUNK] = row[MEM:last].astype(BF)
    half = NEAR // 2
    ends = [row[:MEM, CHUNK - NEAR : CHUNK - half], row[:MEM, CHUNK - half :], row[last:, :half], row[last:, half:NEAR]]
    out_ref[k, :, CHUNK:] = jnp.concatenate(ends, axis=0).astype(BF)


def unpack(msg):
    x = msg.astype(F32)
    own, ends = x[:, :CHUNK], x[:, CHUNK:]
    fill = jnp.zeros((MEM, CHUNK - 2 * ends.shape[1]), F32)
    before = jnp.concatenate([fill, ends[:MEM], ends[MEM : 2 * MEM]], axis=1)
    after = jnp.concatenate([ends[2 * MEM : 3 * MEM], ends[3 * MEM :], fill], axis=1)
    return jnp.concatenate([before, own, after], axis=0)


def windows(lats, narrow):
    parts = [[] for _ in range(4)]
    side = 2 * VARS
    for a in lats:
        rows = a.shape[0]
        before = jnp.concatenate([a[rows - MEM :, CHUNK - side :], a[: rows - MEM, CHUNK - side :]], axis=0)
        after = jnp.concatenate([a[MEM:, :side], a[:MEM, :side]], axis=0)
        parts[0] += [before, a[:, : 3 * side]]
        parts[1].append(a[:, side : 5 * side])
        parts[2].append(a[:, 3 * side : 7 * side])
        parts[3] += [a[:, 5 * side :], after]
    if narrow:
        parts = [[x[MEM : x.shape[0] - MEM] for x in p] for p in parts]
    return jnp.concatenate([jnp.concatenate(p, axis=1) for p in parts], axis=0).astype(BF)


def latitude(pred, d):
    per = pred.shape[0] // 4
    return jnp.concatenate([pred[res * per : (res + 1) * per, d * CELL : (d + 1) * CELL] for res in range(4)], axis=1)


def of_band(band, values, *at):
    got = values[(0, *at)]
    for g in range(1, values.shape[0]):
        got = jnp.where(band == g, values[(g, *at)], got)
    return got


def block_at(index, ref):
    return pl.multiple_of(jnp.clip(index, 0, ref.shape[1] // BLK - 1) * BLK, BLK)


def block_pre(b, band, s_ref, in_ref, cidx, iidx, coup_ref, inp_ref, other=None):
    pieces = []
    mats = [coup_ref[band, (2 * b + k) * BLK : (2 * b + k + 1) * BLK, :] for k in range(2)]
    mats.append(inp_ref[band, b * BLK : (b + 1) * BLK, :])
    for k in range(2):
        pieces.append(s_ref[:, pl.ds(block_at(of_band(band, cidx, k, b), s_ref), BLK)])
    pieces.append(in_ref[:, pl.ds(block_at(of_band(band, iidx, b), in_ref), BLK)])
    if other is not None:
        used, ref, at = other
        pieces[2] = jnp.where(used, ref[:, pl.ds(at, BLK)], pieces[2])
    return lax.dot_general(jnp.concatenate(pieces, axis=1), jnp.concatenate(mats, axis=1), NT, preferred_element_type=F32)


def half_of(r, rest_lats):
    return pl.ds(pl.multiple_of((1 - r if rest_lats else r) * 2 * CELL, 2 * CELL), 2 * CELL)


def send_edge(r, state, read_ref, msg_ref, edge_ref, s_ref):
    s_ref[...] = state
    pred = lax.dot_general(state, read_ref[half_of(r, False), :], NT, preferred_element_type=F32)
    for d in range(2):
        row = latitude(pred, d)
        pack(row, msg_ref, d)
        edge_ref[d] = row.astype(BF)


def widen(own, left, right):
    fill = jnp.zeros((MEM, CHUNK - HALF), F32)
    left = jnp.concatenate([fill, left.astype(F32)], axis=1)
    right = jnp.concatenate([right.astype(F32), fill], axis=1)
    return jnp.concatenate([left, own.astype(F32), right], axis=0)


def first_kernel(slots, row_ref, band_ref, cidx_ref, iidx_ref, coup_ref, inp_ref, _, own_ref, s0_ref, s1_ref, fl_ref, *rest):
    fr_ref = rest[slots]
    outs = rest[slots + 1 : -3]
    xs_ref, s_ref, in_ref = rest[-3:]
    for k in range(2):
        xs_ref[k] = jnp.zeros(xs_ref.shape[1:], F32)
        xs_ref[10 + k] = jnp.zeros(xs_ref.shape[1:], F32)
    for d in range(8):
        at, lane = (d % 2) * MEM, (d // 2 % 2) * HALF
        left = fl_ref[2 + d // 4, at : at + MEM, lane : lane + HALF]
        right = fr_ref[2 + d // 4, at : at + MEM, lane : lane + HALF]
        xs_ref[2 + d] = widen(own_ref[d], left, right)
    empty = jnp.zeros((MEM, s_ref.shape[1]), F32)
    bands, cidx, iidx = band_ref[...], cidx_ref[...], iidx_ref[...]
    for slot, src in ((1, s1_ref), (0, s0_ref)):
        r = row_of(slot, row_ref)
        per = src.shape[0] // 4
        rows = []
        for res in range(4):
            rows.append(fl_ref[r, (res - 2) * MEM : (res - 1) * MEM].astype(F32) if res >= 2 else empty)
            rows.append(src[res * per : (res + 1) * per].astype(F32))
            rows.append(fr_ref[r, res * MEM : (res + 1) * MEM].astype(F32) if res < 2 else empty)
        states = jnp.concatenate(rows, axis=0).astype(BF)
        inputs = windows([xs_ref[4 * r + d] for d in range(8)], False)
        if slot < slots:
            outs[2 * slot][...] = states
            outs[2 * slot + 1][...] = inputs
            continue
        s_ref[...] = states
        in_ref[...] = inputs
        band = jnp.where(r == 0, bands[0], bands[1])
        pres = [block_pre(b, band, s_ref, in_ref, cidx, iidx, coup_ref, inp_ref) for b in range(iidx_ref.shape[1])]
        outs[2 * slots][...] = jnp.concatenate([jnp.tanh(p).astype(BF) for p in pres], axis=1)


def first_edge_kernel(slot, row_ref, band_ref, cidx_ref, iidx_ref, coup_ref, inp_ref, read_ref, s_ref, in_ref, dl_ref, lat_ref, dr_ref, *rest):
    got_ref = rest[-1]
    r = row_of(slot, row_ref)
    lats = []
    for k in range(2):
        at = k * MEM
        lats.append(widen(lat_ref[k], dl_ref[at : at + MEM, :HALF], dr_ref[at : at + MEM]))
    got_ref[...] = windows(lats, False)
    bands, cidx, iidx = band_ref[...], cidx_ref[...], iidx_ref[...]
    band = jnp.where(r == 0, bands[0], bands[1])
    parts = []
    for b in range(iidx_ref.shape[1]):
        k = of_band(band, iidx, b) - 15 * r
        used = jnp.logical_and(k >= 0, k < 5)
        pre = block_pre(b, band, s_ref, in_ref, cidx, iidx, coup_ref, inp_ref, (used, got_ref, block_at(k, got_ref)))
        parts.append(jnp.tanh(pre).astype(BF))
    send_edge(r, jnp.concatenate(parts, axis=1), read_ref, *rest[:3])


def narrowed(s):
    per = s.shape[0] // 4
    return jnp.concatenate([s[res * per + MEM : (res + 1) * per - MEM] for res in range(4)], axis=0)


def shadow_kernel(second, last, slots, row_ref, band_ref, cidx_ref, iidx_ref, coup_ref, inp_ref, read_ref, *rest):
    rest = list(rest)

    def take(n):
        got = rest[:n]
        del rest[:n]
        return got

    edge_refs, s_refs = take(slots), take(slots)
    far_refs = take((1 if second else 2) * (2 - slots))
    pre_refs = take(slots)
    out_far = take(2 * (2 - slots))
    xs_ref, in_ref = take(2)
    rows_at = [row_of(0, row_ref), row_of(1, row_ref)]
    for k in range(2):
        xs_ref[k] = jnp.zeros(xs_ref.shape[1:], F32)
        xs_ref[10 + k] = jnp.zeros(xs_ref.shape[1:], F32)
    for slot in range(slots):
        r = rows_at[slot]
        pred = lax.dot_general(s_refs[slot][...], read_ref[half_of(r, True), :], NT, preferred_element_type=F32)
        for d in range(2):
            xs_ref[2 + 4 * r + 2 * r + d] = edge_refs[slot][d].astype(F32)
            xs_ref[2 + 4 * r + 2 * (1 - r) + d] = latitude(pred, d).astype(BF).astype(F32)
    if far_refs:
        s_refs = [s_refs[0], far_refs[-1]]
        if second:
            pred = lax.dot_general(far_refs[0][...], read_ref[...], NT, preferred_element_type=F32)
        for d in range(4):
            lat = latitude(pred, d).astype(BF) if second else far_refs[0][d]
            xs_ref[2 + 4 * rows_at[1] + d] = lat.astype(F32)
    if last:
        short_refs = take(2)
        for slot in range(2):
            short_refs[slot][...] = narrowed(s_refs[slot][...].astype(F32)).astype(BF)
        s_refs = short_refs

    bands, cidx, iidx = band_ref[...], cidx_ref[...], iidx_ref[...]
    copy = None
    for slot in (1, 0):
        r = rows_at[slot]
        band = jnp.where(r == 0, bands[0], bands[1])
        in_ref[...] = windows([xs_ref[4 * r + d] for d in range(8)], last)
        blocks = iidx_ref.shape[1]
        pres = [block_pre(b, band, s_refs[slot], in_ref, cidx, iidx, coup_ref, inp_ref) for b in range(blocks)]
        if slot < slots:
            for b in range(blocks):
                pre_refs[slot][:, b * BLK : (b + 1) * BLK] = pres[b]
            continue
        state = jnp.concatenate([jnp.tanh(p).astype(BF) for p in pres], axis=1)
        if last:
            stage_ref, sem = take(2)
            copy = put_states(r, state, stage_ref, out_far[1], sem)
        else:
            out_far[1][...] = state
        pred = lax.dot_general(state, read_ref[...], NT, preferred_element_type=F32)
        for d in range(4):
            out_far[0][d] = latitude(pred, d).astype(BF)
    if copy is not None:
        copy.wait()


def put_states(r, state, stage_ref, states_hbm, sem):
    per = state.shape[0] // 4
    for res in range(4):
        for q in range(per // MEM):
            at = res * per + q * MEM
            stage_ref[4 * q + res] = state[at : at + MEM]
    copy = pltpu.make_async_copy(stage_ref, states_hbm.at[r], sem)
    copy.start()
    return copy


def late_kernel(slot, last, final, row_ref, band_ref, iidx_ref, inp_ref, read_ref, pre_ref, got_ref, *rest):
    r = row_of(slot, row_ref)
    bands, iidx = band_ref[...], iidx_ref[...]
    band = jnp.where(r == 0, bands[0], bands[1])
    in_ref = rest[-1]
    in_ref[...] = windows([unpack(got_ref[k]) for k in range(2)], last)
    parts = []
    for b in range(iidx_ref.shape[1]):
        k = of_band(band, iidx, b) - 15 * r
        used = jnp.logical_and(k >= 0, k < 5)
        at = pl.multiple_of(jnp.where(used, k, 0) * BLK, BLK)
        term = lax.dot_general(in_ref[:, pl.ds(at, BLK)], inp_ref[band, b * BLK : (b + 1) * BLK, :], NT, preferred_element_type=F32)
        pre = pre_ref[:, b * BLK : (b + 1) * BLK] + jnp.where(used, term, 0.0)
        parts.append(jnp.tanh(pre).astype(BF))
    state = jnp.concatenate(parts, axis=1)
    if not last:
        send_edge(r, state, read_ref, *rest[:3])
        return
    if not final:
        lats_ref, states_hbm, stage_ref, sem = rest[:4]
    else:
        other_ref, _, field_hbm, states_hbm, stage_ref, sem, field_ref, field_sem = rest[:8]
    pred = lax.dot_general(state, read_ref[...], NT, preferred_element_type=F32)
    copy = put_states(r, state, stage_ref, states_hbm, sem)
    mine = [latitude(pred, d) for d in range(4)]
    if not final:
        for d in range(4):
            lats_ref[d] = mine[d].astype(BF)
        copy.wait()
        return
    other = [other_ref[d].astype(F32) for d in range(4)]
    low = r == 0
    rows = [jnp.where(low, mine[d], other[d])[None] for d in range(4)]
    rows += [jnp.where(low, other[d], mine[d])[None] for d in range(4)]
    tiles = jnp.transpose(jnp.concatenate(rows, axis=0), (1, 0, 2)).astype(BF)
    for q in range(field_ref.shape[2] // CHUNK):
        for m in range(MEM):
            field_ref[m, :, q * CHUNK : (q + 1) * CHUNK] = tiles[q * MEM + m]
    out = pltpu.make_async_copy(field_ref, field_hbm, field_sem)
    out.start()
    copy.wait()
    out.wait()


def call(kernel, out_shape, out_specs, scratch, operands, flops=0, aliases=None):
    arrays = [pltpu.with_memory_space_constraint(x, pltpu.HBM) if s is HB else x for x, s in operands]
    size = sum(x.size * x.dtype.itemsize for x, _ in operands)
    return pl.pallas_call(
        kernel,
        out_shape=out_shape,
        in_specs=[s for _, s in operands],
        out_specs=out_specs,
        scratch_shapes=scratch,
        input_output_aliases=aliases or {},
        compiler_params=pltpu.CompilerParams(vmem_limit_bytes=40 * 1024 * 1024),
        cost_estimate=pl.CostEstimate(flops=flops, bytes_accessed=size, transcendentals=0),
    )(*arrays)


def per_device(field_state, reservoir_state, coupling_blocks, coupling_index, input_blocks, input_index, readout, region_band):
    lat_count, lon_count = lax.axis_size("lat"), lax.axis_size("lon")
    lat_at = lax.axis_index("lat").astype(jnp.int32)
    region_rows, regions, members, units = reservoir_state.shape
    outs = readout.shape[1]
    assert region_rows == 2 and members == MEM and regions % 4 == 0
    chunks = regions // 4
    own_rows = chunks * MEM
    wide = own_rows + 2 * MEM
    rows = 4 * wide
    short = 4 * own_rows
    swap = lat_count == 2
    slots = 1 if swap else 2

    def bf(*dims):
        return jax.ShapeDtypeStruct(dims, BF)

    def vm(dims, dtype=BF):
        return pltpu.VMEM(dims, dtype)

    def send(x, lat_step, lon_step):
        pairs = []
        for i in range(lat_count):
            to = 1 - i if swap and lat_step else i + lat_step
            if 0 <= to < lat_count:
                for j in range(lon_count):
                    pairs.append((i * lon_count + j, to * lon_count + (j + lon_step) % lon_count))
        return lax.ppermute(x, ("lat", "lon"), pairs)

    def across(xs, lon_step=0):
        if swap:
            return [send(xs[0], 1, lon_step)]
        return [send(xs[1], 1, lon_step), send(xs[0], -1, lon_step)]

    row = ((1 - lat_at if swap else lat_at * 0).reshape(1), SM)
    small = [(region_band, VM), (coupling_index.transpose(0, 2, 1), VM), (input_index, VM)]
    band, _, iidx = small
    flops = 2 * rows * units * (3 * BLK + outs)

    mail = call(
        functools.partial(message_kernel, slots),
        [bf(4, 2 * MEM, 2 * HALF)] * 2 + [bf(8, own_rows, CHUNK)] + [bf(2 * MEM, 1536), bf(2, own_rows, CHUNK), bf(2 * MEM, HALF)] * slots,
        [VM] * (3 + 3 * slots),
        [vm(field_state.shape), vm((2, region_rows, 2, MEM, units)), pltpu.SemaphoreType.DMA((3,))],
        [row, (field_state, HB), (reservoir_state, HB)],
        AHEAD,
    )
    from_left = send(mail[0], 0, 1)
    from_dleft = across(mail[3::3], 1)
    from_lat = across(mail[4::3])
    from_right = send(mail[1], 0, -1)
    from_dright = across(mail[5::3], -1)
    own = (mail[2], VM)
    waits = [from_left] + from_dleft
    s0s1 = []
    for slot in range(2):
        operands = [row, (reservoir_state, VM)] + [(x, VM) for x in waits]
        s0s1.append(call(functools.partial(own_kernel, slot), bf(short, units), VM, [], operands, ORDER[slot]))
        waits = from_lat + s0s1
    s0, s1 = s0s1
    weights = [(x, VM) for x in (coupling_blocks, input_blocks, readout[0])]
    states_shape = bf(region_rows, regions, MEM, units)
    stage = [vm((regions, MEM, units)), pltpu.SemaphoreType.DMA]
    padded = vm((12, wide, CHUNK), F32)
    send_out = [bf(2, own_rows, CHUNK + NEAR // 2), bf(2, wide, CHUNK), bf(rows, units)]

    first = call(
        functools.partial(first_kernel, slots),
        [bf(rows, units), bf(rows, 16 * CELL)] * slots + [bf(rows, units)] * (2 - slots),
        [VM] * (2 + slots),
        [padded, vm((rows, units)), vm((rows, 16 * CELL))],
        [row] + small + weights + [own, (s0, VM), (s1, VM), (from_left, VM)] + [(x, VM) for x in from_lat] + [(from_right, VM)],
    )
    far = list(first[2 * slots :])
    sent, edges, states = [None] * slots, [None] * slots, [None] * slots
    for slot in range(slots):
        known = [(x, VM) for x in first[2 * slot : 2 * slot + 2]]
        corners = [(x[slot], VM) for x in (from_dleft, from_lat, from_dright)]
        sent[slot], edges[slot], states[slot] = call(
            functools.partial(first_edge_kernel, slot),
            send_out,
            [VM] * 3,
            [vm((rows, 4 * CELL))],
            [row] + small + weights + known + corners,
            flops,
        )

    for step in range(1, STEPS):
        last = step == STEPS - 1
        got = across(sent)
        pre_rows = short if last else rows
        out = [jax.ShapeDtypeStruct((pre_rows, units), F32)] * slots
        specs = [VM] * slots
        scratch = [padded, vm((pre_rows, 16 * CELL))] + [vm((short, units))] * (2 if last else 0)
        if swap:
            out += [bf(4, own_rows if last else wide, CHUNK), states_shape if last else bf(rows, units)]
            specs += [VM, HB if last else VM]
            scratch += stage if last else []
        shadow = call(
            functools.partial(shadow_kernel, step == 1, last, slots),
            out,
            specs,
            scratch,
            [row] + small + weights + [(x, VM) for x in edges + states + far],
            2 * flops,
        )
        far = list(shadow[slots:])
        for slot in reversed(range(slots)):
            operands = [row, band, iidx] + weights[1:] + [(shadow[slot], VM), (got[slot], VM)]
            inputs = [vm((pre_rows, 4 * CELL))]
            if not last:
                sent[slot], edges[slot], states[slot] = call(
                    functools.partial(late_kernel, slot, False, False), send_out, [VM] * 3, inputs, operands, flops
                )
            elif slot == 1:
                far = call(
                    functools.partial(late_kernel, slot, True, False),
                    [bf(4, own_rows, CHUNK), states_shape],
                    [VM, HB],
                    stage + inputs,
                    operands,
                    flops,
                )
            else:
                return call(
                    functools.partial(late_kernel, slot, True, True),
                    [bf(MEM, 8, regions * CELL), states_shape],
                    [HB, HB],
                    stage + [vm((MEM, 8, regions * CELL)), pltpu.SemaphoreType.DMA] + inputs,
                    operands + [(far[0], VM), (far[1], HB)],
                    flops,
                    {len(operands) + 1: 1},
                )


def solution(mesh):
    return jax.shard_map(
        per_device,
        mesh=mesh,
        in_specs=(
            P(None, "lat", "lon"),
            P("lat", "lon", None, None),
            P("lat", None, None),
            P("lat", None, None),
            P("lat", None, None),
            P("lat", None),
            P("lat", None, None),
            P("lat"),
        ),
        out_specs=(P(None, "lat", "lon"), P("lat", "lon", None, None)),
        check_vma=False,
    )
```

```python
import functools

import jax
import jax.numpy as jnp
from jax import lax
from jax.experimental import pallas as pl
from jax.experimental.pallas import tpu as pltpu
from jax.sharding import PartitionSpec as P

VARS = 40
STEPS = 3
CELL = 4 * VARS
CHUNK = 4 * CELL
HALF = 512
NEAR = 256
MEM = 4
BLK = 128
AHEAD = 10**9
ORDER = (3 * 10**8, 3 * 10**8)
BF = jnp.bfloat16
F32 = jnp.float32
VM = pl.BlockSpec(memory_space=pltpu.VMEM)
SM = pl.BlockSpec(memory_space=pltpu.SMEM)
HB = pl.BlockSpec(memory_space=pltpu.HBM)
NT = (((1,), (1,)), ((), ()))


def row_of(slot, row_ref):
    return row_ref[0] if slot == 0 else 1 - row_ref[0]


def message_kernel(slots, row_ref, field_hbm, state_hbm, right_ref, left_ref, own_ref, *rest):
    field_ref, state_ref, sems = rest[3 * slots :]
    regions = state_hbm.shape[1]
    copies = [
        pltpu.make_async_copy(field_hbm, field_ref, sems.at[0]),
        pltpu.make_async_copy(state_hbm.at[:, pl.ds(regions - 2, 2)], state_ref.at[0], sems.at[1]),
        pltpu.make_async_copy(state_hbm.at[:, pl.ds(0, 2)], state_ref.at[1], sems.at[2]),
    ]
    for c in copies:
        c.start()
    chunks = field_ref.shape[2] // CHUNK
    copies[0].wait()
    tiles = []
    for q in range(chunks):
        for m in range(MEM):
            tiles.append(field_ref[m, :, q * CHUNK : (q + 1) * CHUNK].astype(F32)[None])
    rows = jnp.transpose(jnp.concatenate(tiles, axis=0), (1, 0, 2)).astype(BF)
    own_ref[...] = rows
    last = (chunks - 1) * MEM
    for c in copies[1:]:
        c.wait()
    for k, out in enumerate((right_ref, left_ref)):
        for r in range(2):
            for j in range(2):
                out[r, j * MEM : (j + 1) * MEM, : 2 * HALF] = state_ref[k, r, j]
        for d in range(8):
            at, lane = (d % 2) * MEM, (d // 2 % 2) * HALF
            out[2 + d // 4, at : at + MEM, lane : lane + HALF] = rows[d, last:, CHUNK - HALF :] if k == 0 else rows[d, :MEM, :HALF]
    for slot in range(slots):
        low = row_of(slot, row_ref) == 0
        dright_ref, edge_ref, dleft_ref = rest[3 * slot : 3 * slot + 3]
        for k in range(2):
            row = jnp.where(low, rows[k], rows[6 + k])
            edge_ref[k] = row
            dright_ref[k * MEM : (k + 1) * MEM, :HALF] = row[last:, CHUNK - HALF :]
            dleft_ref[k * MEM : (k + 1) * MEM] = row[:MEM, :HALF]


def own_kernel(slot, row_ref, state_ref, *rest):
    r = row_of(slot, row_ref)
    rows = [state_ref[r, 4 * q + res].astype(F32) for res in range(4) for q in range(state_ref.shape[1] // 4)]
    rest[-1][...] = jnp.concatenate(rows, axis=0).astype(BF)


def pack(row, out_ref, k):
    last = row.shape[0] - MEM
    out_ref[k, :, :CHUNK] = row[MEM:last].astype(BF)
    half = NEAR // 2
    ends = [row[:MEM, CHUNK - NEAR : CHUNK - half], row[:MEM, CHUNK - half :], row[last:, :half], row[last:, half:NEAR]]
    out_ref[k, :, CHUNK:] = jnp.concatenate(ends, axis=0).astype(BF)


def unpack(msg):
    x = msg.astype(F32)
    own, ends = x[:, :CHUNK], x[:, CHUNK:]
    fill = jnp.zeros((MEM, CHUNK - 2 * ends.shape[1]), F32)
    before = jnp.concatenate([fill, ends[:MEM], ends[MEM : 2 * MEM]], axis=1)
    after = jnp.concatenate([ends[2 * MEM : 3 * MEM], ends[3 * MEM :], fill], axis=1)
    return jnp.concatenate([before, own, after], axis=0)


def windows(lats, narrow):
    parts = [[] for _ in range(4)]
    side = 2 * VARS
    for a in lats:
        rows = a.shape[0]
        before = jnp.concatenate([a[rows - MEM :, CHUNK - side :], a[: rows - MEM, CHUNK - side :]], axis=0)
        after = jnp.concatenate([a[MEM:, :side], a[:MEM, :side]], axis=0)
        parts[0] += [before, a[:, : 3 * side]]
        parts[1].append(a[:, side : 5 * side])
        parts[2].append(a[:, 3 * side : 7 * side])
        parts[3] += [a[:, 5 * side :], after]
    if narrow:
        parts = [[x[MEM : x.shape[0] - MEM] for x in p] for p in parts]
    return jnp.concatenate([jnp.concatenate(p, axis=1) for p in parts], axis=0).astype(BF)


def latitude(pred, d):
    per = pred.shape[0] // 4
    return jnp.concatenate([pred[res * per : (res + 1) * per, d * CELL : (d + 1) * CELL] for res in range(4)], axis=1)


def of_band(band, values, *at):
    got = values[(0, *at)]
    for g in range(1, values.shape[0]):
        got = jnp.where(band == g, values[(g, *at)], got)
    return got


def block_at(index, ref):
    return pl.multiple_of(jnp.clip(index, 0, ref.shape[1] // BLK - 1) * BLK, BLK)


def block_pre(b, band, s_ref, in_ref, cidx, iidx, coup_ref, inp_ref, other=None):
    pieces = []
    mats = [coup_ref[band, (2 * b + k) * BLK : (2 * b + k + 1) * BLK, :] for k in range(2)]
    mats.append(inp_ref[band, b * BLK : (b + 1) * BLK, :])
    for k in range(2):
        pieces.append(s_ref[:, pl.ds(block_at(of_band(band, cidx, k, b), s_ref), BLK)])
    pieces.append(in_ref[:, pl.ds(block_at(of_band(band, iidx, b), in_ref), BLK)])
    if other is not None:
        used, ref, at = other
        pieces[2] = jnp.where(used, ref[:, pl.ds(at, BLK)], pieces[2])
    return lax.dot_general(jnp.concatenate(pieces, axis=1), jnp.concatenate(mats, axis=1), NT, preferred_element_type=F32)


def half_of(r, rest_lats):
    return pl.ds(pl.multiple_of((1 - r if rest_lats else r) * 2 * CELL, 2 * CELL), 2 * CELL)


def send_edge(r, state, read_ref, msg_ref, edge_ref, s_ref):
    s_ref[...] = state
    pred = lax.dot_general(state, read_ref[half_of(r, False), :], NT, preferred_element_type=F32)
    for d in range(2):
        row = latitude(pred, d)
        pack(row, msg_ref, d)
        edge_ref[d] = row.astype(BF)


def widen(own, left, right):
    fill = jnp.zeros((MEM, CHUNK - HALF), F32)
    left = jnp.concatenate([fill, left.astype(F32)], axis=1)
    right = jnp.concatenate([right.astype(F32), fill], axis=1)
    return jnp.concatenate([left, own.astype(F32), right], axis=0)


def first_kernel(slots, row_ref, band_ref, cidx_ref, iidx_ref, coup_ref, inp_ref, _, own_ref, s0_ref, s1_ref, fl_ref, *rest):
    fr_ref = rest[slots]
    outs = rest[slots + 1 : -3]
    xs_ref, s_ref, in_ref = rest[-3:]
    for k in range(2):
        xs_ref[k] = jnp.zeros(xs_ref.shape[1:], F32)
        xs_ref[10 + k] = jnp.zeros(xs_ref.shape[1:], F32)
    for d in range(8):
        at, lane = (d % 2) * MEM, (d // 2 % 2) * HALF
        left = fl_ref[2 + d // 4, at : at + MEM, lane : lane + HALF]
        right = fr_ref[2 + d // 4, at : at + MEM, lane : lane + HALF]
        xs_ref[2 + d] = widen(own_ref[d], left, right)
    empty = jnp.zeros((MEM, s_ref.shape[1]), F32)
    bands, cidx, iidx = band_ref[...], cidx_ref[...], iidx_ref[...]
    for slot, src in ((1, s1_ref), (0, s0_ref)):
        r = row_of(slot, row_ref)
        per = src.shape[0] // 4
        rows = []
        for res in range(4):
            rows.append(fl_ref[r, (res - 2) * MEM : (res - 1) * MEM].astype(F32) if res >= 2 else empty)
            rows.append(src[res * per : (res + 1) * per].astype(F32))
            rows.append(fr_ref[r, res * MEM : (res + 1) * MEM].astype(F32) if res < 2 else empty)
        states = jnp.concatenate(rows, axis=0).astype(BF)
        inputs = windows([xs_ref[4 * r + d] for d in range(8)], False)
        if slot < slots:
            outs[2 * slot][...] = states
            outs[2 * slot + 1][...] = inputs
            continue
        s_ref[...] = states
        in_ref[...] = inputs
        band = jnp.where(r == 0, bands[0], bands[1])
        pres = [block_pre(b, band, s_ref, in_ref, cidx, iidx, coup_ref, inp_ref) for b in range(iidx_ref.shape[1])]
        outs[2 * slots][...] = jnp.concatenate([jnp.tanh(p).astype(BF) for p in pres], axis=1)


def first_edge_kernel(slot, row_ref, band_ref, cidx_ref, iidx_ref, coup_ref, inp_ref, read_ref, s_ref, in_ref, dl_ref, lat_ref, dr_ref, *rest):
    got_ref = rest[-1]
    r = row_of(slot, row_ref)
    lats = []
    for k in range(2):
        at = k * MEM
        lats.append(widen(lat_ref[k], dl_ref[at : at + MEM, :HALF], dr_ref[at : at + MEM]))
    got_ref[...] = windows(lats, False)
    bands, cidx, iidx = band_ref[...], cidx_ref[...], iidx_ref[...]
    band = jnp.where(r == 0, bands[0], bands[1])
    parts = []
    for b in range(iidx_ref.shape[1]):
        k = of_band(band, iidx, b) - 15 * r
        used = jnp.logical_and(k >= 0, k < 5)
        pre = block_pre(b, band, s_ref, in_ref, cidx, iidx, coup_ref, inp_ref, (used, got_ref, block_at(k, got_ref)))
        parts.append(jnp.tanh(pre).astype(BF))
    send_edge(r, jnp.concatenate(parts, axis=1), read_ref, *rest[:3])


def narrowed(s):
    per = s.shape[0] // 4
    return jnp.concatenate([s[res * per + MEM : (res + 1) * per - MEM] for res in range(4)], axis=0)


def shadow_kernel(second, last, slots, row_ref, band_ref, cidx_ref, iidx_ref, coup_ref, inp_ref, read_ref, *rest):
    rest = list(rest)

    def take(n):
        got = rest[:n]
        del rest[:n]
        return got

    edge_refs, s_refs = take(slots), take(slots)
    far_refs = take((1 if second else 2) * (2 - slots))
    pre_refs = take(slots)
    out_far = take(2 * (2 - slots))
    xs_ref, in_ref = take(2)
    rows_at = [row_of(0, row_ref), row_of(1, row_ref)]
    for k in range(2):
        xs_ref[k] = jnp.zeros(xs_ref.shape[1:], F32)
        xs_ref[10 + k] = jnp.zeros(xs_ref.shape[1:], F32)
    for slot in range(slots):
        r = rows_at[slot]
        pred = lax.dot_general(s_refs[slot][...], read_ref[half_of(r, True), :], NT, preferred_element_type=F32)
        for d in range(2):
            xs_ref[2 + 4 * r + 2 * r + d] = edge_refs[slot][d].astype(F32)
            xs_ref[2 + 4 * r + 2 * (1 - r) + d] = latitude(pred, d).astype(BF).astype(F32)
    if far_refs:
        s_refs = [s_refs[0], far_refs[-1]]
        if second:
            pred = lax.dot_general(far_refs[0][...], read_ref[...], NT, preferred_element_type=F32)
        for d in range(4):
            lat = latitude(pred, d).astype(BF) if second else far_refs[0][d]
            xs_ref[2 + 4 * rows_at[1] + d] = lat.astype(F32)
    if last:
        short_refs = take(2)
        for slot in range(2):
            short_refs[slot][...] = narrowed(s_refs[slot][...].astype(F32)).astype(BF)
        s_refs = short_refs

    bands, cidx, iidx = band_ref[...], cidx_ref[...], iidx_ref[...]
    copy = None
    for slot in (1, 0):
        r = rows_at[slot]
        band = jnp.where(r == 0, bands[0], bands[1])
        in_ref[...] = windows([xs_ref[4 * r + d] for d in range(8)], last)
        blocks = iidx_ref.shape[1]
        pres = [block_pre(b, band, s_refs[slot], in_ref, cidx, iidx, coup_ref, inp_ref) for b in range(blocks)]
        if slot < slots:
            for b in range(blocks):
                pre_refs[slot][:, b * BLK : (b + 1) * BLK] = pres[b]
            continue
        state = jnp.concatenate([jnp.tanh(p).astype(BF) for p in pres], axis=1)
        if last:
            stage_ref, sem = take(2)
            copy = put_states(r, state, stage_ref, out_far[1], sem)
        else:
            out_far[1][...] = state
        pred = lax.dot_general(state, read_ref[...], NT, preferred_element_type=F32)
        for d in range(4):
            out_far[0][d] = latitude(pred, d).astype(BF)
    if copy is not None:
        copy.wait()


def put_states(r, state, stage_ref, states_hbm, sem):
    per = state.shape[0] // 4
    for res in range(4):
        for q in range(per // MEM):
            at = res * per + q * MEM
            stage_ref[4 * q + res] = state[at : at + MEM]
    copy = pltpu.make_async_copy(stage_ref, states_hbm.at[r], sem)
    copy.start()
    return copy


def late_kernel(slot, last, final, row_ref, band_ref, iidx_ref, inp_ref, read_ref, pre_ref, got_ref, *rest):
    r = row_of(slot, row_ref)
    bands, iidx = band_ref[...], iidx_ref[...]
    band = jnp.where(r == 0, bands[0], bands[1])
    in_ref = rest[-1]
    in_ref[...] = windows([unpack(got_ref[k]) for k in range(2)], last)
    parts = []
    for b in range(iidx_ref.shape[1]):
        k = of_band(band, iidx, b) - 15 * r
        used = jnp.logical_and(k >= 0, k < 5)
        at = pl.multiple_of(jnp.where(used, k, 0) * BLK, BLK)
        term = lax.dot_general(in_ref[:, pl.ds(at, BLK)], inp_ref[band, b * BLK : (b + 1) * BLK, :], NT, preferred_element_type=F32)
        pre = pre_ref[:, b * BLK : (b + 1) * BLK] + jnp.where(used, term, 0.0)
        parts.append(jnp.tanh(pre).astype(BF))
    state = jnp.concatenate(parts, axis=1)
    if not last:
        send_edge(r, state, read_ref, *rest[:3])
        return
    if not final:
        lats_ref, states_hbm, stage_ref, sem = rest[:4]
    else:
        other_ref, _, field_hbm, states_hbm, stage_ref, sem, field_ref, field_sem = rest[:8]
    pred = lax.dot_general(state, read_ref[...], NT, preferred_element_type=F32)
    copy = put_states(r, state, stage_ref, states_hbm, sem)
    mine = [latitude(pred, d) for d in range(4)]
    if not final:
        for d in range(4):
            lats_ref[d] = mine[d].astype(BF)
        copy.wait()
        return
    other = [other_ref[d].astype(F32) for d in range(4)]
    low = r == 0
    rows = [jnp.where(low, mine[d], other[d])[None] for d in range(4)]
    rows += [jnp.where(low, other[d], mine[d])[None] for d in range(4)]
    tiles = jnp.transpose(jnp.concatenate(rows, axis=0), (1, 0, 2)).astype(BF)
    for q in range(field_ref.shape[2] // CHUNK):
        for m in range(MEM):
            field_ref[m, :, q * CHUNK : (q + 1) * CHUNK] = tiles[q * MEM + m]
    out = pltpu.make_async_copy(field_ref, field_hbm, field_sem)
    out.start()
    copy.wait()
    out.wait()


def call(kernel, out_shape, out_specs, scratch, operands, flops=0, aliases=None):
    arrays = [pltpu.with_memory_space_constraint(x, pltpu.HBM) if s is HB else x for x, s in operands]
    size = sum(x.size * x.dtype.itemsize for x, _ in operands)
    return pl.pallas_call(
        kernel,
        out_shape=out_shape,
        in_specs=[s for _, s in operands],
        out_specs=out_specs,
        scratch_shapes=scratch,
        input_output_aliases=aliases or {},
        compiler_params=pltpu.CompilerParams(vmem_limit_bytes=40 * 1024 * 1024),
        cost_estimate=pl.CostEstimate(flops=flops, bytes_accessed=size, transcendentals=0),
    )(*arrays)


def per_device(field_state, reservoir_state, coupling_blocks, coupling_index, input_blocks, input_index, readout, region_band):
    lat_count, lon_count = lax.axis_size("lat"), lax.axis_size("lon")
    lat_at = lax.axis_index("lat").astype(jnp.int32)
    region_rows, regions, members, units = reservoir_state.shape
    outs = readout.shape[1]
    assert region_rows == 2 and members == MEM and regions % 4 == 0
    chunks = regions // 4
    own_rows = chunks * MEM
    wide = own_rows + 2 * MEM
    rows = 4 * wide
    short = 4 * own_rows
    swap = lat_count == 2
    slots = 1 if swap else 2

    def bf(*dims):
        return jax.ShapeDtypeStruct(dims, BF)

    def vm(dims, dtype=BF):
        return pltpu.VMEM(dims, dtype)

    def send(x, lat_step, lon_step):
        pairs = []
        for i in range(lat_count):
            to = 1 - i if swap and lat_step else i + lat_step
            if 0 <= to < lat_count:
                for j in range(lon_count):
                    pairs.append((i * lon_count + j, to * lon_count + (j + lon_step) % lon_count))
        return lax.ppermute(x, ("lat", "lon"), pairs)

    def across(xs, lon_step=0):
        if swap:
            return [send(xs[0], 1, lon_step)]
        return [send(xs[1], 1, lon_step), send(xs[0], -1, lon_step)]

    row = ((1 - lat_at if swap else lat_at * 0).reshape(1), SM)
    small = [(region_band, VM), (coupling_index.transpose(0, 2, 1), VM), (input_index, VM)]
    band, _, iidx = small
    flops = 2 * rows * units * (3 * BLK + outs)

    mail = call(
        functools.partial(message_kernel, slots),
        [bf(4, 2 * MEM, 2 * HALF)] * 2 + [bf(8, own_rows, CHUNK)] + [bf(2 * MEM, 1536), bf(2, own_rows, CHUNK), bf(2 * MEM, HALF)] * slots,
        [VM] * (3 + 3 * slots),
        [vm(field_state.shape), vm((2, region_rows, 2, MEM, units)), pltpu.SemaphoreType.DMA((3,))],
        [row, (field_state, HB), (reservoir_state, HB)],
        AHEAD,
    )
    from_left = send(mail[0], 0, 1)
    from_dleft = across(mail[3::3], 1)
    from_lat = across(mail[4::3])
    from_right = send(mail[1], 0, -1)
    from_dright = across(mail[5::3], -1)
    own = (mail[2], VM)
    waits = [from_left] + from_dleft
    s0s1 = []
    for slot in range(2):
        operands = [row, (reservoir_state, VM)] + [(x, VM) for x in waits]
        s0s1.append(call(functools.partial(own_kernel, slot), bf(short, units), VM, [], operands, ORDER[slot]))
        waits = from_lat + s0s1
    s0, s1 = s0s1
    weights = [(x, VM) for x in (coupling_blocks, input_blocks, readout[0])]
    states_shape = bf(region_rows, regions, MEM, units)
    stage = [vm((regions, MEM, units)), pltpu.SemaphoreType.DMA]
    padded = vm((12, wide, CHUNK), F32)
    send_out = [bf(2, own_rows, CHUNK + NEAR // 2), bf(2, wide, CHUNK), bf(rows, units)]

    first = call(
        functools.partial(first_kernel, slots),
        [bf(rows, units), bf(rows, 16 * CELL)] * slots + [bf(rows, units)] * (2 - slots),
        [VM] * (2 + slots),
        [padded, vm((rows, units)), vm((rows, 16 * CELL))],
        [row] + small + weights + [own, (s0, VM), (s1, VM), (from_left, VM)] + [(x, VM) for x in from_lat] + [(from_right, VM)],
    )
    far = list(first[2 * slots :])
    sent, edges, states = [None] * slots, [None] * slots, [None] * slots
    for slot in range(slots):
        known = [(x, VM) for x in first[2 * slot : 2 * slot + 2]]
        corners = [(x[slot], VM) for x in (from_dleft, from_lat, from_dright)]
        sent[slot], edges[slot], states[slot] = call(
            functools.partial(first_edge_kernel, slot),
            send_out,
            [VM] * 3,
            [vm((rows, 4 * CELL))],
            [row] + small + weights + known + corners,
            flops,
        )

    for step in range(1, STEPS):
        last = step == STEPS - 1
        got = across(sent)
        pre_rows = short if last else rows
        out = [jax.ShapeDtypeStruct((pre_rows, units), F32)] * slots
        specs = [VM] * slots
        scratch = [padded, vm((pre_rows, 16 * CELL))] + [vm((short, units))] * (2 if last else 0)
        if swap:
            out += [bf(4, own_rows if last else wide, CHUNK), states_shape if last else bf(rows, units)]
            specs += [VM, HB if last else VM]
            scratch += stage if last else []
        shadow = call(
            functools.partial(shadow_kernel, step == 1, last, slots),
            out,
            specs,
            scratch,
            [row] + small + weights + [(x, VM) for x in edges + states + far],
            2 * flops,
        )
        far = list(shadow[slots:])
        for slot in reversed(range(slots)):
            operands = [row, band, iidx] + weights[1:] + [(shadow[slot], VM), (got[slot], VM)]
            inputs = [vm((pre_rows, 4 * CELL))]
            if not last:
                sent[slot], edges[slot], states[slot] = call(
                    functools.partial(late_kernel, slot, False, False), send_out, [VM] * 3, inputs, operands, flops
                )
            elif slot == 1:
                far = call(
                    functools.partial(late_kernel, slot, True, False),
                    [bf(4, own_rows, CHUNK), states_shape],
                    [VM, HB],
                    stage + inputs,
                    operands,
                    flops,
                )
            else:
                return call(
                    functools.partial(late_kernel, slot, True, True),
                    [bf(MEM, 8, regions * CELL), states_shape],
                    [HB, HB],
                    stage + [vm((MEM, 8, regions * CELL)), pltpu.SemaphoreType.DMA] + inputs,
                    operands + [(far[0], VM), (far[1], HB)],
                    flops,
                    {len(operands) + 1: 1},
                )


def solution(mesh):
    return jax.shard_map(
        per_device,
        mesh=mesh,
        in_specs=(
            P(None, "lat", "lon"),
            P("lat", "lon", None, None),
            P("lat", None, None),
            P("lat", None, None),
            P("lat", None, None),
            P("lat", None),
            P("lat", None, None),
            P("lat"),
        ),
        out_specs=(P(None, "lat", "lon"), P("lat", "lon", None, None)),
        check_vma=False,
    )
```
